32 devices in a mesh: seq: 4 (over x, core), rows: 8 (over z, y).
Axes of the slice: x: 2, y: 2, z: 4, core: 2. Of those that a mesh axis runs over, the one named last changes fastest.
Arguments:
- inputs: bfloat16 [16, 2048, 768], P('rows', 'seq'), may hold values from -6 to 6
- query_weight: bfloat16 [768, 768], replicated, may hold values from -0.21875 to 0.21875
- query_bias: bfloat16 [768], replicated, may hold values from -1.5 to 1.5
- key_weight: bfloat16 [768, 768], replicated, may hold values from -0.21875 to 0.21875
- value_weight: bfloat16 [768, 768], replicated, may hold values from -0.21875 to 0.21875
- value_bias: bfloat16 [768], replicated, may hold values from -1.5 to 1.5
- output_weight: bfloat16 [768, 768], replicated, may hold values from -1.5 to 1.5
- output_bias: bfloat16 [768], replicated, may hold values from -1.5 to 1.5
- first_gain: bfloat16 [768], replicated, may hold values from 0.5 to 1.5
- first_shift: bfloat16 [768], replicated, may hold values from -1 to 1
- inner_weight: bfloat16 [768, 3072], replicated, may hold values from -0.21875 to 0.21875
- inner_bias: bfloat16 [3072], replicated, may hold values from -1.5 to 1.5
- outer_weight: bfloat16 [3072, 768], replicated, may hold values from -0.109375 to 0.109375
- outer_bias: bfloat16 [768], replicated, may hold values from -1.5 to 1.5
- second_gain: bfloat16 [768], replicated, may hold values from 0.5 to 1.5
- second_shift: bfloat16 [768], replicated, may hold values from -1 to 1
- doc_tokens: int32 [16], P('rows'), may hold values from 512 to 2048, as said below
- random_blocks: int32 [16, 32, 3], P('rows'), may hold values from 2 to 31, as said below
- cotangent: bfloat16 [16, 2048, 768], P('rows', 'seq'), may hold values from -6 to 6
Outputs:
- outputs: bfloat16 [16, 2048, 768], P('rows', 'seq')
- input_gradient: bfloat16 [16, 2048, 768], P('rows', 'seq')
- query_weight_gradient: float32 [768, 768], replicated
- query_bias_gradient: float32 [768], replicated
- key_weight_gradient: float32 [768, 768], replicated
- value_weight_gradient: float32 [768, 768], replicated
- value_bias_gradient: float32 [768], replicated
- output_weight_gradient: float32 [768, 768], replicated
- output_bias_gradient: float32 [768], replicated
- first_gain_gradient: float32 [768], replicated
- first_shift_gradient: float32 [768], replicated
- inner_weight_gradient: float32 [768, 3072], replicated
- inner_bias_gradient: float32 [3072], replicated
- outer_weight_gradient: float32 [3072, 768], replicated
- outer_bias_gradient: float32 [768], replicated
- second_gain_gradient: float32 [768], replicated
- second_shift_gradient: float32 [768], replicated
The draws below stay inside these ranges and needn't reach their ends.
Inputs may be any that keep to these rules, and one draw needn't show every extreme that they name: `doc_tokens`: in each aligned block of 2 rows one row, drawn from the seed, holds a document of more than 1536 tokens; one row of the batch, drawn from the seed, holds exactly 2048. `random_blocks`: for query block i of a row the 3 entries are distinct, and none of them is 0, 1, i - 1, i or i + 1.
All inputs are finite; a program needn't handle non-finite values.
Results may differ from the reference program's by a relative error of at most 0.015.
Values may be sent and summed in bfloat16 or wider, within the bound.
No kernel may reach another device: no remote copies, remote signals or barrier semaphores. Data moves between devices by JAX's collectives and lax.ppermute only.
A program may use at most 512 MiB of HBM per device.

```python
import jax
import jax.numpy as jnp
from jax import lax

D = 768
HEADS = 12
HEAD = 64
FF = 3072
BLOCK = 64
RANDOM = 3
ROWS_DEV = 2
SEQ_DEV = 512
MIN_DOC = 512
SEQ_LEN = 2048
ROWS = 16
BLOCKS = 32


def draw_doc_tokens(key, part):
    key = jax.random.fold_in(key, 11)
    key_len, key_pick, key_long, key_full = jax.random.split(key, 4)
    drawn = jax.random.randint(key_len, (ROWS,), MIN_DOC, SEQ_LEN + 1)
    reaching = jax.random.randint(key_long, (ROWS,), SEQ_LEN - SEQ_DEV + 1, SEQ_LEN + 1)
    picked = jax.random.randint(key_pick, (ROWS // ROWS_DEV,), 0, ROWS_DEV)
    long_row = jnp.arange(ROWS) % ROWS_DEV == jnp.repeat(picked, ROWS_DEV)
    lengths = jnp.where(long_row, reaching, drawn)
    full_at = jax.random.randint(key_full, (), 0, ROWS)
    lengths = jnp.where(jnp.arange(ROWS) == full_at, SEQ_LEN, lengths)
    return lengths.astype(jnp.int32)


def draw_random_blocks(key, part):
    key = jax.random.fold_in(key, 12)
    noise = jax.random.randint(key, (ROWS, BLOCKS, BLOCKS), 0, 1 << 20)
    column = jnp.arange(BLOCKS)[None, :]
    place = jnp.arange(BLOCKS)[:, None]
    ranked = noise * BLOCKS + column
    barred = (column < 2) | (jnp.abs(column - place) <= 1)
    ranked = jnp.where(barred[None], -1, ranked)
    best_vals, picked = lax.top_k(ranked, RANDOM)
    return picked.astype(jnp.int32)


def level_of(key, shape, cuts, least, largest):
    loudness = 1.0
    for dim, parts in cuts:
        draws = jax.random.uniform(jax.random.fold_in(jax.random.fold_in(key, 6), dim), (parts,), jnp.float32, least / len(cuts), largest / len(cuts))
        loudness = loudness * jnp.repeat(jnp.exp(draws), shape[dim] // parts).reshape((-1,) + (1,) * (len(shape) - 1 - dim))
    return loudness


def centred(rng, shape, width, limit, cuts=(), held_as=jnp.bfloat16):
    level = level_of(rng, shape, cuts, -0.22, 0.18) if cuts else 1.0
    values = jax.random.normal(rng, shape, jnp.float32) * width * level
    return jnp.minimum(jnp.maximum(values, -limit), limit).astype(held_as)


def setup_inputs(seed: int = 0) -> dict:
    splits = jax.random.split(jax.random.key(seed), 20)
    inputs = centred(splits[0], (ROWS, SEQ_LEN, D), 1.0, 6.0, ((0, 8), (1, 4)))
    query_weight = centred(splits[1], (D, D), D ** -0.5, 0.21875)
    query_bias = centred(splits[2], (D,), 0.3, 1.5)
    key_weight = centred(splits[3], (D, D), D ** -0.5, 0.21875)
    value_weight = centred(splits[4], (D, D), D ** -0.5, 0.21875)
    value_bias = centred(splits[5], (D,), 0.3, 1.5)
    output_weight = centred(splits[6], (D, D), (max(D // 48, 1)) ** -0.5, 1.5)
    output_bias = centred(splits[7], (D,), 0.3, 1.5)
    first_gain = jnp.clip(1.0 + 0.1 * jax.random.normal(splits[8], (D,), jnp.float32), 0.5, 1.5).astype(jnp.bfloat16)
    first_shift = centred(splits[9], (D,), 0.2, 1.0)
    inner_weight = centred(splits[10], (D, FF), D ** -0.5, 0.21875)
    inner_bias = centred(splits[11], (FF,), 0.3, 1.5)
    outer_weight = centred(splits[12], (FF, D), FF ** -0.5, 0.109375)
    outer_bias = centred(splits[13], (D,), 0.3, 1.5)
    second_gain = jnp.clip(1.0 + 0.1 * jax.random.normal(splits[14], (D,), jnp.float32), 0.5, 1.5).astype(jnp.bfloat16)
    second_shift = centred(splits[15], (D,), 0.2, 1.0)
    doc_tokens = draw_doc_tokens(jax.random.fold_in(splits[19], 71), 0)
    random_blocks = draw_random_blocks(jax.random.fold_in(splits[19], 71), 0)
    cotangent = centred(splits[18], (ROWS, SEQ_LEN, D), 1.0, 6.0, ((0, 8), (1, 4)))
    return dict(inputs=inputs, query_weight=query_weight, query_bias=query_bias, key_weight=key_weight, value_weight=value_weight, value_bias=value_bias, output_weight=output_weight, output_bias=output_bias, first_gain=first_gain, first_shift=first_shift, inner_weight=inner_weight, inner_bias=inner_bias, outer_weight=outer_weight, outer_bias=outer_bias, second_gain=second_gain, second_shift=second_shift, doc_tokens=doc_tokens, random_blocks=random_blocks, cotangent=cotangent)


@jax.custom_vjp
def low(v):
    return lax.optimization_barrier(v.astype(jnp.bfloat16)).astype(jnp.float32)

@jax.custom_vjp
def low_back(v):
    return v

def low_keep(v):
    return (low(v), None)

def low_pass(kept, grad):
    return (grad,)

def back_keep(v):
    return (v, None)

def back_low(kept, grad):
    return (low(grad),)
low.defvjp(low_keep, low_pass)
low_back.defvjp(back_keep, back_low)
EPSILON = 1e-05
NEG_FILL = -1e+30

def matmul(left, right):
    return jnp.dot(left, right, precision=lax.Precision.HIGHEST)

def layer_norm(value, gain, shift):
    center = value - lax.optimization_barrier(jnp.mean(value, -1, keepdims=True))
    spread = lax.optimization_barrier(jnp.mean(center * center, -1, keepdims=True))
    return center * lax.rsqrt(spread + EPSILON) * gain + shift

def softmax_rows(score):
    row_max = lax.optimization_barrier(jnp.max(score, -1, keepdims=True))
    expo = jnp.exp(score - row_max)
    return expo / lax.optimization_barrier(jnp.sum(expo, -1, keepdims=True))

def key_layout(length, chosen):
    block_count = chosen.shape[0]
    block_ids = jnp.arange(block_count, dtype=jnp.int32)
    before = block_ids - 1
    after_id = block_ids + 1
    fixed = jnp.stack([block_ids * 0, block_ids * 0 + 1, before, block_ids, after_id], -1)
    index = jnp.concatenate([fixed, chosen.astype(jnp.int32)], -1)
    always_on = block_ids >= 0
    allowed = jnp.stack([always_on, always_on, before >= 2, always_on, after_id < block_count] + [always_on] * RANDOM, -1)
    index = jnp.clip(index, 0, block_count - 1).astype(jnp.int32)
    places = index[:, :, None] * BLOCK + jnp.arange(BLOCK, dtype=jnp.int32)
    valid = (places < length) & allowed[:, :, None]
    return (index, valid.reshape(block_count, -1))

def layer(x, query_weight, query_bias, key_weight, value_weight, value_bias, output_weight, output_bias, first_gain, first_shift, inner_weight, inner_bias, outer_weight, outer_bias, second_gain, second_shift, length, chosen):
    seq_len = x.shape[0]
    block_count = seq_len // BLOCK
    per_group = SEQ_DEV // BLOCK
    group_count = block_count // per_group
    scale = HEAD ** (-0.5)
    query = low_back(low(matmul(x, query_weight) + query_bias)).reshape(seq_len, HEADS, HEAD)
    key_all = low_back(low(matmul(x, key_weight))).reshape(seq_len, HEADS, HEAD)
    value_all = low_back(low(matmul(x, value_weight) + value_bias)).reshape(seq_len, HEADS, HEAD)
    index, valid = key_layout(length, chosen)
    key_tiles = key_all.reshape(block_count, BLOCK, HEADS, HEAD)
    value_tiles = value_all.reshape(block_count, BLOCK, HEADS, HEAD)

    def attend_group(item):
        query_group, index_group, valid_group = item
        key_group = key_tiles[index_group].reshape(per_group, -1, HEADS, HEAD)
        value_group = value_tiles[index_group].reshape(per_group, -1, HEADS, HEAD)
        score = jnp.einsum('bqhd,bkhd->bhqk', query_group, key_group, precision=lax.Precision.HIGHEST) * scale
        score = jnp.where(valid_group[:, None, None, :], low_back(score), NEG_FILL)
        weight = low(softmax_rows(score))
        return jnp.einsum('bhqk,bkhd->bqhd', weight, value_group, precision=lax.Precision.HIGHEST)
    local = lax.map(jax.checkpoint(attend_group), (query.reshape(group_count, per_group, BLOCK, HEADS, HEAD), index.reshape(group_count, per_group, -1), valid.reshape(group_count, per_group, -1)))
    key_valid = jnp.arange(seq_len, dtype=jnp.int32) < length
    lead = 2 * BLOCK
    global_score = jnp.einsum('qhd,khd->hqk', query[:lead], key_all, precision=lax.Precision.HIGHEST) * scale
    global_score = jnp.where(key_valid, low_back(global_score), NEG_FILL)
    global_context = jnp.einsum('hqk,khd->qhd', low(softmax_rows(global_score)), value_all, precision=lax.Precision.HIGHEST)
    context = jnp.concatenate([global_context, local.reshape(seq_len, HEADS, HEAD)[lead:]], 0).reshape(seq_len, D)
    context = low_back(low(context))
    attended = low_back(matmul(context, output_weight) + output_bias)
    first = layer_norm(x + attended, first_gain, first_shift)
    inner = low_back(matmul(low(first), inner_weight) + inner_bias)
    active = low(jax.nn.gelu(inner, approximate=True))
    outer = low_back(matmul(active, outer_weight) + outer_bias)
    return layer_norm(first + outer, second_gain, second_shift)

def reference(inputs, query_weight, query_bias, key_weight, value_weight, value_bias, output_weight, output_bias, first_gain, first_shift, inner_weight, inner_bias, outer_weight, outer_bias, second_gain, second_shift, doc_tokens, random_blocks, cotangent):
    weights = tuple((item.astype(jnp.float32) for item in (query_weight, query_bias, key_weight, value_weight, value_bias, output_weight, output_bias, first_gain, first_shift, inner_weight, inner_bias, outer_weight, outer_bias, second_gain, second_shift)))

    def one_row(carry, item):
        row_in, row_grad, length, chosen = item

        def forward(row_x, *params):
            return layer(row_x, *params, length, chosen)
        result, pull = jax.vjp(forward, row_in, *weights)
        grads = pull(row_grad)
        summed = tuple((accum + piece for accum, piece in zip(carry, grads[1:])))
        return (summed, (result.astype(jnp.bfloat16), grads[0].astype(jnp.bfloat16)))
    start = tuple((jnp.zeros(item.shape, jnp.float32) for item in weights))
    totals, (outputs, input_gradient) = lax.scan(one_row, start, (inputs.astype(jnp.float32), cotangent.astype(jnp.float32), doc_tokens, random_blocks))
    return (outputs, input_gradient) + totals
```

```python
import functools
from functools import partial

import jax
import jax.numpy as jnp
from jax import lax
from jax.experimental import pallas as pl
from jax.experimental.pallas import tpu as pltpu
from jax.sharding import PartitionSpec as P

D = 768
HEADS = 12
HEAD = 64
BLOCK = 64
SETS = 8
CHIPS_Z = 4

EPSILON = 1e-05
NEG_FILL = -1e30

NT = (((1,), (1,)), ((), ()))
NN = (((1,), (0,)), ((), ()))
TN = (((0,), (0,)), ((), ()))


def dot(left, right, dims):
    return lax.dot_general(left, right, dims, preferred_element_type=jnp.float32)


def head_groups(heads):
    groups, at = [], 0
    while at < heads:
        n = 2 if heads - at >= 2 else 1
        groups.append((at, n))
        at += n
    return groups


def spread_heads(block, diag, n):
    if n == 1:
        return block
    w = n * HEAD
    return jnp.concatenate([block] * n, 0) * diag[:w, :w]


def fold_heads(full, diag, n):
    if n == 1:
        return full
    w = n * HEAD
    kept = full * diag[:w, :w]
    out = kept[:HEAD]
    for h in range(1, n):
        out = out + kept[h * HEAD : (h + 1) * HEAD]
    return out


def rows_of(slot):
    return pl.ds(pl.multiple_of(slot * BLOCK, BLOCK), BLOCK)


def gather_rows(ref, slots, lanes):
    return jnp.concatenate([ref[rows_of(s), lanes] for s in slots], 0)


def attend_kernel(
    heads,
    nb,
    key_at_ref,
    bias_at_ref,
    query_at_ref,
    q_ref,
    k_ref,
    v_ref,
    bias_ref,
    diag_ref,
    o_ref,
    lse_ref,
    top_ref,
    sum_ref,
    acc_ref,
):
    groups = head_groups(heads)
    scale = jnp.bfloat16(HEAD**-0.5)

    def local(t, carry):
        ks = [key_at_ref[t, b] for b in range(SETS)]
        bs = [bias_at_ref[t, b] for b in range(SETS)]
        qs = query_at_ref[t]
        bias = gather_rows(bias_ref, bs, slice(None))
        diag = diag_ref[...]
        diag_f = diag.astype(jnp.float32)
        for at, n in groups:
            w = n * HEAD
            lanes = slice(at * HEAD, at * HEAD + w)
            query = spread_heads(q_ref[rows_of(qs), lanes] * scale, diag, n)
            score = dot(gather_rows(k_ref, ks, lanes), query, NT) + bias[:, :w]
            top = jnp.max(score, 0, keepdims=True)
            prob = jnp.exp(score - top)
            total = jnp.sum(prob, 0, keepdims=True)
            prob = (prob * (1.0 / total)).astype(jnp.bfloat16)
            out = fold_heads(dot(prob, gather_rows(v_ref, ks, lanes), TN), diag_f, n)
            o_ref[rows_of(qs), lanes] = out.astype(jnp.bfloat16)
            lse_ref[qs, :, lanes] = top + jnp.log(total)
        return carry

    lax.fori_loop(0, nb - 2, local, 0)

    chunks = nb // SETS

    def lead(b, carry):
        qs = query_at_ref[nb - 2 + b * chunks]
        top_ref[...] = jnp.full_like(top_ref, NEG_FILL)
        sum_ref[...] = jnp.zeros_like(sum_ref)
        acc_ref[...] = jnp.zeros_like(acc_ref)
        diag = diag_ref[...]
        diag_f = diag.astype(jnp.float32)

        def chunk(c, carry):
            keys = pl.ds(pl.multiple_of(c * (SETS * BLOCK), SETS * BLOCK), SETS * BLOCK)
            bias = bias_ref[keys, :]
            for at, n in groups:
                w = n * HEAD
                lanes = slice(at * HEAD, at * HEAD + w)
                query = spread_heads(q_ref[rows_of(qs), lanes] * scale, diag, n)
                score = dot(k_ref[keys, lanes], query, NT) + bias[:, :w]
                was = top_ref[:, lanes]
                top = jnp.maximum(was, jnp.max(score, 0, keepdims=True))
                prob = jnp.exp(score - top)
                keep = jnp.exp(was - top)
                top_ref[:, lanes] = top
                sum_ref[:, lanes] = sum_ref[:, lanes] * keep + jnp.sum(prob, 0, keepdims=True)
                part = dot(v_ref[keys, lanes], prob.astype(jnp.bfloat16), TN)
                acc_ref[lanes, :w] = acc_ref[lanes, :w] * keep + part
            return carry

        lax.fori_loop(0, chunks, chunk, 0)
        for at, n in groups:
            w = n * HEAD
            lanes = slice(at * HEAD, at * HEAD + w)
            total = sum_ref[:, lanes]
            full = (acc_ref[lanes, :w] * (1.0 / total)).T
            o_ref[rows_of(qs), lanes] = fold_heads(full, diag_f, n).astype(jnp.bfloat16)
            lse_ref[qs, :, lanes] = top_ref[:, lanes] + jnp.log(total)
        return carry

    lax.fori_loop(0, 2, lead, 0)


def attend_back_kernel(
    heads,
    nb,
    tasks,
    key_at_ref,
    bias_at_ref,
    query_at_ref,
    q_ref,
    k_ref,
    v_ref,
    g_ref,
    bias_ref,
    diag_ref,
    lse_ref,
    delta_ref,
    dq_ref,
    dk_ref,
    dv_ref,
    dq_acc,
    dk_acc,
    dv_acc,
):
    groups = head_groups(heads)
    dq_acc[...] = jnp.zeros_like(dq_acc)
    dk_acc[...] = jnp.zeros_like(dk_acc)
    dv_acc[...] = jnp.zeros_like(dv_acc)
    scale = HEAD**-0.5

    def task(t, carry):
        ks = [key_at_ref[t, b] for b in range(SETS)]
        bs = [bias_at_ref[t, b] for b in range(SETS)]
        qs = query_at_ref[t]
        bias = gather_rows(bias_ref, bs, slice(None))
        diag = diag_ref[...]
        diag_f = diag.astype(jnp.float32)
        for at, n in groups:
            w = n * HEAD
            lanes = slice(at * HEAD, at * HEAD + w)
            query = spread_heads(q_ref[rows_of(qs), lanes] * jnp.bfloat16(scale), diag, n)
            grad = spread_heads(g_ref[rows_of(qs), lanes], diag, n)
            keys = gather_rows(k_ref, ks, lanes)
            values = gather_rows(v_ref, ks, lanes)
            score = dot(keys, query, NT) + bias[:, :w]
            prob = jnp.exp(score - lse_ref[qs, :, lanes])
            d_prob = dot(values, grad, NT)
            d_score = (prob * (d_prob - delta_ref[qs, :, lanes])).astype(jnp.bfloat16)
            d_value = dot(prob.astype(jnp.bfloat16), grad, NN)
            d_key = dot(d_score, query, NN)
            before = [(dk_acc[rows_of(a), lanes], dv_acc[rows_of(a), lanes]) for a in bs]
            for i, a in enumerate(bs):
                part = slice(i * BLOCK, (i + 1) * BLOCK)
                dk_acc[rows_of(a), lanes] = before[i][0] + d_key[part]
                dv_acc[rows_of(a), lanes] = before[i][1] + d_value[part]
            d_query = fold_heads(dot(d_score, keys, TN), diag_f, n)
            dq_acc[rows_of(qs), lanes] += d_query * scale
        return carry

    lax.fori_loop(0, tasks, task, 0)
    dq_ref[...] = dq_acc[...].astype(jnp.bfloat16)
    dk_ref[...] = dk_acc[: nb * BLOCK].astype(jnp.bfloat16)
    dv_ref[...] = dv_acc[: nb * BLOCK].astype(jnp.bfloat16)


VMEM = pl.BlockSpec(memory_space=pltpu.VMEM)
SMEM = pl.BlockSpec(memory_space=pltpu.SMEM)


def diagonal_mask():
    head = jnp.arange(2 * HEAD) // HEAD
    return (head[:, None] == head[None, :]).astype(jnp.bfloat16)


def attend(q, k, v, tables, heads, nb):
    key_at, bias_at, query_at, bias = tables
    width = heads * HEAD
    return pl.pallas_call(
        partial(attend_kernel, heads, nb),
        out_shape=(
            jax.ShapeDtypeStruct((nb * BLOCK, width), jnp.bfloat16),
            jax.ShapeDtypeStruct((nb, 1, width), jnp.float32),
        ),
        in_specs=[SMEM] * 3 + [VMEM] * 5,
        out_specs=(VMEM, VMEM),
        scratch_shapes=[
            pltpu.VMEM((1, width), jnp.float32),
            pltpu.VMEM((1, width), jnp.float32),
            pltpu.VMEM((width, 2 * HEAD), jnp.float32),
        ],
        compiler_params=pltpu.CompilerParams(vmem_limit_bytes=48 << 20),
        cost_estimate=pl.CostEstimate(
            flops=40_000_000_000, bytes_accessed=8 << 20, transcendentals=0
        ),
        name="attend",
    )(key_at, bias_at, query_at, q, k, v, bias, diagonal_mask())


def attend_back(q, k, v, grad, tables, lse, delta, heads, nb):
    key_at, bias_at, query_at, bias = tables
    width = heads * HEAD
    out = jax.ShapeDtypeStruct((nb * BLOCK, width), jnp.bfloat16)
    return pl.pallas_call(
        partial(attend_back_kernel, heads, nb, key_at.shape[0]),
        out_shape=(out, out, out),
        in_specs=[SMEM] * 3 + [VMEM] * 8,
        out_specs=(VMEM, VMEM, VMEM),
        scratch_shapes=[
            pltpu.VMEM((nb * BLOCK, width), jnp.float32),
            pltpu.VMEM(((nb + 1) * BLOCK, width), jnp.float32),
            pltpu.VMEM(((nb + 1) * BLOCK, width), jnp.float32),
        ],
        compiler_params=pltpu.CompilerParams(vmem_limit_bytes=52 << 20),
        cost_estimate=pl.CostEstimate(
            flops=45_000_000_000, bytes_accessed=10 << 20, transcendentals=0
        ),
        name="attend_back",
    )(key_at, bias_at, query_at, q, k, v, grad, bias, diagonal_mask(), lse, delta)


def block_tables(block_of_slot, doc, random_blocks):
    nb = random_blocks.shape[0]
    every = jnp.arange(nb, dtype=jnp.int32)
    slot_of_block = jnp.sum(
        jnp.where(block_of_slot[None, :] == every[:, None], every[None, :], 0), 1
    )
    ids = every[2:]
    before, after = ids - 1, ids + 1
    always_on = ids >= 0
    index = jnp.concatenate(
        [jnp.stack([ids * 0, ids * 0 + 1, before, ids, after], -1), random_blocks[2:]], -1
    )
    allowed = jnp.stack(
        [always_on, always_on, before >= 2, always_on, after < nb] + [always_on] * 3, -1
    )
    index = jnp.clip(index, 0, nb - 1)
    slots = jnp.sum(jnp.where(index[..., None] == block_of_slot, every, 0), -1)
    chunks = nb // SETS
    lead = jnp.tile(every.reshape(chunks, SETS), (2, 1))
    key_at = jnp.concatenate([slots, lead], 0)
    bias_at = jnp.concatenate([jnp.where(allowed, slots, nb), lead], 0)
    query_at = jnp.concatenate([slot_of_block[2:], jnp.repeat(slot_of_block[:2], chunks)])
    places = block_of_slot[:, None] * BLOCK + jnp.arange(BLOCK, dtype=jnp.int32)
    bias = jnp.where(places < doc, 0.0, NEG_FILL).astype(jnp.float32).reshape(-1)
    bias = jnp.concatenate([bias, jnp.full((BLOCK,), NEG_FILL, jnp.float32)])
    bias = jnp.broadcast_to(bias[:, None], (bias.shape[0], 2 * HEAD))
    return key_at, bias_at, query_at, bias


class Ring:
    def __init__(self, axis, size, at, perm):
        self.axis, self.size, self.at, self.perm = axis, size, at, perm

    def send(self, value, by):
        return lax.ppermute(value, self.axis, self.perm(by))

    def scatter_sum(self, value):
        part = value.shape[0] // self.size

        def cut(i):
            return lax.dynamic_slice_in_dim(value, lax.rem(i, self.size) * part, part, 0)

        if self.size == 1:
            return value
        total = cut(self.at).astype(jnp.float32)
        for by in range(1, self.size):
            total = total + self.send(cut(self.at + by), by).astype(jnp.float32)
        return total.astype(value.dtype)

    def gather(self, value):
        if self.size == 1:
            return value
        part = value.shape[0]
        if self.size == 2:
            other = self.send(value, 1)
            first = jnp.where(self.at == 0, value, other)
            second = jnp.where(self.at == 0, other, value)
            return jnp.concatenate([first, second], 0)
        out = jnp.zeros((self.size * part,) + value.shape[1:], value.dtype)
        out = lax.dynamic_update_slice_in_dim(out, value, self.at * part, 0)
        for by in range(1, self.size):
            came = lax.rem(self.at + self.size - by, self.size)
            out = lax.dynamic_update_slice_in_dim(out, self.send(value, by), came * part, 0)
        return out


def make_rings(seq, rows):
    half = seq // 2
    deep = CHIPS_Z if rows % CHIPS_Z == 0 else 1
    wide = rows // deep
    s, r = lax.axis_index("seq"), lax.axis_index("rows")
    near = Ring(
        "seq",
        half,
        lax.rem(s, half),
        lambda by: [(i, i // half * half + (i + by) % half) for i in range(seq)],
    )
    far = Ring("seq", 2, s // half, lambda by: [(i, (i + half) % seq) for i in range(seq)])
    y = Ring(
        "rows",
        wide,
        lax.rem(r, wide),
        lambda by: [(i, i // wide * wide + (i + by) % wide) for i in range(rows)],
    )
    z = Ring("rows", deep, r // wide, lambda by: [(i, (i + by * wide) % rows) for i in range(rows)])
    return near, far, y, z


def summed(value, order):
    for ring in order:
        value = ring.scatter_sum(value)
    for ring in reversed(order):
        value = ring.gather(value)
    return value


def layer_norm(value, gain, shift):
    center = value - jnp.mean(value, -1, keepdims=True)
    spread = jnp.mean(center * center, -1, keepdims=True)
    return center * lax.rsqrt(spread + EPSILON) * gain + shift


def column_sum(values):
    return jnp.sum(values.astype(jnp.float32), 0)


def per_device(
    seq,
    rows,
    inputs,
    query_weight,
    query_bias,
    key_weight,
    value_weight,
    value_bias,
    output_weight,
    output_bias,
    first_gain,
    first_shift,
    inner_weight,
    inner_bias,
    outer_weight,
    outer_bias,
    second_gain,
    second_shift,
    doc_tokens,
    random_blocks,
    cotangent,
):
    low, full = jnp.bfloat16, jnp.float32
    near, far, y, z = make_rings(seq, rows)
    half = seq // 2
    width = inputs.shape[1]
    nb = random_blocks.shape[1]
    heads = HEADS // half
    cols = heads * HEAD
    mine, at = far.at, near.at

    def to_rows(array):
        own = lax.dynamic_index_in_dim(array, mine, 0, False)
        return own, far.send(lax.dynamic_index_in_dim(array, 1 - mine, 0, False), 1)

    def from_rows(value):
        own, other = value[:width], far.send(value[width:], 1)
        return jnp.where(mine == 0, jnp.stack([own, other]), jnp.stack([other, own]))

    x_pair = jnp.concatenate(to_rows(inputs), 0)
    tokens = x_pair.shape[0]
    x_all = jnp.concatenate([x_pair] + [near.send(x_pair, half - k) for k in range(1, half)], 0)
    cot = jnp.concatenate(to_rows(cotangent), 0)

    shards = []
    for k in range(half):
        own = mine * half + lax.rem(at + k, half)
        shards += [own, lax.rem(own + half, seq)]
    per_shard = width // BLOCK
    block_of_slot = (
        jnp.stack(shards)[:, None] * per_shard + jnp.arange(per_shard, dtype=jnp.int32)
    ).reshape(-1).astype(jnp.int32)
    doc = lax.dynamic_index_in_dim(doc_tokens, mine, 0, False)
    chosen = lax.dynamic_index_in_dim(random_blocks, mine, 0, False)
    tables = block_tables(block_of_slot, doc, chosen)

    def my_cols(weight):
        return lax.dynamic_slice_in_dim(weight, at * cols, cols, weight.ndim - 1)

    wq, wk, wv = my_cols(query_weight), my_cols(key_weight), my_cols(value_weight)
    query = (dot(x_all, wq, NN) + my_cols(query_bias).astype(full)).astype(low)
    key = dot(x_all, wk, NN).astype(low)
    value = (dot(x_all, wv, NN) + my_cols(value_bias).astype(full)).astype(low)

    heads_context, lse = attend(query, key, value, tables, heads, nb)
    context = jnp.concatenate(
        [heads_context[:tokens]]
        + [near.send(heads_context[k * tokens : (k + 1) * tokens], k) for k in range(1, half)],
        1,
    )
    wo = jnp.concatenate(
        [
            lax.dynamic_slice_in_dim(
                output_weight, lax.rem(at + half - k, half) * cols, cols, 0
            )
            for k in range(half)
        ],
        0,
    )
    first_gain_f, first_shift_f = first_gain.astype(full), first_shift.astype(full)
    second_gain_f, second_shift_f = second_gain.astype(full), second_shift.astype(full)
    resid = x_pair.astype(full) + dot(context, wo, NN) + output_bias.astype(full)
    first = layer_norm(resid, first_gain_f, first_shift_f)
    first_low = first.astype(low)
    inner = dot(first_low, inner_weight, NN) + inner_bias.astype(full)
    active = jax.nn.gelu(inner, approximate=True).astype(low)
    second = first + dot(active, outer_weight, NN) + outer_bias.astype(full)
    result = layer_norm(second, second_gain_f, second_shift_f).astype(low)
    result = from_rows(result)

    second_pull = jax.vjp(layer_norm, second, second_gain_f, second_shift_f)[1]
    d_second, second_gain_grad, second_shift_grad = second_pull(cot.astype(full))
    d_outer = d_second.astype(low)
    outer_grad = dot(active, d_outer, TN).astype(low)
    gelu_pull = jax.vjp(partial(jax.nn.gelu, approximate=True), inner)[1]
    d_inner = gelu_pull(dot(d_outer, outer_weight, NT))[0].astype(low)
    inner_grad = dot(first_low, d_inner, TN).astype(low)
    d_first = d_second + dot(d_inner, inner_weight, NT)
    first_pull = jax.vjp(layer_norm, resid, first_gain_f, first_shift_f)[1]
    d_resid, first_gain_grad, first_shift_grad = first_pull(d_first)
    d_attended = d_resid.astype(low)
    out_grad = dot(context, d_attended, TN)
    out_grad = jnp.concatenate(
        [
            lax.dynamic_slice_in_dim(out_grad, lax.rem(at + half - k, half) * cols, cols, 0)
            for k in range(half)
        ],
        0,
    )
    d_context = dot(d_attended, wo, NT).astype(low)
    heads_grad = jnp.concatenate(
        [d_context[:, :cols]]
        + [near.send(d_context[:, k * cols : (k + 1) * cols], half - k) for k in range(1, half)],
        0,
    )
    delta = jnp.sum(
        (heads_grad.astype(full) * heads_context.astype(full)).reshape(nb, BLOCK, heads, HEAD), -1
    )
    delta = delta.transpose(0, 2, 1).reshape(nb, 1, cols)
    d_query, d_key, d_value = attend_back(
        query, key, value, heads_grad, tables, lse, delta, heads, nb
    )
    d_part = (dot(d_query, wq, NT) + dot(d_key, wk, NT) + dot(d_value, wv, NT)).astype(low)
    d_input = d_resid + d_part[:tokens].astype(full)
    for k in range(1, half):
        d_input = d_input + near.send(d_part[k * tokens : (k + 1) * tokens], k).astype(full)
    d_input = from_rows(d_input.astype(low))

    vectors = (
        column_sum(d_attended),
        first_gain_grad,
        first_shift_grad,
        column_sum(d_inner),
        column_sum(d_outer),
        second_gain_grad,
        second_shift_grad,
    )
    packed = jnp.concatenate(vectors).reshape(-1, D)
    packed = jnp.pad(packed, ((0, 128 - packed.shape[0]), (0, 0)))
    out_grad = jnp.concatenate([out_grad, packed], 0).astype(low)
    outer_grad = summed(outer_grad, [near, far, y, z]).astype(full)
    inner_grad = summed(inner_grad, [near, y, z, far]).astype(full)
    out_grad = summed(out_grad, [near, z, far, y]).astype(full)

    def with_bias(weight_grad, bias_grad):
        extra = jnp.pad(bias_grad[None, :], ((0, 31), (0, 0)))
        return jnp.concatenate([weight_grad, extra], 0).astype(low)

    def heads_summed(value, order):
        value = summed(value, order)
        parts = near.gather(value[None])
        return jnp.concatenate([parts[k] for k in range(half)], 1).astype(full)

    query_grad = heads_summed(
        with_bias(dot(x_all, d_query, TN), column_sum(d_query)), [far, y, z]
    )
    key_grad = heads_summed(dot(x_all, d_key, TN).astype(low), [y, z, far])
    value_grad = heads_summed(
        with_bias(dot(x_all, d_value, TN), column_sum(d_value)), [z, far, y]
    )
    at_768 = out_grad[D:]
    return (
        result,
        d_input,
        query_grad[:D],
        query_grad[D],
        key_grad,
        value_grad[:D],
        value_grad[D],
        out_grad[:D],
        at_768[0],
        at_768[1],
        at_768[2],
        inner_grad,
        at_768[3:7].reshape(-1),
        outer_grad,
        at_768[7],
        at_768[8],
        at_768[9],
    )


def solution(mesh):
    tokens = P("rows", "seq", None)
    in_specs = (tokens,) + (P(),) * 15 + (P("rows"), P("rows", None, None), tokens)
    out_specs = (tokens, tokens) + (P(),) * 15
    return jax.shard_map(
        partial(per_device, mesh.shape["seq"], mesh.shape["rows"]),
        mesh=mesh,
        in_specs=in_specs,
        out_specs=out_specs,
        check_vma=False,
    )
```

```python
import functools
from functools import partial

import jax
import jax.numpy as jnp
from jax import lax
from jax.experimental import pallas as pl
from jax.experimental.pallas import tpu as pltpu
from jax.sharding import PartitionSpec as P

D = 768
HEADS = 12
HEAD = 64
BLOCK = 64
SETS = 8
CHIPS_Z = 4

EPSILON = 1e-05
NEG_FILL = -1e30

NT = (((1,), (1,)), ((), ()))
NN = (((1,), (0,)), ((), ()))
TN = (((0,), (0,)), ((), ()))


def dot(left, right, dims):
    return lax.dot_general(left, right, dims, preferred_element_type=jnp.float32)


def head_groups(heads):
    groups, at = [], 0
    while at < heads:
        n = 2 if heads - at >= 2 else 1
        groups.append((at, n))
        at += n
    return groups


def lanes_of(at, n):
    return slice(at * HEAD, (at + n) * HEAD)


def diagonal(n, rows):
    row = lax.broadcasted_iota(jnp.int32, (n * rows, n * HEAD), 0) // rows
    lane = lax.broadcasted_iota(jnp.int32, (n * rows, n * HEAD), 1) // HEAD
    return (row == lane).astype(jnp.float32)


def spread_heads(block, diag, n):
    if n == 1:
        return block
    return jnp.concatenate([block] * n, 0) * diag.astype(block.dtype)


def fold_heads(full, diag, n):
    if n == 1:
        return full
    rows = full.shape[0] // n
    kept = full * diag
    out = kept[:rows]
    for h in range(1, n):
        out = out + kept[h * rows : (h + 1) * rows]
    return out


def rows_of(slot):
    return pl.ds(pl.multiple_of(slot * BLOCK, BLOCK), BLOCK)


def gather_rows(ref, slots, lanes):
    return jnp.concatenate([ref[rows_of(s), lanes] for s in slots], 0)


def as_row(column):
    n = column.shape[0]
    same = lax.broadcasted_iota(jnp.int32, (n, n), 0) == lax.broadcasted_iota(jnp.int32, (n, n), 1)
    return jnp.sum(jnp.where(same, column, 0.0), 0, keepdims=True)


def attend_kernel(
    heads,
    nb,
    abreast,
    key_at_ref,
    query_at_ref,
    q_ref,
    k_ref,
    v_ref,
    task_bias_ref,
    lead_bias_ref,
    o_ref,
    lse_ref,
    top_ref,
    sum_ref,
    acc_ref,
):
    groups = head_groups(heads)
    scale = jnp.bfloat16(HEAD**-0.5)
    diags = {n: diagonal(n, BLOCK) for _, n in groups}

    def local(i, carry):
        work, scores, probs = [], [], []
        for u in range(abreast):
            t = abreast * i + u
            ks = [key_at_ref[t, b] for b in range(SETS)]
            work += [(t, ks, query_at_ref[t], lanes_of(at, n), n) for at, n in groups]
        for t, ks, qs, lanes, n in work:
            query = spread_heads(q_ref[rows_of(qs), lanes] * scale, diags[n], n)
            score = dot(query, gather_rows(k_ref, ks, lanes), NT)
            scores.append(score + task_bias_ref[pl.ds(t, 1), :])
        for score in scores:
            top = jnp.max(score, 1, keepdims=True)
            prob = jnp.exp(score - top)
            probs.append((prob.astype(jnp.bfloat16), top, jnp.sum(prob, 1, keepdims=True)))
        for (t, ks, qs, lanes, n), (prob, top, total) in zip(work, probs):
            out = dot(prob, gather_rows(v_ref, ks, lanes), NN) * (1.0 / total)
            out = fold_heads(out, diags[n], n)
            o_ref[rows_of(qs), lanes] = out.astype(jnp.bfloat16)
            lse_ref[qs, :, lanes] = as_row(top + jnp.log(total))
        return carry

    lax.fori_loop(0, (nb - 2) // abreast, local, 0)

    rows = 2 * BLOCK
    qs = query_at_ref[nb - 2]
    lead_rows = pl.ds(pl.multiple_of(qs * BLOCK, BLOCK), rows)
    top_ref[...] = jnp.full_like(top_ref, NEG_FILL)
    sum_ref[...] = jnp.zeros_like(sum_ref)
    acc_ref[...] = jnp.zeros_like(acc_ref)

    def chunk(c, carry):
        keys = pl.ds(pl.multiple_of(c * (SETS * BLOCK), SETS * BLOCK), SETS * BLOCK)
        scores, probs = [], []
        for at, n in groups:
            lanes = lanes_of(at, n)
            query = spread_heads(q_ref[lead_rows, lanes] * scale, diagonal(n, rows), n)
            scores.append(dot(query, k_ref[keys, lanes], NT) + lead_bias_ref[pl.ds(c, 1), :])
        for g, ((at, n), score) in enumerate(zip(groups, scores)):
            was = top_ref[g, : n * rows, :1]
            top = jnp.maximum(was, jnp.max(score, 1, keepdims=True))
            prob = jnp.exp(score - top)
            keep = jnp.exp(was - top)
            total = sum_ref[g, : n * rows, :1] * keep + jnp.sum(prob, 1, keepdims=True)
            top_ref[g, : n * rows, :] = jnp.broadcast_to(top, (n * rows, 128))
            sum_ref[g, : n * rows, :] = jnp.broadcast_to(total, (n * rows, 128))
            probs.append((prob.astype(jnp.bfloat16), keep))
        for g, ((at, n), (prob, keep)) in enumerate(zip(groups, probs)):
            part = dot(prob, v_ref[keys, lanes_of(at, n)], NN)
            space = (g, slice(0, n * rows), slice(0, n * HEAD))
            acc_ref[space] = acc_ref[space] * keep + part
        return carry

    lax.fori_loop(0, nb // SETS, chunk, 0)
    for g, (at, n) in enumerate(groups):
        lanes = lanes_of(at, n)
        total = sum_ref[g, : n * rows, :1]
        out = acc_ref[g, : n * rows, : n * HEAD] * (1.0 / total)
        o_ref[lead_rows, lanes] = fold_heads(out, diagonal(n, rows), n).astype(jnp.bfloat16)
        lse = top_ref[g, : n * rows, :1] + jnp.log(total)
        each = [as_row(lse[h * rows : (h + 1) * rows]) for h in range(n)]
        for b in range(2):
            part = slice(b * BLOCK, (b + 1) * BLOCK)
            lse_ref[qs + b, :, lanes] = jnp.concatenate([row[:, part] for row in each], 1)


def attend_back_kernel(
    heads,
    nb,
    tasks,
    abreast,
    pieces,
    key_at_ref,
    bias_at_ref,
    query_at_ref,
    q_ref,
    k_ref,
    v_ref,
    o_ref,
    lse_ref,
    bias_ref,
    *rest,
):
    dq_ref, dk_ref, dv_ref, dq_acc, dk_acc, dv_acc, delta_ref, g_ref = rest[-8:]
    rows = nb * BLOCK // pieces
    for i in range(pieces):
        g_ref[i * rows : (i + 1) * rows, :] = rest[i][...]
    groups = head_groups(heads)
    diags = {n: diagonal(n, BLOCK) for _, n in groups}
    dq_acc[...] = jnp.zeros_like(dq_acc)
    dk_acc[...] = jnp.zeros_like(dk_acc)
    dv_acc[...] = jnp.zeros_like(dv_acc)
    scale = HEAD**-0.5

    for at, n in groups:
        lanes = lanes_of(at, n)
        row = lax.broadcasted_iota(jnp.int32, (16, n * HEAD), 0)
        pick = row == lax.broadcasted_iota(jnp.int32, (16, n * HEAD), 1) // HEAD
        pick = pick.astype(jnp.float32).astype(jnp.bfloat16)
        for s in range(0, nb, 4):
            some = slice(s * BLOCK, (s + 4) * BLOCK)
            both = g_ref[some, lanes].astype(jnp.float32) * o_ref[some, lanes].astype(jnp.float32)
            high = both.astype(jnp.bfloat16)
            less = (both - high.astype(jnp.float32)).astype(jnp.bfloat16)
            delta = dot(pick, high, NT) + dot(pick, less, NT)
            for j in range(4):
                part = slice(j * BLOCK, (j + 1) * BLOCK)
                delta_ref[s + j, :, lanes] = jnp.concatenate(
                    [delta[h : h + 1, part] for h in range(n)], 1
                )

    def several(i, carry):
        work, scores, probs, grads = [], [], [], []
        for u in range(abreast):
            t = abreast * i + u
            ks = [key_at_ref[t, b] for b in range(SETS)]
            bs = [bias_at_ref[t, b] for b in range(SETS)]
            work += [(ks, bs, query_at_ref[t], lanes_of(at, n), n) for at, n in groups]
        for ks, bs, qs, lanes, n in work:
            diag = diags[n]
            query = spread_heads(q_ref[rows_of(qs), lanes] * jnp.bfloat16(scale), diag, n)
            grad = spread_heads(g_ref[rows_of(qs), lanes], diag, n)
            keys = gather_rows(k_ref, ks, lanes)
            score = dot(keys, query, NT)
            d_prob = dot(gather_rows(v_ref, ks, lanes), grad, NT)
            scores.append((query, grad, keys, score, d_prob))
        for (ks, bs, qs, lanes, n), (query, grad, keys, score, d_prob) in zip(work, scores):
            bias = gather_rows(bias_ref, bs, slice(None))[:, : n * HEAD]
            prob = jnp.exp(score + bias - lse_ref[qs, :, lanes])
            d_score = (prob * (d_prob - delta_ref[qs, :, lanes])).astype(jnp.bfloat16)
            probs.append((prob.astype(jnp.bfloat16), d_score))
        for (query, grad, keys, _, _), (prob, d_score) in zip(scores, probs):
            grads.append((dot(prob, grad, NN), dot(d_score, query, NN), dot(d_score, keys, TN)))
        for (ks, bs, qs, lanes, n), (d_value, d_key, d_query) in zip(work, grads):
            before = [(dk_acc[rows_of(a), lanes], dv_acc[rows_of(a), lanes]) for a in bs]
            for j, a in enumerate(bs):
                part = slice(j * BLOCK, (j + 1) * BLOCK)
                dk_acc[rows_of(a), lanes] = before[j][0] + d_key[part]
                dv_acc[rows_of(a), lanes] = before[j][1] + d_value[part]
            dq_acc[rows_of(qs), lanes] += fold_heads(d_query, diags[n], n) * scale
        return carry

    lax.fori_loop(0, tasks // abreast, several, 0)
    dq_ref[...] = dq_acc[...].astype(jnp.bfloat16)
    dk_ref[...] = dk_acc[: nb * BLOCK].astype(jnp.bfloat16)
    dv_ref[...] = dv_acc[: nb * BLOCK].astype(jnp.bfloat16)


VMEM = pl.BlockSpec(memory_space=pltpu.VMEM)
SMEM = pl.BlockSpec(memory_space=pltpu.SMEM)


def columns(array, at, width):
    if array.shape[1] == width or width % 128 == 0:
        return array, pl.BlockSpec((array.shape[0], width), lambda i: (0, at))
    array = array[:, at * width : (at + 1) * width]
    return array, pl.BlockSpec(array.shape, lambda i: (0, 0))


def attend(qkv, tables, heads, nb):
    key_at, _, query_at, _, task_bias, lead_bias = tables
    width = heads * HEAD
    operands, specs = zip(*[columns(qkv, i, width) for i in range(3)])
    groups = len(head_groups(heads))
    return pl.pallas_call(
        partial(attend_kernel, heads, nb, 2),
        grid=(1,),
        out_shape=(
            jax.ShapeDtypeStruct((nb * BLOCK, width), jnp.bfloat16),
            jax.ShapeDtypeStruct((nb, 1, width), jnp.float32),
        ),
        in_specs=[SMEM] * 2 + list(specs) + [VMEM] * 2,
        out_specs=(VMEM, VMEM),
        scratch_shapes=[
            pltpu.VMEM((groups, 4 * BLOCK, 128), jnp.float32),
            pltpu.VMEM((groups, 4 * BLOCK, 128), jnp.float32),
            pltpu.VMEM((groups, 4 * BLOCK, 128), jnp.float32),
        ],
        compiler_params=pltpu.CompilerParams(vmem_limit_bytes=48 << 20),
        cost_estimate=pl.CostEstimate(
            flops=20_000_000_000, bytes_accessed=8 << 20, transcendentals=0
        ),
        name="attend",
    )(key_at, query_at, *operands, task_bias, lead_bias)


def attend_back(qkv, grads, context, lse, tables, heads, nb, held, at):
    key_at, bias_at, query_at, bias, _, _ = tables
    total = context.shape[1]
    width = heads * HEAD
    parts = total // width
    operands, specs = zip(
        *[columns(qkv, i * parts + at, width) for i in range(3)], columns(context, at, width)
    )
    pieces, piece_specs = zip(*[columns(g, at, width) for g in grads])
    lse_spec = pl.BlockSpec((nb, 1, width), lambda i: (0, 0, at))
    out = jax.ShapeDtypeStruct((nb * BLOCK, total), jnp.bfloat16)
    out_spec = pl.BlockSpec((nb * BLOCK, width), lambda i: (0, at))
    count = 3 + len(operands) + 2 + len(pieces)
    return pl.pallas_call(
        partial(attend_back_kernel, heads, nb, key_at.shape[0], 5, len(pieces)),
        grid=(1,),
        out_shape=(out, out, out),
        in_specs=[SMEM] * 3
        + list(specs)
        + [lse_spec, VMEM]
        + list(piece_specs)
        + [pl.BlockSpec(memory_space=pl.ANY)] * len(held),
        out_specs=(out_spec,) * 3,
        input_output_aliases={count + i: i for i in range(len(held))},
        scratch_shapes=[
            pltpu.VMEM((nb * BLOCK, width), jnp.float32),
            pltpu.VMEM(((nb + 1) * BLOCK, width), jnp.float32),
            pltpu.VMEM(((nb + 1) * BLOCK, width), jnp.float32),
            pltpu.VMEM((nb, 1, width), jnp.float32),
            pltpu.VMEM((nb * BLOCK, width), jnp.bfloat16),
        ],
        compiler_params=pltpu.CompilerParams(vmem_limit_bytes=52 << 20),
        cost_estimate=pl.CostEstimate(
            flops=15_000_000_000, bytes_accessed=6 << 20, transcendentals=0
        ),
        name="attend_back",
    )(key_at, bias_at, query_at, *operands, lse, bias, *pieces, *held)


def block_tables(block_of_slot, doc, random_blocks):
    nb = random_blocks.shape[0]
    every = jnp.arange(nb, dtype=jnp.int32)
    slot_of_block = jnp.sum(
        jnp.where(block_of_slot[None, :] == every[:, None], every[None, :], 0), 1
    )
    ids = every[2:]
    before, after = ids - 1, ids + 1
    always_on = ids >= 0
    index = jnp.concatenate(
        [jnp.stack([ids * 0, ids * 0 + 1, before, ids, after], -1), random_blocks[2:]], -1
    )
    allowed = jnp.stack(
        [always_on, always_on, before >= 2, always_on, after < nb] + [always_on] * 3, -1
    )
    index = jnp.clip(index, 0, nb - 1)
    slots = jnp.sum(jnp.where(index[..., None] == block_of_slot, every, 0), -1)
    chunks = nb // SETS
    lead = jnp.tile(every.reshape(chunks, SETS), (2, 1))
    key_at = jnp.concatenate([slots, lead], 0)
    bias_at = jnp.concatenate([jnp.where(allowed, slots, nb), lead], 0)
    query_at = jnp.concatenate([slot_of_block[2:], jnp.repeat(slot_of_block[:2], chunks)])
    empty = -key_at.shape[0] % 5
    key_at = jnp.pad(key_at, ((0, empty), (0, 0)))
    bias_at = jnp.pad(bias_at, ((0, empty), (0, 0)), constant_values=nb)
    query_at = jnp.pad(query_at, (0, empty))
    inside = jnp.arange(BLOCK, dtype=jnp.int32)
    bias = jnp.where(block_of_slot[:, None] * BLOCK + inside < doc, 0.0, NEG_FILL)
    bias = bias.astype(jnp.float32)
    lead_bias = bias.reshape(chunks, SETS * BLOCK)
    task_bias = (index[..., None] * BLOCK + inside < doc) & allowed[..., None]
    task_bias = jnp.where(task_bias, 0.0, NEG_FILL).astype(jnp.float32).reshape(nb - 2, -1)
    bias = jnp.concatenate([bias.reshape(-1), jnp.full((BLOCK,), NEG_FILL, jnp.float32)])
    bias = jnp.broadcast_to(bias[:, None], (bias.shape[0], 2 * HEAD))
    return key_at, bias_at, query_at, bias, task_bias, lead_bias


TANH_SCALE = 0.7978845608028654
TANH_CUBE = 0.044715


def norm_rows(value):
    center = value - jnp.mean(value, -1, keepdims=True)
    scale = lax.rsqrt(jnp.mean(center * center, -1, keepdims=True) + EPSILON)
    return center * scale, scale


def norm_back(grad, normal, scale):
    return scale * (
        grad
        - jnp.mean(grad, -1, keepdims=True)
        - normal * jnp.mean(grad * normal, -1, keepdims=True)
    )


def feed_forward_kernel(
    chunk,
    few,
    pieces,
    mine_ref,
    x_ref,
    cot_own_ref,
    cot_came_ref,
    wo_ref,
    w1_ref,
    w2_ref,
    vec_ref,
    b1_ref,
    *refs,
):
    context_refs, refs = refs[:pieces], refs[pieces:]
    result_ref, first_ref, active_ref, d_inner_ref, d_outer_ref, d_attended_ref = refs[:6]
    d_resid_ref, sums_ref, inner_sum_ref = refs[6:9]
    d_context_refs, refs = refs[9 : 9 + pieces], refs[9 + pieces :]
    slope_ref, held_ref, normal_ref, scale_ref, acc_ref = refs
    cols = D // pieces
    low, full = jnp.bfloat16, jnp.float32
    tokens, hidden = active_ref.shape

    @pl.when(pl.program_id(0) == 0)
    def _():
        sums_ref[...] = jnp.zeros_like(sums_ref)
        inner_sum_ref[...] = jnp.zeros_like(inner_sum_ref)

    bo, g1, s1, b2, g2, s2 = [vec_ref[i : i + 1, :] for i in range(6)]

    def each_rows(body):
        def step(i, carry):
            body(pl.ds(pl.multiple_of(i * few, few), few))
            return carry

        lax.fori_loop(0, tokens // few, step, 0)

    def each_columns(body):
        def step(i, carry):
            body(pl.ds(pl.multiple_of(i * chunk, chunk), chunk))
            return carry

        lax.fori_loop(0, hidden // chunk, step, 0)

    def add_sum(row, values):
        sums_ref[row : row + 1, :] += jnp.sum(values, 0, keepdims=True)

    for k, ref in enumerate(context_refs):
        part = dot(ref[...], wo_ref[k * cols : (k + 1) * cols, :], NN)
        acc_ref[...] = part if k == 0 else acc_ref[...] + part

    @each_rows
    def _(rows):
        normal, scale = norm_rows(x_ref[rows, :].astype(full) + acc_ref[rows, :] + bo)
        first = normal * g1 + s1
        normal_ref[rows, :] = normal
        scale_ref[rows, :] = jnp.broadcast_to(scale, (few, 128))
        held_ref[rows, :] = first
        first_ref[rows, :] = first.astype(low)

    @each_columns
    def _(cols):
        u = dot(first_ref[...], w1_ref[:, cols], NN) + b1_ref[:1, cols]
        square = u * u
        tanh = jnp.tanh(u * (TANH_SCALE + (TANH_SCALE * TANH_CUBE) * square))
        share = 0.5 * tanh + 0.5
        active_ref[:, cols] = (u * share).astype(low)
        slope_ref[:, cols] = share + (0.5 * u) * (1.0 - tanh * tanh) * (
            TANH_SCALE + (3 * TANH_SCALE * TANH_CUBE) * square
        )

    acc_ref[...] = dot(active_ref[...], w2_ref[...], NN)

    @each_rows
    def _(rows):
        normal, scale = norm_rows(held_ref[rows, :] + acc_ref[rows, :] + b2)
        result_ref[rows, :] = (normal * g2 + s2).astype(low)
        own = pl.program_id(0) == 0
        cot = jnp.where(own, cot_own_ref[0, rows, :], cot_came_ref[rows, :]).astype(full)
        d_second = norm_back(cot * g2, normal, scale)
        held_ref[rows, :] = d_second
        d_outer = d_second.astype(low)
        d_outer_ref[rows, :] = d_outer
        add_sum(3, d_outer.astype(full))
        add_sum(4, cot * normal)
        add_sum(5, cot)

    @each_columns
    def _(cols):
        d_inner = (dot(d_outer_ref[...], w2_ref[cols, :], NT) * slope_ref[:, cols]).astype(low)
        d_inner_ref[:, cols] = d_inner
        inner_sum_ref[:1, cols] += jnp.sum(d_inner.astype(full), 0, keepdims=True)

    acc_ref[...] = dot(d_inner_ref[...], w1_ref[...], NT)

    @each_rows
    def _(rows):
        d_first = held_ref[rows, :] + acc_ref[rows, :]
        normal = normal_ref[rows, :]
        add_sum(1, d_first * normal)
        add_sum(2, d_first)
        d_resid = norm_back(d_first * g1, normal, scale_ref[rows, :1])
        d_resid_ref[rows, :] = d_resid
        d_attended = d_resid.astype(low)
        d_attended_ref[rows, :] = d_attended
        add_sum(0, d_attended.astype(full))

    for k, ref in enumerate(d_context_refs):
        ref[...] = dot(d_attended_ref[...], wo_ref[k * cols : (k + 1) * cols, :], NT).astype(low)


def feed_forward(mine, x, cot, cot_came, context, wo, w1, w2, vec, b1):
    low, full = jnp.bfloat16, jnp.float32
    tile, hidden = cot_came.shape[0], w1.shape[1]
    tokens, cols = 2 * tile, context[0].shape[1]
    row = pl.BlockSpec((tile, D), lambda i, at: (i, 0))
    part = pl.BlockSpec((tile, cols), lambda i, at: (i, 0))
    wide = pl.BlockSpec((tile, hidden), lambda i, at: (i, 0))
    once = pl.Buffered(1)
    whole = lambda a: pl.BlockSpec(a.shape, lambda i, at: (0,) * a.ndim, pipeline_mode=once)
    shape = jax.ShapeDtypeStruct
    return pl.pallas_call(
        partial(feed_forward_kernel, 512, 128, len(context)),
        grid_spec=pltpu.PrefetchScalarGridSpec(
            num_scalar_prefetch=1,
            grid=(tokens // tile,),
            in_specs=[
                row,
                pl.BlockSpec((1, tile, D), lambda i, at: (at[0], 0, 0), pipeline_mode=once),
            ]
            + [whole(a) for a in (cot_came, wo, w1, w2, vec, b1)]
            + [part] * len(context),
            out_specs=[row, row, wide, wide, row, row, row]
            + [pl.BlockSpec((8, n), lambda i, at: (0, 0)) for n in (D, hidden)]
            + [part] * len(context),
            scratch_shapes=[
                pltpu.VMEM((tile, hidden), full),
                pltpu.VMEM((tile, D), full),
                pltpu.VMEM((tile, D), full),
                pltpu.VMEM((tile, 128), full),
                pltpu.VMEM((tile, D), full),
            ],
        ),
        out_shape=[
            shape((tokens, D), low),
            shape((tokens, D), low),
            shape((tokens, hidden), low),
            shape((tokens, hidden), low),
            shape((tokens, D), low),
            shape((tokens, D), low),
            shape((tokens, D), full),
            shape((8, D), full),
            shape((8, hidden), full),
        ]
        + [shape((tokens, cols), low)] * len(context),
        compiler_params=pltpu.CompilerParams(vmem_limit_bytes=58 << 20),
        cost_estimate=pl.CostEstimate(
            flops=50_000_000_000, bytes_accessed=40 << 20, transcendentals=0
        ),
        name="feed_forward",
    )(jnp.reshape(mine, (1,)).astype(jnp.int32), x, cot, cot_came, wo, w1, w2, vec, b1, *context)


def wide_kernel(at_ref, left_ref, right_ref, out_ref, turned_ref):
    i = pl.program_id(0)

    @pl.when(i == 0)
    def _():
        turned_ref[...] = left_ref[...].T

    rows = out_ref.shape[0]
    some = pl.ds(pl.multiple_of(lax.rem(i, D // rows) * rows, rows), rows)
    out_ref[...] = dot(turned_ref[some, :], right_ref[...], NN).astype(jnp.bfloat16)


def tall_kernel(at_ref, left_ref, right_ref, out_ref):
    out_ref[...] = dot(left_ref[...], right_ref[...], TN).astype(jnp.bfloat16)


def tall_product(left, right, half, count, tile):
    tokens, width = right.shape[0], left.shape[1]
    part = width // count
    per = part // tile
    return pl.pallas_call(
        tall_kernel,
        grid_spec=pltpu.PrefetchScalarGridSpec(
            num_scalar_prefetch=1,
            grid=(per,),
            in_specs=[
                pl.BlockSpec((tokens, tile), lambda i, at: (0, at[0] * per + i)),
                pl.BlockSpec((tokens, right.shape[1]), lambda i, at: (0, 0)),
            ],
            out_specs=pl.BlockSpec((tile, right.shape[1]), lambda i, at: (i, 0)),
        ),
        out_shape=jax.ShapeDtypeStruct((part, right.shape[1]), jnp.bfloat16),
        compiler_params=pltpu.CompilerParams(vmem_limit_bytes=48 << 20),
        cost_estimate=pl.CostEstimate(
            flops=2 * tokens * part * right.shape[1], bytes_accessed=8 << 20, transcendentals=0
        ),
        name="tall_product",
    )(jnp.reshape(half, (1,)).astype(jnp.int32), left, right)


def wide_product(left, right, half, count, rows):
    tokens, width = right.shape
    part = width // count
    blocks, per = part // D, D // rows
    return pl.pallas_call(
        wide_kernel,
        grid_spec=pltpu.PrefetchScalarGridSpec(
            num_scalar_prefetch=1,
            grid=(blocks * per,),
            in_specs=[
                pl.BlockSpec((tokens, D), lambda i, at: (0, 0)),
                pl.BlockSpec((tokens, D), lambda i, at: (0, at[0] * blocks + i // per)),
            ],
            out_specs=pl.BlockSpec((rows, D), lambda i, at: (i, 0)),
            scratch_shapes=[pltpu.VMEM((D, tokens), jnp.bfloat16)],
        ),
        out_shape=jax.ShapeDtypeStruct((part, D), jnp.bfloat16),
        compiler_params=pltpu.CompilerParams(vmem_limit_bytes=48 << 20),
        cost_estimate=pl.CostEstimate(
            flops=2 * tokens * part * D, bytes_accessed=8 << 20, transcendentals=0
        ),
        name="wide_product",
    )(jnp.reshape(half, (1,)).astype(jnp.int32), left, right)


def heads_kernel(x_ref, d_query_ref, d_key_ref, d_value_ref, out_ref, turned_ref):
    tokens, rows = x_ref.shape[0], turned_ref.shape[0]

    @pl.when(pl.program_id(0) == 0)
    def _():
        turned_ref[:D, :] = x_ref[...].T
        row = lax.broadcasted_iota(jnp.int32, (rows - D, tokens), 0)
        turned_ref[D:, :] = (row == 0).astype(jnp.float32).astype(jnp.bfloat16)

    for i, ref in enumerate((d_query_ref, d_key_ref, d_value_ref)):

        @pl.when(pl.program_id(0) == i)
        def _():
            out_ref[...] = dot(turned_ref[...], ref[...], NN).astype(jnp.bfloat16)


def heads_products(x, d_query, d_key, d_value):
    tokens, cols = d_query.shape
    rows = D + 32
    each = pl.BlockSpec((tokens, cols), lambda i: (0, 0))
    return pl.pallas_call(
        heads_kernel,
        grid=(3,),
        in_specs=[pl.BlockSpec((tokens, D), lambda i: (0, 0)), each, each, each],
        out_specs=pl.BlockSpec((rows, cols), lambda i: (0, i)),
        out_shape=jax.ShapeDtypeStruct((rows, 3 * cols), jnp.bfloat16),
        scratch_shapes=[pltpu.VMEM((rows, tokens), jnp.bfloat16)],
        compiler_params=pltpu.CompilerParams(vmem_limit_bytes=48 << 20),
        cost_estimate=pl.CostEstimate(
            flops=6 * tokens * rows * cols, bytes_accessed=8 << 20, transcendentals=0
        ),
        name="heads_products",
    )(x, d_query, d_key, d_value)


def spread_heads_kernel(at_ref, pool_ref, *refs):
    for i, ref in enumerate(refs[-3:]):

        @pl.when(pl.program_id(0) == i)
        def _():
            ref[...] = pool_ref[...].astype(jnp.float32)


def spread_columns(pool, half, held):
    cols = pool.shape[1] // 3
    shape = jax.ShapeDtypeStruct((D, D), jnp.float32)
    return pl.pallas_call(
        spread_heads_kernel,
        grid_spec=pltpu.PrefetchScalarGridSpec(
            num_scalar_prefetch=1,
            grid=(3,),
            in_specs=[pl.BlockSpec((D, cols), lambda i, at: (0, i))]
            + [pl.BlockSpec(memory_space=pl.ANY)] * len(held),
            out_specs=[pl.BlockSpec((D, cols), lambda i, at: (0, at[0]))] * 3,
        ),
        out_shape=[shape] * 3,
        input_output_aliases={2 + i: i for i in range(len(held))},
        compiler_params=pltpu.CompilerParams(vmem_limit_bytes=32 << 20),
        cost_estimate=pl.CostEstimate(flops=0, bytes_accessed=6 << 20, transcendentals=0),
        name="spread_columns",
    )(jnp.reshape(half, (1,)).astype(jnp.int32), pool, *held)


def spread_kernel(at_ref, pool_ref, *refs):
    outer_ref, inner_ref, out_ref = refs[-3:]
    i = pl.program_id(0)
    value = pool_ref[...].astype(jnp.float32)

    @pl.when(i < 4)
    def _():
        outer_ref[...] = value

    @pl.when((i >= 4) & (i < 8))
    def _():
        inner_ref[...] = value

    @pl.when(i == 8)
    def _():
        out_ref[...] = value


def spread_pool(pool, half, held):
    rows = D // 2
    hidden = 8 * rows
    shape = jax.ShapeDtypeStruct

    def inner_at(i, at):
        j = jnp.clip(i - 4, 0, 3)
        return (j % 2, at[0] * 2 + j // 2)

    return pl.pallas_call(
        spread_kernel,
        grid_spec=pltpu.PrefetchScalarGridSpec(
            num_scalar_prefetch=1,
            grid=(9,),
            in_specs=[pl.BlockSpec((rows, D), lambda i, at: (i, 0))]
            + [pl.BlockSpec(memory_space=pl.ANY)] * len(held),
            out_specs=(
                pl.BlockSpec((rows, D), lambda i, at: (at[0] * 4 + jnp.clip(i, 0, 3), 0)),
                pl.BlockSpec((rows, D), inner_at),
                pl.BlockSpec((rows, D), lambda i, at: (at[0], 0)),
            ),
        ),
        out_shape=(
            shape((hidden, D), jnp.float32),
            shape((D, hidden), jnp.float32),
            shape((D, D), jnp.float32),
        ),
        input_output_aliases={2 + i: i for i in range(len(held))},
        compiler_params=pltpu.CompilerParams(vmem_limit_bytes=32 << 20),
        cost_estimate=pl.CostEstimate(flops=0, bytes_accessed=18 << 20, transcendentals=0),
        name="spread_pool",
    )(jnp.reshape(half, (1,)).astype(jnp.int32), pool, *held)


class Ring:
    def __init__(self, axis, size, at, perm):
        self.axis, self.size, self.at, self.perm = axis, size, at, perm

    def send(self, value, by):
        return lax.ppermute(value, self.axis, self.perm(by))


class Pairs:
    def __init__(self, seq, rows, masks, core):
        me = lax.axis_index("seq") * rows + lax.axis_index("rows")
        bits = [lax.rem(me // mask, 2) for mask in masks]
        self.bit = jnp.where(lax.rem(me // core, 2) == 0, bits[0], bits[1])
        self.perm = [(i, i ^ masks[i // core % 2]) for i in range(seq * rows)]

    def swap(self, value):
        return lax.ppermute(value, ("seq", "rows"), self.perm)

    def keep(self, value):
        part = value.shape[0] // 2
        return lax.dynamic_slice_in_dim(value, self.bit * part, part, 0)

    def give(self, value):
        part = value.shape[0] // 2
        return lax.dynamic_slice_in_dim(value, (1 - self.bit) * part, part, 0)

    def halved(self, value, came):
        return (self.keep(value).astype(jnp.float32) + came.astype(jnp.float32)).astype(value.dtype)

    def halve(self, value):
        return self.halved(value, self.swap(self.give(value)))

    def joined(self, value, came):
        first = jnp.where(self.bit == 0, value, came)
        second = jnp.where(self.bit == 0, came, value)
        return jnp.concatenate([first, second], 0)

    def join(self, value):
        return self.joined(value, self.swap(value))


def powers(step, count):
    masks = []
    while count > 1:
        masks.append(step)
        step, count = step * 2, count // 2
    return masks


def make_links(seq, rows):
    half = seq // 2
    deep = CHIPS_Z if rows % CHIPS_Z == 0 else 1
    wide = rows // deep
    s = lax.axis_index("seq")
    near = Ring(
        "seq",
        half,
        lax.rem(s, half),
        lambda by: [(i, i // half * half + (i + by) % half) for i in range(seq)],
    )

    def pairs(first, second=None):
        return Pairs(seq, rows, (first, second or first), rows)

    far_mask = half * rows
    y, z = powers(1, wide), powers(wide, deep)
    far = pairs(far_mask)
    inside = [pairs(mask) for mask in powers(rows, half)]
    main = [pairs(far_mask, y[0]), pairs(y[0], z[0]), pairs(z[0], far_mask)]
    side = [pairs(z[0]), pairs(far_mask), pairs(y[0])]
    last = [pairs(mask) for mask in y[1:] + z[1:]]
    return near, far, inside, [main, side], last


def in_step(values):
    return list(lax.optimization_barrier(tuple(values)))


def cut(value, sizes):
    out, at = [], 0
    for size in sizes:
        out.append(value[at : at + size])
        at += size
    return out


class HalveStep:
    def __init__(self, pairs):
        self.pairs = pairs

    def start(self, parts):
        return [pair.swap(pair.give(part)) for pair, part in zip(self.pairs, parts)]

    def finish(self, parts, came):
        return [pair.halved(*both) for pair, *both in zip(self.pairs, parts, came)]


class JoinStep:
    def __init__(self, pairs):
        self.pairs = pairs

    def start(self, parts):
        return [pair.swap(part) for pair, part in zip(self.pairs, parts)]

    def finish(self, parts, came):
        return [pair.joined(*both) for pair, *both in zip(self.pairs, parts, came)]


class Together:
    def __init__(self, step):
        self.step = step

    def start(self, parts):
        pair = self.step.pairs[0]
        if isinstance(self.step, HalveStep):
            parts = [pair.give(p) for p in parts]
        return cut(pair.swap(jnp.concatenate(parts, 0)), [p.shape[0] for p in parts])

    def finish(self, parts, came):
        return self.step.finish(parts, came)


class Chain:
    def __init__(self, parts, steps):
        self.parts, self.steps, self.came = list(parts), list(steps), None

    def start(self):
        self.came = self.steps[0].start(self.parts)

    def finish(self, *after):
        came = in_step(list(self.came) + list(after))[: len(self.came)]
        self.parts = self.steps.pop(0).finish(self.parts, came)
        self.came = None

    def step(self, *after):
        if self.came is None:
            self.start()
        self.finish(*after)
        if self.steps:
            self.start()


def column_sum(values):
    return jnp.sum(values.astype(jnp.float32), 0)


def per_device(
    seq,
    rows,
    inputs,
    query_weight,
    query_bias,
    key_weight,
    value_weight,
    value_bias,
    output_weight,
    output_bias,
    first_gain,
    first_shift,
    inner_weight,
    inner_bias,
    outer_weight,
    outer_bias,
    second_gain,
    second_shift,
    doc_tokens,
    random_blocks,
    cotangent,
):
    low, full = jnp.bfloat16, jnp.float32
    near, far, inside, routes, last = make_links(seq, rows)
    main, side = routes
    half = seq // 2
    width = inputs.shape[1]
    tokens = 2 * width
    nb = random_blocks.shape[1]
    heads = HEADS // half
    cols = heads * HEAD
    mine, at = far.bit, near.at

    def own_and_other(array):
        own = lax.dynamic_index_in_dim(array, mine, 0, False)
        return own, lax.dynamic_index_in_dim(array, 1 - mine, 0, False)

    def from_rows(own, other):
        return jnp.where(mine == 0, jnp.stack([own, other]), jnp.stack([other, own]))

    x_own, x_other = own_and_other(inputs)
    x_came = far.swap(x_other)
    x_parts = [x_own, x_came]
    for k in range(1, half):
        x_parts += [near.send(x_own, half - k), near.send(x_came, half - k)]
    x_all = jnp.concatenate(x_parts, 0)
    x_all, cotangent = lax.optimization_barrier((x_all, cotangent))
    cot_came = far.swap(lax.dynamic_index_in_dim(cotangent, 1 - mine, 0, False))

    shards = []
    for k in range(half):
        own = mine * half + lax.rem(at + k, half)
        shards += [own, lax.rem(own + half, seq)]
    per_shard = width // BLOCK
    block_of_slot = (
        jnp.stack(shards)[:, None] * per_shard + jnp.arange(per_shard, dtype=jnp.int32)
    ).reshape(-1).astype(jnp.int32)
    doc = lax.dynamic_index_in_dim(doc_tokens, mine, 0, False)
    chosen = lax.dynamic_index_in_dim(random_blocks, mine, 0, False)
    tables = block_tables(block_of_slot, doc, chosen)

    def my_cols(weight):
        return lax.dynamic_slice_in_dim(weight, at * cols, cols, weight.ndim - 1)

    w_qkv = jnp.concatenate([my_cols(w) for w in (query_weight, key_weight, value_weight)], 1)
    b_qkv = jnp.concatenate(
        [my_cols(query_bias), jnp.zeros((cols,), low), my_cols(value_bias)]
    ).astype(full)
    wo = jnp.concatenate(
        [
            lax.dynamic_slice_in_dim(
                output_weight, lax.rem(at + half - k, half) * cols, cols, 0
            )
            for k in range(half)
        ],
        0,
    )
    vec = jnp.stack(
        [output_bias, first_gain, first_shift, outer_bias, second_gain, second_shift]
    ).astype(full)
    vec = jnp.pad(vec, ((0, 2), (0, 0)))
    b1 = jnp.broadcast_to(inner_bias.astype(full), (8, inner_bias.shape[0]))

    qkv = (dot(x_all, w_qkv, NN) + b_qkv).astype(low)
    qkv, wo, vec, b1, *tables = in_step([qkv, wo, vec, b1, *tables])
    heads_context, lse = attend(qkv, tables, heads, nb)
    heads_context, lse, cot_came = in_step([heads_context, lse, cot_came])
    context = [heads_context] + [
        near.send(heads_context[k * tokens : (k + 1) * tokens], k) for k in range(1, half)
    ]
    (
        result,
        first_low,
        active,
        d_inner,
        d_outer,
        d_attended,
        d_resid,
        sums,
        inner_sum,
        *d_context,
    ) = feed_forward(
        mine, x_all, cotangent, cot_came, context, wo, inner_weight, outer_weight, vec, b1
    )
    heads_grad = [d_context[0]] + [near.send(d_context[k], half - k) for k in range(1, half)]

    packed = jnp.concatenate([sums[:6].reshape(-1), inner_sum[0]]).reshape(-1, D)
    packed = jnp.pad(packed, ((0, 256 - packed.shape[0]), (0, 0))).astype(low)

    def shared(product, *beside):
        parts = [product(lax.rem(at + k, half), k) for k in range(1, half)]
        *parts, beside = in_step(parts + list(beside)) + [beside]
        if beside:
            parts, beside = parts[: half - 1], parts[half - 1 :]
        came = [near.send(part, k) for k, part in enumerate(parts, 1)]
        kept = product(at, 0)
        kept, *came = in_step([kept] + came)
        total = kept.astype(full)
        for value in came:
            total = total + value.astype(full)
        return total.astype(low), beside

    def out_product(part, k):
        k = (half - k) % half
        if cols % 128:
            return dot(context[k][:tokens], d_attended, TN).astype(low)
        return tall_product(context[k], d_attended, 0, 1, cols)

    outer_grad, heads_grad = shared(
        lambda part, k: tall_product(active, d_outer, part, half, 384), *heads_grad
    )
    outer_main = outer_grad.shape[0] * 2 // 3
    early = Chain([outer_grad[:outer_main], outer_grad[outer_main:]], [HalveStep([main[0], side[0]])])
    outer_grad, first_low, d_attended = in_step([outer_grad, first_low, d_attended])
    early.start()
    inner_grad, early.came = shared(
        lambda part, k: wide_product(first_low, d_inner, part, half, 384), *early.came
    )
    early.finish()
    out_grad, _ = shared(out_product)
    packed, _ = shared(
        lambda part, k: lax.dynamic_slice_in_dim(packed, part * (256 // half), 256 // half, 0)
    )
    inner_main = inner_grad.shape[0] * 11 // 12
    mixed = jnp.concatenate([inner_grad[inner_main:], out_grad, packed], 0)
    rest = Chain([inner_grad[:inner_main], mixed], [HalveStep([main[0], side[0]])])
    heads_grad[0], *rest.parts = in_step([heads_grad[0]] + early.parts + rest.parts)
    early.parts, rest.parts = rest.parts[:2], rest.parts[2:]

    first_sizes = [
        (outer_main // 2, inner_main // 2),
        ((outer_grad.shape[0] - outer_main) // 2, mixed.shape[0] // 2),
    ]
    first = Chain([], [HalveStep([main[i], side[i]]) for i in (1, 2)])
    first.steps += [Together(HalveStep([pair] * 2)) for pair in last]
    first.steps += [Together(JoinStep([pair] * 2)) for pair in reversed(last)]
    first.steps += [JoinStep([main[i], side[i]]) for i in (2, 1)]

    steps = cols // 128 if cols % 128 == 0 else 1
    d_qkv = ()
    result_half = result[width:]
    result_came = []
    for k in range(steps):
        chain = first if first.parts else rest
        chain.start()
        if k == 2:
            result_came.append(far.swap(result_half[: width // 2]))
        d_qkv = attend_back(
            qkv, heads_grad, heads_context, lse, tables, heads // steps, nb, d_qkv, k
        )
        d_query, d_key, d_value, *came = in_step(list(d_qkv) + chain.came + result_came)
        d_qkv = (d_query, d_key, d_value)
        chain.came, result_came = came[: len(chain.came)], came[len(chain.came) :]
        chain.finish()
        if chain is rest:
            first.parts = [
                jnp.concatenate([e, r], 0) for e, r in zip(early.parts, rest.parts)
            ]
        d_query, *first.parts = in_step([d_query] + first.parts)
        d_qkv = (d_query, d_key, d_value)

    first.start()
    result_came.append(far.swap(result_half[width // 2 * len(result_came) :]))
    if cols % 128 == 0:
        heads_part = heads_products(x_all, *d_qkv)
    else:
        sums_of = [jnp.pad(column_sum(d)[None, :], ((0, 31), (0, 0))) for d in d_qkv]
        heads_part = [
            jnp.concatenate([dot(x_all, d, TN), total], 0) for d, total in zip(d_qkv, sums_of)
        ]
        heads_part = jnp.concatenate(heads_part, 1).astype(low)
    wq, wk, wv = (w_qkv[:, i * cols : (i + 1) * cols] for i in range(3))
    d_part = (dot(d_query, wq, NT) + dot(d_key, wk, NT) + dot(d_value, wv, NT)).astype(low)
    d_part, heads_part, *came = in_step([d_part, heads_part] + first.came + result_came)
    first.came, result_came = came[: len(first.came)], came[len(first.came) :]
    first.finish()

    second = Chain([heads_part], [HalveStep([main[i]]) for i in range(3)])
    second.steps += [HalveStep([pair]) for pair in last]
    second.steps += [JoinStep([pair]) for pair in reversed(last)]
    second.steps += [JoinStep([main[i]]) for i in (2, 1, 0)]
    second.start()
    first.start()
    d_came = [near.send(d_part[k * tokens : (k + 1) * tokens], k) for k in range(1, half)]
    result = from_rows(result[:width], jnp.concatenate(result_came, 0))
    second.step()
    d_came = in_step(d_came + second.parts)[: half - 1]
    d_input = d_resid + d_part[:tokens].astype(full)
    for value in d_came:
        d_input = d_input + value.astype(full)
    d_input = d_input.astype(low)
    first.step(*second.parts)
    d_input_came = far.swap(d_input[width:])
    while first.steps:
        second.step(*first.parts)
        first.step(*second.parts)
    first = Chain(
        [p for share, size in zip(first.parts, first_sizes) for p in cut(share, size)],
        [JoinStep([main[0], main[0], side[0], side[0]])],
    )
    first.start()
    second.step()
    second.step()
    d_input_came, *_ = in_step([d_input_came] + second.parts)
    d_input = from_rows(d_input[:width], d_input_came)
    first.finish(*second.parts)
    outer_a, inner_a, outer_b, mixed = first.parts
    sizes = [inner_grad.shape[0] - inner_main, out_grad.shape[0], packed.shape[0]]
    inner_b, out_grad, packed = cut(mixed, sizes)
    pool = jnp.concatenate([outer_a, outer_b, inner_a, inner_b, out_grad], 0)
    packed = packed[None]
    for pairs in inside:
        packed = pairs.join(packed)
    packed = packed.reshape(-1, D).astype(full)
    if half == 2:
        pool_came = near.send(pool, 1)
        placed = spread_pool(pool, at, ())
        second.finish(*placed)
        if second.steps:
            second.start()
        pool_came, *_ = in_step([pool_came] + second.parts)
        placed = spread_pool(pool_came, 1 - at, placed)
        outer_grad, inner_grad, out_grad = placed
    else:
        pool = pool[None]
        for pairs in inside:
            pool = pairs.join(pool)
        pool = pool.astype(full)
        parts = [outer_grad.shape[0], inner_grad.shape[0], out_grad.shape[0]]
        outer_grad, inner_grad, out_grad = (
            jnp.concatenate([cut(p, parts)[i] for p in pool], 0) for i in range(3)
        )
        inner_grad = inner_grad.reshape(-1, D, D).transpose(1, 0, 2).reshape(D, -1)

    while second.steps:
        second.step()
    heads_parts = second.parts[0]
    if half == 2:
        heads_came = near.send(heads_parts, 1)
        query_grad, key_grad, value_grad = spread_columns(
            heads_came, 1 - at, spread_columns(heads_parts, at, ())
        )
        biases = [p[D].astype(full) for p in (heads_parts, heads_came)]
        biases = jnp.where(at == 0, jnp.stack(biases), jnp.stack(biases[::-1]))
        query_bias_grad = biases[:, :cols].reshape(-1)
        value_bias_grad = biases[:, 2 * cols :].reshape(-1)
    else:
        heads_parts = heads_parts[None]
        for pairs in inside:
            heads_parts = pairs.join(heads_parts)
        query_grad, key_grad, value_grad = (
            jnp.concatenate([p[:, i * cols : (i + 1) * cols] for p in heads_parts], 1).astype(full)
            for i in range(3)
        )
        query_bias_grad, value_bias_grad = query_grad[D], value_grad[D]
        query_grad, key_grad, value_grad = query_grad[:D], key_grad[:D], value_grad[:D]
    return (
        result,
        d_input,
        query_grad,
        query_bias_grad,
        key_grad,
        value_grad,
        value_bias_grad,
        out_grad,
        packed[0],
        packed[1],
        packed[2],
        inner_grad,
        packed[6:10].reshape(-1),
        outer_grad,
        packed[3],
        packed[4],
        packed[5],
    )


def solution(mesh):
    tokens = P("rows", "seq", None)
    in_specs = (tokens,) + (P(),) * 15 + (P("rows"), P("rows", None, None), tokens)
    out_specs = (tokens, tokens) + (P(),) * 15
    return jax.shard_map(
        partial(per_device, mesh.shape["seq"], mesh.shape["rows"]),
        mesh=mesh,
        in_specs=in_specs,
        out_specs=out_specs,
        check_vma=False,
    )
```

```python
import functools
from functools import partial

import jax
import jax.numpy as jnp
from jax import lax
from jax.experimental import pallas as pl
from jax.experimental.pallas import tpu as pltpu
from jax.sharding import PartitionSpec as P

D = 768
HEADS = 12
HEAD = 64
BLOCK = 64
SETS = 8
CHIPS_Z = 4

EPSILON = 1e-05
NEG_FILL = -1e30

SHORT = pl.CostEstimate(flops=1 << 20, bytes_accessed=1 << 10, transcendentals=0)

NT = (((1,), (1,)), ((), ()))
NN = (((1,), (0,)), ((), ()))
TN = (((0,), (0,)), ((), ()))


def dot(left, right, dims):
    return lax.dot_general(left, right, dims, preferred_element_type=jnp.float32)


def head_groups(heads):
    groups, at = [], 0
    while at < heads:
        n = 2 if heads - at >= 2 else 1
        groups.append((at, n))
        at += n
    return groups


def lanes_of(at, n):
    return slice(at * HEAD, (at + n) * HEAD)


def diagonal(n, rows):
    row = lax.broadcasted_iota(jnp.int32, (n * rows, n * HEAD), 0) // rows
    lane = lax.broadcasted_iota(jnp.int32, (n * rows, n * HEAD), 1) // HEAD
    return (row == lane).astype(jnp.float32)


def spread_heads(block, diag, n):
    if n == 1:
        return block
    return jnp.concatenate([block] * n, 0) * diag.astype(block.dtype)


def fold_heads(full, diag, n):
    if n == 1:
        return full
    rows = full.shape[0] // n
    kept = full * diag
    out = kept[:rows]
    for h in range(1, n):
        out = out + kept[h * rows : (h + 1) * rows]
    return out


def rows_of(slot):
    return pl.ds(pl.multiple_of(slot * BLOCK, BLOCK), BLOCK)


def gather_rows(ref, slots, lanes):
    return jnp.concatenate([ref[rows_of(s), lanes] for s in slots], 0)


def as_row(column):
    n = column.shape[0]
    same = lax.broadcasted_iota(jnp.int32, (n, n), 0) == lax.broadcasted_iota(jnp.int32, (n, n), 1)
    return jnp.sum(jnp.where(same, column, 0.0), 0, keepdims=True)


def attend_kernel(
    heads,
    nb,
    abreast,
    key_at_ref,
    query_at_ref,
    q_ref,
    k_ref,
    v_ref,
    task_bias_ref,
    lead_bias_ref,
    o_ref,
    lse_ref,
):
    groups = head_groups(heads)
    scale = jnp.bfloat16(HEAD**-0.5)
    diags = {n: diagonal(n, BLOCK) for _, n in groups}

    def local(i, carry):
        work, scores, probs = [], [], []
        for u in range(abreast):
            t = abreast * i + u
            ks = [key_at_ref[t, b] for b in range(SETS)]
            work += [(t, ks, query_at_ref[t], lanes_of(at, n), n) for at, n in groups]
        for t, ks, qs, lanes, n in work:
            query = spread_heads(q_ref[rows_of(qs), lanes] * scale, diags[n], n)
            score = dot(query, gather_rows(k_ref, ks, lanes), NT)
            scores.append(score + task_bias_ref[pl.ds(t, 1), :])
        for score in scores:
            top = jnp.max(score, 1, keepdims=True)
            prob = jnp.exp(score - top)
            probs.append((prob.astype(jnp.bfloat16), top, jnp.sum(prob, 1, keepdims=True)))
        for (t, ks, qs, lanes, n), (prob, top, total) in zip(work, probs):
            out = dot(prob, gather_rows(v_ref, ks, lanes), NN) * (1.0 / total)
            out = fold_heads(out, diags[n], n)
            o_ref[rows_of(qs), lanes] = out.astype(jnp.bfloat16)
            lse_ref[qs, :, lanes] = as_row(top + jnp.log(total))
        return carry

    lax.fori_loop(0, (nb - 2) // abreast, local, 0)

    rows = 2 * BLOCK
    qs = query_at_ref[nb - 2]
    lead_rows = pl.ds(pl.multiple_of(qs * BLOCK, BLOCK), rows)
    scores, probs = [], []
    for at, n in groups:
        lanes = lanes_of(at, n)
        query = spread_heads(q_ref[lead_rows, lanes] * scale, diagonal(n, rows), n)
        scores.append(dot(query, k_ref[:, lanes], NT) + lead_bias_ref[...])
    for score in scores:
        top = jnp.max(score, 1, keepdims=True)
        prob = jnp.exp(score - top)
        probs.append((prob.astype(jnp.bfloat16), top, jnp.sum(prob, 1, keepdims=True)))
    for (at, n), (prob, top, total) in zip(groups, probs):
        lanes = lanes_of(at, n)
        out = dot(prob, v_ref[:, lanes], NN) * (1.0 / total)
        o_ref[lead_rows, lanes] = fold_heads(out, diagonal(n, rows), n).astype(jnp.bfloat16)
        lse = top + jnp.log(total)
        each = [as_row(lse[h * rows : (h + 1) * rows]) for h in range(n)]
        for b in range(2):
            part = slice(b * BLOCK, (b + 1) * BLOCK)
            lse_ref[qs + b, :, lanes] = jnp.concatenate([row[:, part] for row in each], 1)


def attend_back_kernel(
    heads,
    nb,
    abreast,
    pieces,
    key_at_ref,
    bias_at_ref,
    query_at_ref,
    q_ref,
    k_ref,
    v_ref,
    o_ref,
    lse_ref,
    bias_ref,
    *rest,
):
    dq_ref, dk_ref, dv_ref, dk_acc, dv_acc, delta_ref, g_ref = rest[-7:]
    rows = nb * BLOCK // pieces
    for i in range(pieces):
        g_ref[i * rows : (i + 1) * rows, :] = rest[i][...]
    groups = head_groups(heads)
    diags = {n: diagonal(n, BLOCK) for _, n in groups}
    every = nb * BLOCK
    dk_acc[every:, :] = jnp.zeros_like(dk_acc[every:, :])
    dv_acc[every:, :] = jnp.zeros_like(dv_acc[every:, :])
    scale = HEAD**-0.5

    for at, n in groups:
        lanes = lanes_of(at, n)
        row = lax.broadcasted_iota(jnp.int32, (16, n * HEAD), 0)
        pick = row == lax.broadcasted_iota(jnp.int32, (16, n * HEAD), 1) // HEAD
        pick = pick.astype(jnp.float32).astype(jnp.bfloat16)
        for s in range(0, nb, 4):
            some = slice(s * BLOCK, (s + 4) * BLOCK)
            both = g_ref[some, lanes].astype(jnp.float32) * o_ref[some, lanes].astype(jnp.float32)
            high = both.astype(jnp.bfloat16)
            less = (both - high.astype(jnp.float32)).astype(jnp.bfloat16)
            delta = dot(pick, high, NT) + dot(pick, less, NT)
            for j in range(4):
                part = slice(j * BLOCK, (j + 1) * BLOCK)
                delta_ref[s + j, :, lanes] = jnp.concatenate(
                    [delta[h : h + 1, part] for h in range(n)], 1
                )

    both_rows = 2 * BLOCK
    lead = query_at_ref[nb - 2]
    lead_rows = pl.ds(pl.multiple_of(lead * BLOCK, BLOCK), both_rows)

    def lead_row(ref, lanes, n):
        first, second = ref[lead, :, lanes], ref[lead + 1, :, lanes]
        heads_of = [slice(h * HEAD, (h + 1) * HEAD) for h in range(n)]
        return jnp.concatenate([r[:, h] for h in heads_of for r in (first, second)], 1)

    for at, n in groups:
        lanes, diag = lanes_of(at, n), diagonal(n, both_rows)
        query = spread_heads(q_ref[lead_rows, lanes] * jnp.bfloat16(scale), diag, n)
        grad = spread_heads(g_ref[lead_rows, lanes], diag, n)
        score = dot(k_ref[:, lanes], query, NT)
        bias = jnp.concatenate([bias_ref[:every, :]] * n, 1)
        prob = jnp.exp(score + bias - lead_row(lse_ref, lanes, n))
        d_prob = dot(v_ref[:, lanes], grad, NT)
        d_score = (prob * (d_prob - lead_row(delta_ref, lanes, n))).astype(jnp.bfloat16)
        dv_acc[:every, lanes] = dot(prob.astype(jnp.bfloat16), grad, NN)
        dk_acc[:every, lanes] = dot(d_score, query, NN)
        d_query = fold_heads(dot(d_score, k_ref[:, lanes], TN), diag, n) * scale
        dq_ref[lead_rows, lanes] = d_query.astype(jnp.bfloat16)

    def several(i, carry):
        work, scores, probs, grads = [], [], [], []
        for u in range(abreast):
            t = abreast * i + u
            ks = [key_at_ref[t, b] for b in range(SETS)]
            bs = [bias_at_ref[t, b] for b in range(SETS)]
            work += [(ks, bs, query_at_ref[t], lanes_of(at, n), n) for at, n in groups]
        for ks, bs, qs, lanes, n in work:
            diag = diags[n]
            query = spread_heads(q_ref[rows_of(qs), lanes] * jnp.bfloat16(scale), diag, n)
            grad = spread_heads(g_ref[rows_of(qs), lanes], diag, n)
            keys = gather_rows(k_ref, ks, lanes)
            score = dot(keys, query, NT)
            d_prob = dot(gather_rows(v_ref, ks, lanes), grad, NT)
            scores.append((query, grad, keys, score, d_prob))
        for (ks, bs, qs, lanes, n), (query, grad, keys, score, d_prob) in zip(work, scores):
            bias = gather_rows(bias_ref, bs, slice(None))[:, : n * HEAD]
            prob = jnp.exp(score + bias - lse_ref[qs, :, lanes])
            d_score = (prob * (d_prob - delta_ref[qs, :, lanes])).astype(jnp.bfloat16)
            probs.append((prob.astype(jnp.bfloat16), d_score))
        for (query, grad, keys, _, _), (prob, d_score) in zip(scores, probs):
            grads.append((dot(prob, grad, NN), dot(d_score, query, NN), dot(d_score, keys, TN)))
        for (ks, bs, qs, lanes, n), (d_value, d_key, d_query) in zip(work, grads):
            before = [(dk_acc[rows_of(a), lanes], dv_acc[rows_of(a), lanes]) for a in bs]
            for j, a in enumerate(bs):
                part = slice(j * BLOCK, (j + 1) * BLOCK)
                dk_acc[rows_of(a), lanes] = before[j][0] + d_key[part]
                dv_acc[rows_of(a), lanes] = before[j][1] + d_value[part]
            d_query = fold_heads(d_query, diags[n], n) * scale
            dq_ref[rows_of(qs), lanes] = d_query.astype(jnp.bfloat16)
        return carry

    lax.fori_loop(0, (nb - 2) // abreast, several, 0)
    dk_ref[...] = dk_acc[: nb * BLOCK].astype(jnp.bfloat16)
    dv_ref[...] = dv_acc[: nb * BLOCK].astype(jnp.bfloat16)


VMEM = pl.BlockSpec(memory_space=pltpu.VMEM)
SMEM = pl.BlockSpec(memory_space=pltpu.SMEM)


def columns(array, at, width):
    if array.shape[1] == width or width % 128 == 0:
        return array, pl.BlockSpec((array.shape[0], width), lambda i: (0, at))
    array = array[:, at * width : (at + 1) * width]
    return array, pl.BlockSpec(array.shape, lambda i: (0, 0))


def attend(qkv, tables, heads, nb):
    key_at, _, query_at, _, task_bias, lead_bias = tables
    width = heads * HEAD
    operands, specs = zip(*[columns(qkv, i, width) for i in range(3)])
    return pl.pallas_call(
        partial(attend_kernel, heads, nb, 2),
        grid=(1,),
        out_shape=(
            jax.ShapeDtypeStruct((nb * BLOCK, width), jnp.bfloat16),
            jax.ShapeDtypeStruct((nb, 1, width), jnp.float32),
        ),
        in_specs=[SMEM] * 2 + list(specs) + [VMEM] * 2,
        out_specs=(VMEM, VMEM),
        compiler_params=pltpu.CompilerParams(vmem_limit_bytes=48 << 20),
        cost_estimate=pl.CostEstimate(
            flops=20_000_000_000, bytes_accessed=8 << 20, transcendentals=0
        ),
        name="attend",
    )(key_at, query_at, *operands, task_bias, lead_bias)


def attend_back(qkv, grads, context, lse, tables, heads, nb, held, at):
    key_at, bias_at, query_at, bias, _, _ = tables
    total = context.shape[1]
    width = heads * HEAD
    parts = total // width
    operands, specs = zip(
        *[columns(qkv, i * parts + at, width) for i in range(3)], columns(context, at, width)
    )
    pieces, piece_specs = zip(*[columns(g, at, width) for g in grads])
    lse_spec = pl.BlockSpec((nb, 1, width), lambda i: (0, 0, at))
    out = jax.ShapeDtypeStruct((nb * BLOCK, total), jnp.bfloat16)
    out_spec = pl.BlockSpec((nb * BLOCK, width), lambda i: (0, at))
    count = 3 + len(operands) + 2 + len(pieces)
    abreast = 5 if (nb - 2) % 5 == 0 else 2
    return pl.pallas_call(
        partial(attend_back_kernel, heads, nb, abreast, len(pieces)),
        grid=(1,),
        out_shape=(out, out, out),
        in_specs=[SMEM] * 3
        + list(specs)
        + [lse_spec, VMEM]
        + list(piece_specs)
        + [pl.BlockSpec(memory_space=pl.ANY)] * len(held),
        out_specs=(out_spec,) * 3,
        input_output_aliases={count + i: i for i in range(len(held))},
        scratch_shapes=[
            pltpu.VMEM(((nb + 1) * BLOCK, width), jnp.float32),
            pltpu.VMEM(((nb + 1) * BLOCK, width), jnp.float32),
            pltpu.VMEM((nb, 1, width), jnp.float32),
            pltpu.VMEM((nb * BLOCK, width), jnp.bfloat16),
        ],
        compiler_params=pltpu.CompilerParams(vmem_limit_bytes=52 << 20),
        cost_estimate=pl.CostEstimate(
            flops=15_000_000_000, bytes_accessed=6 << 20, transcendentals=0
        ),
        name="attend_back",
    )(key_at, bias_at, query_at, *operands, lse, bias, *pieces, *held)


def block_tables(block_of_slot, doc, random_blocks):
    nb = random_blocks.shape[0]
    every = jnp.arange(nb, dtype=jnp.int32)
    slot_of_block = jnp.sum(
        jnp.where(block_of_slot[None, :] == every[:, None], every[None, :], 0), 1
    )
    ids = every[2:]
    before, after = ids - 1, ids + 1
    always_on = ids >= 0
    index = jnp.concatenate(
        [jnp.stack([ids * 0, ids * 0 + 1, before, ids, after], -1), random_blocks[2:]], -1
    )
    allowed = jnp.stack(
        [always_on, always_on, before >= 2, always_on, after < nb] + [always_on] * 3, -1
    )
    index = jnp.clip(index, 0, nb - 1)
    slots = jnp.sum(jnp.where(index[..., None] == block_of_slot, every, 0), -1)
    key_at = slots
    bias_at = jnp.where(allowed, slots, nb)
    query_at = jnp.concatenate([slot_of_block[2:], slot_of_block[:2]])
    inside = jnp.arange(BLOCK, dtype=jnp.int32)
    bias = jnp.where(block_of_slot[:, None] * BLOCK + inside < doc, 0.0, NEG_FILL)
    bias = bias.astype(jnp.float32)
    lead_bias = bias.reshape(1, -1)
    task_bias = (index[..., None] * BLOCK + inside < doc) & allowed[..., None]
    task_bias = jnp.where(task_bias, 0.0, NEG_FILL).astype(jnp.float32).reshape(nb - 2, -1)
    bias = jnp.concatenate([bias.reshape(-1), jnp.full((BLOCK,), NEG_FILL, jnp.float32)])
    bias = jnp.broadcast_to(bias[:, None], (bias.shape[0], 2 * HEAD))
    return key_at, bias_at, query_at, bias, task_bias, lead_bias


TANH_SCALE = 0.7978845608028654
TANH_CUBE = 0.044715


def norm_rows(value):
    center = value - jnp.mean(value, -1, keepdims=True)
    scale = lax.rsqrt(jnp.mean(center * center, -1, keepdims=True) + EPSILON)
    return center * scale, scale


def norm_back(grad, normal, scale):
    return scale * (
        grad
        - jnp.mean(grad, -1, keepdims=True)
        - normal * jnp.mean(grad * normal, -1, keepdims=True)
    )


def feed_forward_kernel(
    chunk,
    few,
    pieces,
    mine_ref,
    x_ref,
    cot_own_ref,
    cot_came_ref,
    wo_ref,
    w1_hbm_ref,
    w2_hbm_ref,
    vec_ref,
    b1_ref,
    *refs,
):
    context_refs, refs = refs[:pieces], refs[pieces:]
    result_ref, first_ref, active_out_ref, d_inner_out_ref, d_outer_ref, d_attended_ref = refs[:6]
    d_resid_ref, sums_ref, inner_sum_ref = refs[6:9]
    d_context_refs, refs = refs[9 : 9 + pieces], refs[9 + pieces :]
    w1_ref, w2_ref, active_ref, d_inner_ref, *refs = refs
    slope_ref, held_ref, normal_ref, scale_ref, acc_ref, sems = refs
    cols = D // pieces
    first_step = pl.program_id(0) == 0
    tile = active_ref.shape[0]
    tokens_at = pl.ds(pl.multiple_of(pl.program_id(0) * tile, tile), tile)
    load_w1 = pltpu.make_async_copy(w1_hbm_ref, w1_ref, sems.at[0])
    load_w2 = pltpu.make_async_copy(w2_hbm_ref, w2_ref, sems.at[1])
    store_active = pltpu.make_async_copy(active_ref, active_out_ref.at[tokens_at, :], sems.at[2])
    store_d_inner = pltpu.make_async_copy(d_inner_ref, d_inner_out_ref.at[tokens_at, :], sems.at[3])
    low, full = jnp.bfloat16, jnp.float32
    tokens, hidden = active_ref.shape

    @pl.when(first_step)
    def _():
        load_w1.start()
        load_w2.start()
        sums_ref[...] = jnp.zeros_like(sums_ref)
        inner_sum_ref[...] = jnp.zeros_like(inner_sum_ref)

    bo, g1, s1, b2, g2, s2 = [vec_ref[i : i + 1, :] for i in range(6)]

    def each_rows(body):
        def step(i, carry):
            body(pl.ds(pl.multiple_of(i * few, few), few))
            return carry

        lax.fori_loop(0, tokens // few, step, 0)

    def each_columns(body):
        def step(i, carry):
            body(pl.ds(pl.multiple_of(i * chunk, chunk), chunk))
            return carry

        lax.fori_loop(0, hidden // chunk, step, 0)

    def add_sum(row, values):
        sums_ref[row : row + 1, :] += jnp.sum(values, 0, keepdims=True)

    for k, ref in enumerate(context_refs):
        part = dot(ref[...], wo_ref[k * cols : (k + 1) * cols, :], NN)
        acc_ref[...] = part if k == 0 else acc_ref[...] + part

    @each_rows
    def _(rows):
        normal, scale = norm_rows(x_ref[rows, :].astype(full) + acc_ref[rows, :] + bo)
        first = normal * g1 + s1
        normal_ref[rows, :] = normal
        scale_ref[rows, :] = jnp.broadcast_to(scale, (few, 128))
        held_ref[rows, :] = first
        first_ref[rows, :] = first.astype(low)

    @pl.when(first_step)
    def _():
        load_w1.wait()

    @each_columns
    def _(cols):
        u = dot(first_ref[...], w1_ref[:, cols], NN) + b1_ref[:1, cols]
        square = u * u
        tanh = jnp.tanh(u * (TANH_SCALE + (TANH_SCALE * TANH_CUBE) * square))
        share = 0.5 * tanh + 0.5
        active_ref[:, cols] = (u * share).astype(low)
        slope_ref[:, cols] = share + (0.5 * u) * (1.0 - tanh * tanh) * (
            TANH_SCALE + (3 * TANH_SCALE * TANH_CUBE) * square
        )

    store_active.start()

    @pl.when(first_step)
    def _():
        load_w2.wait()

    acc_ref[...] = dot(active_ref[...], w2_ref[...], NN)

    @each_rows
    def _(rows):
        normal, scale = norm_rows(held_ref[rows, :] + acc_ref[rows, :] + b2)
        result_ref[rows, :] = (normal * g2 + s2).astype(low)
        own = pl.program_id(0) == 0
        cot = jnp.where(own, cot_own_ref[0, rows, :], cot_came_ref[rows, :]).astype(full)
        d_second = norm_back(cot * g2, normal, scale)
        held_ref[rows, :] = d_second
        d_outer = d_second.astype(low)
        d_outer_ref[rows, :] = d_outer
        add_sum(3, d_outer.astype(full))
        add_sum(4, cot * normal)
        add_sum(5, cot)

    @each_columns
    def _(cols):
        d_inner = (dot(d_outer_ref[...], w2_ref[cols, :], NT) * slope_ref[:, cols]).astype(low)
        d_inner_ref[:, cols] = d_inner
        inner_sum_ref[:1, cols] += jnp.sum(d_inner.astype(full), 0, keepdims=True)

    store_d_inner.start()
    acc_ref[...] = dot(d_inner_ref[...], w1_ref[...], NT)

    @each_rows
    def _(rows):
        d_first = held_ref[rows, :] + acc_ref[rows, :]
        normal = normal_ref[rows, :]
        add_sum(1, d_first * normal)
        add_sum(2, d_first)
        d_resid = norm_back(d_first * g1, normal, scale_ref[rows, :1])
        d_resid_ref[rows, :] = d_resid
        d_attended = d_resid.astype(low)
        d_attended_ref[rows, :] = d_attended
        add_sum(0, d_attended.astype(full))

    for k, ref in enumerate(d_context_refs):
        ref[...] = dot(d_attended_ref[...], wo_ref[k * cols : (k + 1) * cols, :], NT).astype(low)
    store_active.wait()
    store_d_inner.wait()


def feed_forward(mine, x, cot, cot_came, context, wo, w1, w2, vec, b1):
    low, full = jnp.bfloat16, jnp.float32
    tile, hidden = cot_came.shape[0], w1.shape[1]
    tokens, cols = 2 * tile, context[0].shape[1]
    row = pl.BlockSpec((tile, D), lambda i, at: (i, 0))
    part = pl.BlockSpec((tile, cols), lambda i, at: (i, 0))
    there = pl.BlockSpec(memory_space=pl.ANY)
    once = pl.Buffered(1)
    whole = lambda a: pl.BlockSpec(a.shape, lambda i, at: (0,) * a.ndim, pipeline_mode=once)
    shape = jax.ShapeDtypeStruct
    return pl.pallas_call(
        partial(feed_forward_kernel, 1024, 256, len(context)),
        grid_spec=pltpu.PrefetchScalarGridSpec(
            num_scalar_prefetch=1,
            grid=(tokens // tile,),
            in_specs=[
                row,
                pl.BlockSpec((1, tile, D), lambda i, at: (at[0], 0, 0), pipeline_mode=once),
            ]
            + [whole(cot_came), whole(wo), there, there, whole(vec), whole(b1)]
            + [part] * len(context),
            out_specs=[row, row, there, there, row, row, row]
            + [pl.BlockSpec((8, n), lambda i, at: (0, 0)) for n in (D, hidden)]
            + [part] * len(context),
            scratch_shapes=[
                pltpu.VMEM(w1.shape, low),
                pltpu.VMEM(w2.shape, low),
                pltpu.VMEM((tile, hidden), low),
                pltpu.VMEM((tile, hidden), low),
                pltpu.VMEM((tile, hidden), full),
                pltpu.VMEM((tile, D), full),
                pltpu.VMEM((tile, D), full),
                pltpu.VMEM((tile, 128), full),
                pltpu.VMEM((tile, D), full),
                pltpu.SemaphoreType.DMA((4,)),
            ],
        ),
        out_shape=[
            shape((tokens, D), low),
            shape((tokens, D), low),
            shape((tokens, hidden), low),
            shape((tokens, hidden), low),
            shape((tokens, D), low),
            shape((tokens, D), low),
            shape((tokens, D), full),
            shape((8, D), full),
            shape((8, hidden), full),
        ]
        + [shape((tokens, cols), low)] * len(context),
        compiler_params=pltpu.CompilerParams(vmem_limit_bytes=58 << 20),
        cost_estimate=pl.CostEstimate(
            flops=50_000_000_000, bytes_accessed=40 << 20, transcendentals=0
        ),
        name="feed_forward",
    )(jnp.reshape(mine, (1,)).astype(jnp.int32), x, cot, cot_came, wo, w1, w2, vec, b1, *context)


def wide_kernel(at_ref, left_ref, right_ref, *refs):
    *came_refs, out_ref, turned_ref = refs
    i = pl.program_id(0)

    @pl.when(i == 0)
    def _():
        turned_ref[...] = left_ref[...].T

    rows = out_ref.shape[0]
    some = pl.ds(pl.multiple_of(lax.rem(i, D // rows) * rows, rows), rows)
    out_ref[...] = add_came(dot(turned_ref[some, :], right_ref[...], NN), came_refs)


def add_came(total, came_refs):
    for ref in came_refs:
        total = total + ref[...].astype(jnp.float32)
    return total.astype(jnp.bfloat16)


def tall_kernel(at_ref, left_ref, right_ref, *refs):
    *came_refs, out_ref = refs
    out_ref[...] = add_came(dot(left_ref[...], right_ref[...], TN), came_refs)


def tall_product(left, right, half, count, tile, came=()):
    tokens, width = right.shape[0], left.shape[1]
    part = width // count
    per = part // tile
    return pl.pallas_call(
        tall_kernel,
        grid_spec=pltpu.PrefetchScalarGridSpec(
            num_scalar_prefetch=1,
            grid=(per,),
            in_specs=[
                pl.BlockSpec((tokens, tile), lambda i, at: (0, at[0] * per + i)),
                pl.BlockSpec((tokens, right.shape[1]), lambda i, at: (0, 0)),
            ]
            + [pl.BlockSpec((tile, right.shape[1]), lambda i, at: (i, 0))] * len(came),
            out_specs=pl.BlockSpec((tile, right.shape[1]), lambda i, at: (i, 0)),
        ),
        out_shape=jax.ShapeDtypeStruct((part, right.shape[1]), jnp.bfloat16),
        compiler_params=pltpu.CompilerParams(vmem_limit_bytes=48 << 20),
        cost_estimate=pl.CostEstimate(
            flops=2 * tokens * part * right.shape[1], bytes_accessed=8 << 20, transcendentals=0
        ),
        name="tall_product",
    )(jnp.reshape(half, (1,)).astype(jnp.int32), left, right, *came)


def wide_product(left, right, half, count, rows, came=()):
    tokens, width = right.shape
    part = width // count
    blocks, per = part // D, D // rows
    return pl.pallas_call(
        wide_kernel,
        grid_spec=pltpu.PrefetchScalarGridSpec(
            num_scalar_prefetch=1,
            grid=(blocks * per,),
            in_specs=[
                pl.BlockSpec((tokens, D), lambda i, at: (0, 0)),
                pl.BlockSpec((tokens, D), lambda i, at: (0, at[0] * blocks + i // per)),
            ]
            + [pl.BlockSpec((rows, D), lambda i, at: (i, 0))] * len(came),
            out_specs=pl.BlockSpec((rows, D), lambda i, at: (i, 0)),
            scratch_shapes=[pltpu.VMEM((D, tokens), jnp.bfloat16)],
        ),
        out_shape=jax.ShapeDtypeStruct((part, D), jnp.bfloat16),
        compiler_params=pltpu.CompilerParams(vmem_limit_bytes=48 << 20),
        cost_estimate=pl.CostEstimate(
            flops=2 * tokens * part * D, bytes_accessed=8 << 20, transcendentals=0
        ),
        name="wide_product",
    )(jnp.reshape(half, (1,)).astype(jnp.int32), left, right, *came)


def heads_kernel(x_ref, d_query_ref, d_key_ref, d_value_ref, out_ref, turned_ref):
    tokens, rows = x_ref.shape[0], turned_ref.shape[0]

    @pl.when(pl.program_id(0) == 0)
    def _():
        turned_ref[:D, :] = x_ref[...].T
        row = lax.broadcasted_iota(jnp.int32, (rows - D, tokens), 0)
        turned_ref[D:, :] = (row == 0).astype(jnp.float32).astype(jnp.bfloat16)

    for i, ref in enumerate((d_query_ref, d_key_ref, d_value_ref)):

        @pl.when(pl.program_id(0) == i)
        def _():
            out_ref[...] = dot(turned_ref[...], ref[...], NN).astype(jnp.bfloat16)


def heads_products(x, d_query, d_key, d_value):
    tokens, cols = d_query.shape
    rows = D + 32
    each = pl.BlockSpec((tokens, cols), lambda i: (0, 0))
    return pl.pallas_call(
        heads_kernel,
        grid=(3,),
        in_specs=[pl.BlockSpec((tokens, D), lambda i: (0, 0)), each, each, each],
        out_specs=pl.BlockSpec((rows, cols), lambda i: (0, i)),
        out_shape=jax.ShapeDtypeStruct((rows, 3 * cols), jnp.bfloat16),
        scratch_shapes=[pltpu.VMEM((rows, tokens), jnp.bfloat16)],
        compiler_params=pltpu.CompilerParams(vmem_limit_bytes=48 << 20),
        cost_estimate=pl.CostEstimate(
            flops=6 * tokens * rows * cols, bytes_accessed=8 << 20, transcendentals=0
        ),
        name="heads_products",
    )(x, d_query, d_key, d_value)


def spread_heads_kernel(at_ref, pool_ref, *refs):
    for i, ref in enumerate(refs[-3:]):

        @pl.when(pl.program_id(0) == i)
        def _():
            ref[...] = pool_ref[...].astype(jnp.float32)


def spread_columns(pool, half, held):
    cols = pool.shape[1] // 3
    shape = jax.ShapeDtypeStruct((D, D), jnp.float32)
    return pl.pallas_call(
        spread_heads_kernel,
        grid_spec=pltpu.PrefetchScalarGridSpec(
            num_scalar_prefetch=1,
            grid=(3,),
            in_specs=[pl.BlockSpec((D, cols), lambda i, at: (0, i))]
            + [pl.BlockSpec(memory_space=pl.ANY)] * len(held),
            out_specs=[pl.BlockSpec((D, cols), lambda i, at: (0, at[0]))] * 3,
        ),
        out_shape=[shape] * 3,
        input_output_aliases={2 + i: i for i in range(len(held))},
        compiler_params=pltpu.CompilerParams(vmem_limit_bytes=32 << 20),
        cost_estimate=SHORT,
        name="spread_columns",
    )(jnp.reshape(half, (1,)).astype(jnp.int32), pool, *held)


def spread_outer_kernel(at_ref, first_ref, second_ref, *refs):
    i, blocks = pl.program_id(0), pl.num_programs(0)

    @pl.when(i < blocks - 1)
    def _():
        refs[-1][...] = first_ref[...].astype(jnp.float32)

    @pl.when(i == blocks - 1)
    def _():
        refs[-1][...] = second_ref[...].astype(jnp.float32)


def spread_inner_kernel(at_ref, first_ref, second_ref, third_ref, *refs):
    inner_ref, out_ref = refs[-2:]
    i, blocks = pl.program_id(0), pl.num_programs(0) - 1

    @pl.when(i < blocks - 1)
    def _():
        inner_ref[...] = first_ref[...].astype(jnp.float32)

    @pl.when(i == blocks - 1)
    def _():
        inner_ref[...] = second_ref[...].astype(jnp.float32)

    @pl.when(i == blocks)
    def _():
        out_ref[...] = third_ref[...].astype(jnp.float32)


def spread_call(kernel, name, half, grid, operands, specs, out_shapes, out_specs, held):
    return pl.pallas_call(
        kernel,
        grid_spec=pltpu.PrefetchScalarGridSpec(
            num_scalar_prefetch=1,
            grid=grid,
            in_specs=specs + [pl.BlockSpec(memory_space=pl.ANY)] * len(held),
            out_specs=out_specs,
        ),
        out_shape=[jax.ShapeDtypeStruct(s, jnp.float32) for s in out_shapes],
        input_output_aliases={1 + len(operands) + i: i for i in range(len(held))},
        compiler_params=pltpu.CompilerParams(vmem_limit_bytes=32 << 20),
        cost_estimate=SHORT,
        name=name,
    )(jnp.reshape(half, (1,)).astype(jnp.int32), *operands, *held)


def spread_outer(first, second, half, held):
    rows = second.shape[0]
    blocks = first.shape[0] // rows + 1
    return spread_call(
        spread_outer_kernel,
        "spread_outer",
        half,
        (blocks,),
        (first, second),
        [
            pl.BlockSpec((rows, D), lambda i, at: (jnp.minimum(i, blocks - 2), 0)),
            pl.BlockSpec((rows, D), lambda i, at: (0, 0)),
        ],
        [(2 * rows * blocks, D)],
        [pl.BlockSpec((rows, D), lambda i, at: (at[0] * blocks + i, 0))],
        held,
    )


def spread_inner(first, mixed, half, held):
    rows = 256
    per = D // rows
    blocks = first.shape[0] // rows + 1
    wide = blocks // per
    out_rows = D // 2

    def inner_at(i, at):
        j = jnp.minimum(i, blocks - 1)
        return (j % per, at[0] * wide + j // per)

    return spread_call(
        spread_inner_kernel,
        "spread_inner",
        half,
        (blocks + 1,),
        (first, mixed, mixed),
        [
            pl.BlockSpec((rows, D), lambda i, at: (jnp.minimum(i, blocks - 2), 0)),
            pl.BlockSpec((rows, D), lambda i, at: (mixed.shape[0] // rows - 1, 0)),
            pl.BlockSpec((out_rows, D), lambda i, at: (0, 0)),
        ],
        [(D, 2 * wide * D), (D, D)],
        [
            pl.BlockSpec((rows, D), inner_at),
            pl.BlockSpec((out_rows, D), lambda i, at: (at[0], 0)),
        ],
        held,
    )


class Ring:
    def __init__(self, axis, size, at, perm):
        self.axis, self.size, self.at, self.perm = axis, size, at, perm

    def send(self, value, by):
        return lax.ppermute(value, self.axis, self.perm(by))


class Pairs:
    def __init__(self, seq, rows, masks, core):
        me = lax.axis_index("seq") * rows + lax.axis_index("rows")
        bits = [lax.rem(me // mask, 2) for mask in masks]
        self.bit = jnp.where(lax.rem(me // core, 2) == 0, bits[0], bits[1])
        self.perm = [(i, i ^ masks[i // core % 2]) for i in range(seq * rows)]

    def swap(self, value):
        return lax.ppermute(value, ("seq", "rows"), self.perm)

    def keep(self, value):
        part = value.shape[0] // 2
        return lax.dynamic_slice_in_dim(value, self.bit * part, part, 0)

    def give(self, value):
        part = value.shape[0] // 2
        return lax.dynamic_slice_in_dim(value, (1 - self.bit) * part, part, 0)

    def halved(self, value, came):
        return (self.keep(value).astype(jnp.float32) + came.astype(jnp.float32)).astype(value.dtype)

    def halve(self, value):
        return self.halved(value, self.swap(self.give(value)))

    def joined(self, value, came):
        first = jnp.where(self.bit == 0, value, came)
        second = jnp.where(self.bit == 0, came, value)
        return jnp.concatenate([first, second], 0)

    def join(self, value):
        return self.joined(value, self.swap(value))


def powers(step, count):
    masks = []
    while count > 1:
        masks.append(step)
        step, count = step * 2, count // 2
    return masks


def make_links(seq, rows):
    half = seq // 2
    deep = CHIPS_Z if rows % CHIPS_Z == 0 else 1
    wide = rows // deep
    s = lax.axis_index("seq")
    near = Ring(
        "seq",
        half,
        lax.rem(s, half),
        lambda by: [(i, i // half * half + (i + by) % half) for i in range(seq)],
    )

    def pairs(first, second=None):
        return Pairs(seq, rows, (first, second or first), rows)

    far_mask = half * rows
    y, z = powers(1, wide), powers(wide, deep)
    far = pairs(far_mask)
    inside = [pairs(mask) for mask in powers(rows, half)]
    main = [pairs(far_mask, y[0]), pairs(y[0], z[0]), pairs(z[0], far_mask)]
    side = [pairs(z[0]), pairs(far_mask), pairs(y[0])]
    last = [pairs(mask) for mask in y[1:] + z[1:]]
    return near, far, inside, [main, side], last


def in_step(values):
    return list(lax.optimization_barrier(tuple(values)))


def cut(value, sizes):
    out, at = [], 0
    for size in sizes:
        out.append(value[at : at + size])
        at += size
    return out


class HalveStep:
    def __init__(self, pairs):
        self.pairs = pairs

    def start(self, parts):
        return [pair.swap(pair.give(part)) for pair, part in zip(self.pairs, parts)]

    def finish(self, parts, came):
        return [pair.halved(*both) for pair, *both in zip(self.pairs, parts, came)]


class JoinStep:
    def __init__(self, pairs):
        self.pairs = pairs

    def start(self, parts):
        return [pair.swap(part) for pair, part in zip(self.pairs, parts)]

    def finish(self, parts, came):
        return [pair.joined(*both) for pair, *both in zip(self.pairs, parts, came)]


class SumStep:
    def __init__(self, pair):
        self.pair = pair

    def start(self, parts):
        return cut(self.pair.swap(jnp.concatenate(parts, 0)), [p.shape[0] for p in parts])

    def finish(self, parts, came):
        return [
            (p.astype(jnp.float32) + c.astype(jnp.float32)).astype(p.dtype)
            for p, c in zip(parts, came)
        ]


class Chain:
    def __init__(self, parts, steps):
        self.parts, self.steps, self.came = list(parts), list(steps), None

    def start(self):
        self.came = self.steps[0].start(self.parts)

    def finish(self, *after):
        came = in_step(list(self.came) + list(after))[: len(self.came)]
        self.parts = self.steps.pop(0).finish(self.parts, came)
        self.came = None

    def step(self, *after):
        if self.came is None:
            self.start()
        self.finish(*after)
        if self.steps:
            self.start()


def column_sum(values):
    return jnp.sum(values.astype(jnp.float32), 0)


def per_device(
    seq,
    rows,
    inputs,
    query_weight,
    query_bias,
    key_weight,
    value_weight,
    value_bias,
    output_weight,
    output_bias,
    first_gain,
    first_shift,
    inner_weight,
    inner_bias,
    outer_weight,
    outer_bias,
    second_gain,
    second_shift,
    doc_tokens,
    random_blocks,
    cotangent,
):
    low, full = jnp.bfloat16, jnp.float32
    near, far, inside, routes, last = make_links(seq, rows)
    main, side = routes
    half = seq // 2
    width = inputs.shape[1]
    tokens = 2 * width
    nb = random_blocks.shape[1]
    heads = HEADS // half
    cols = heads * HEAD
    mine, at = far.bit, near.at

    def own_and_other(array):
        own = lax.dynamic_index_in_dim(array, mine, 0, False)
        return own, lax.dynamic_index_in_dim(array, 1 - mine, 0, False)

    def from_rows(own, other):
        return jnp.where(mine == 0, jnp.stack([own, other]), jnp.stack([other, own]))

    def by_device(values):
        stacked = jnp.stack(values)
        order = lax.rem(at + half - jnp.arange(half), half)
        return jnp.take(stacked, order, axis=0) if half > 2 else jnp.where(at == 0, stacked, stacked[::-1])

    def by_two(values):
        return [values[i : i + 2] for i in range(0, len(values), 2)]

    x_own, x_other = own_and_other(inputs)
    x_came = far.swap(x_other)

    shards = []
    for k in range(half):
        own = mine * half + lax.rem(at + k, half)
        shards += [own, lax.rem(own + half, seq)]
    per_shard = width // BLOCK
    block_of_slot = (
        jnp.stack(shards)[:, None] * per_shard + jnp.arange(per_shard, dtype=jnp.int32)
    ).reshape(-1).astype(jnp.int32)
    doc = lax.dynamic_index_in_dim(doc_tokens, mine, 0, False)
    chosen = lax.dynamic_index_in_dim(random_blocks, mine, 0, False)
    tables = block_tables(block_of_slot, doc, chosen)

    def my_cols(weight):
        return lax.dynamic_slice_in_dim(weight, at * cols, cols, weight.ndim - 1)

    w_qkv = jnp.concatenate([my_cols(w) for w in (query_weight, key_weight, value_weight)], 1)
    b_qkv = jnp.concatenate(
        [my_cols(query_bias), jnp.zeros((cols,), low), my_cols(value_bias)]
    ).astype(full)
    wo = jnp.concatenate(
        [
            lax.dynamic_slice_in_dim(
                output_weight, lax.rem(at + half - k, half) * cols, cols, 0
            )
            for k in range(half)
        ],
        0,
    )
    vec = jnp.stack(
        [output_bias, first_gain, first_shift, outer_bias, second_gain, second_shift]
    ).astype(full)
    vec = jnp.pad(vec, ((0, 2), (0, 0)))
    b1 = jnp.broadcast_to(inner_bias.astype(full), (8, inner_bias.shape[0]))

    x_came, w_qkv, b_qkv, wo, vec, b1, *tables = in_step(
        [x_came, w_qkv, b_qkv, wo, vec, b1, *tables]
    )
    x_parts = [x_own, x_came]
    for k in range(1, half):
        x_parts += [near.send(x_own, half - k), near.send(x_came, half - k)]
    x_all, cotangent = in_step([jnp.concatenate(x_parts, 0), cotangent])
    cot_came = far.swap(lax.dynamic_index_in_dim(cotangent, 1 - mine, 0, False))
    qkv = (dot(x_all, w_qkv, NN) + b_qkv).astype(low)
    qkv, cotangent = in_step([qkv, cotangent])
    heads_context, lse = attend(qkv, tables, heads, nb)
    heads_context, lse, cot_came = in_step([heads_context, lse, cot_came])
    context = [heads_context] + [
        near.send(heads_context[k * tokens : (k + 1) * tokens], k) for k in range(1, half)
    ]
    (
        result,
        first_low,
        active,
        d_inner,
        d_outer,
        d_attended,
        d_resid,
        sums,
        inner_sum,
        *d_context,
    ) = feed_forward(
        mine, x_all, cotangent, cot_came, context, wo, inner_weight, outer_weight, vec, b1
    )
    heads_grad = [d_context[0]] + [near.send(d_context[k], half - k) for k in range(1, half)]

    packed = jnp.concatenate([sums[:6].reshape(-1), inner_sum[0]]).reshape(-1, D)
    packed = jnp.pad(packed, ((0, 256 - packed.shape[0]), (0, 0))).astype(low)

    def outer_product(part, k, came=()):
        return tall_product(active, d_outer, part, half, 768, came)

    def inner_product(part, k, came=()):
        return wide_product(first_low, d_inner, part, half, 768, came)

    def out_product(part, k, came=()):
        k = (half - k) % half
        if cols % 128:
            total = dot(context[k][:tokens], d_attended, TN)
            return sum([c.astype(full) for c in came], total).astype(low)
        return tall_product(context[k], d_attended, 0, 1, cols, came)

    def packed_part(part, k, came=()):
        size = 256 // half
        total = lax.dynamic_slice_in_dim(packed, part * size, size, 0).astype(full)
        return sum([c.astype(full) for c in came], total).astype(low)

    def give(product):
        return [product(lax.rem(at + k, half), k) for k in range(1, half)]

    def send(parts):
        return [near.send(part, k) for k, part in enumerate(parts, 1)]

    outer_give = give(outer_product)
    outer_give[0], first_low, d_attended = in_step([outer_give[0], first_low, d_attended])
    outer_came = send(outer_give)
    inner_came = send(give(inner_product))
    out_came = send(give(out_product))
    packed_came = send(give(packed_part))
    outer_grad = outer_product(at, 0, outer_came)
    outer_main = outer_grad.shape[0] * 3 // 4
    early = Chain([outer_grad[:outer_main], outer_grad[outer_main:]], [HalveStep([main[0], side[0]])])
    early.start()
    inner_came[0], out_came[0], packed_came[0], *early.parts = in_step(
        [inner_came[0], out_came[0], packed_came[0]] + early.parts
    )
    inner_grad = inner_product(at, 0, inner_came)
    out_grad = out_product(at, 0, out_came)
    packed = packed_part(at, 0, packed_came)
    inner_grad, out_grad, packed, *early.came = in_step(
        [inner_grad, out_grad, packed] + early.came
    )
    early.finish()
    inner_main = inner_grad.shape[0] * 5 // 6
    mixed = jnp.concatenate([out_grad, packed, inner_grad[inner_main:]], 0)
    rest = Chain([inner_grad[:inner_main], mixed], [HalveStep([main[0], side[0]])])
    heads_grad[0], *rest.parts = in_step([heads_grad[0]] + early.parts + rest.parts)
    early.parts, rest.parts = rest.parts[:2], rest.parts[2:]

    first_sizes = [
        (outer_main // 2, inner_main // 2),
        ((outer_grad.shape[0] - outer_main) // 2, mixed.shape[0] // 2),
    ]
    first = Chain([], [HalveStep([main[i], side[i]]) for i in (1, 2)])
    first.steps += [SumStep(pair) for pair in last]
    first.steps += [JoinStep([main[i], side[i]]) for i in (2, 1)]

    steps = cols // 128 if cols % 128 == 0 else 1
    d_qkv = ()
    result_half = [result[width : width + width // 2], result[width + width // 2 :]]
    result_came = []
    for k in range(steps):
        chain = first if first.parts else rest
        chain.start()
        if k == 2:
            result_half[0], d_query = in_step([result_half[0], d_qkv[0]])
            d_qkv = (d_query,) + d_qkv[1:]
            result_came.append(far.swap(result_half[0]))
        d_qkv = attend_back(
            qkv, heads_grad, heads_context, lse, tables, heads // steps, nb, d_qkv, k
        )
        d_query, d_key, d_value, *came = in_step(list(d_qkv) + chain.came + result_came)
        d_qkv = (d_query, d_key, d_value)
        chain.came, result_came = came[: len(chain.came)], came[len(chain.came) :]
        chain.finish()
        if chain is rest:
            first.parts = [
                jnp.concatenate([e, r], 0) for e, r in zip(early.parts, rest.parts)
            ]
        d_query, *first.parts = in_step([d_query] + first.parts)
        d_qkv = (d_query, d_key, d_value)

    while len(first.steps) > 3:
        first.start()
        first.finish()
    sums_at_last = first.steps.pop(0)
    last_came = sums_at_last.start(first.parts[:1]) + sums_at_last.start(first.parts[1:])
    result_half[1:], d_query = in_step([*result_half[1:], d_query])[:-1], d_query
    result_came += [far.swap(piece) for piece in result_half[len(result_came) :]]
    if cols % 128 == 0:
        heads_part = heads_products(x_all, *d_qkv)
    else:
        sums_of = [jnp.pad(column_sum(d)[None, :], ((0, 31), (0, 0))) for d in d_qkv]
        heads_part = [
            jnp.concatenate([dot(x_all, d, TN), total], 0) for d, total in zip(d_qkv, sums_of)
        ]
        heads_part = jnp.concatenate(heads_part, 1).astype(low)
    heads_part, d_query, *result_came = in_step([heads_part, d_query] + result_came)

    second = Chain([heads_part], [HalveStep([main[i]]) for i in range(3)])
    second.steps += [SumStep(pair) for pair in last]
    second.steps += [JoinStep([main[i]]) for i in (2, 1, 0)]
    second.start()
    wq, wk, wv = (w_qkv[:, i * cols : (i + 1) * cols] for i in range(3))
    d_part = (dot(d_query, wq, NT) + dot(d_key, wk, NT) + dot(d_value, wv, NT)).astype(low)
    result = from_rows(result[:width], jnp.concatenate(result_came, 0))
    d_part, result, *came = in_step([d_part, result] + last_came + second.came)
    first.parts, second.came = sums_at_last.finish(first.parts, came[:2]), came[2:]
    second.finish()

    def together(*beside):
        count = len(first.came or ())
        values = in_step(list(first.came or ()) + second.came + list(beside))
        if count:
            first.came = values[:count]
            first.finish()
        second.came = values[count : count + len(second.came)]
        second.finish()
        return values[len(values) - len(beside) :]

    second.start()
    first.start()
    d_came = [near.send(d_part[k * tokens : (k + 1) * tokens], k) for k in range(1, half)]
    d_came = together(*d_came)
    second.start()
    first.start()
    d_input = d_resid + d_part[:tokens].astype(full)
    for value in d_came:
        d_input = d_input + value.astype(full)
    d_input = d_input.astype(low)
    (d_input,) = together(d_input)
    for _ in last[:-1]:
        second.step()
    second.start()
    pieces = [p for share, size in zip(first.parts, first_sizes) for p in cut(share, size)]
    outer = Chain([pieces[0], pieces[2]], [JoinStep([main[0], side[0]])])
    inner = Chain([pieces[1], pieces[3]], [JoinStep([main[0], side[0]])])
    outer.start()
    d_input_came = [far.swap(d_input[width : width + width // 2])]
    outer.came, inner.parts, d_input_came = (
        lambda v: (v[:2], v[2:4], v[4:])
    )(together(*outer.came, *inner.parts, *d_input_came))
    outer.finish()
    second.start()
    inner.start()
    outer_came = [near.send(part, k) for k in range(1, half) for part in outer.parts]
    placed = spread_outer(*outer.parts, at, ()) if half == 2 else outer.parts
    count = 2 + len(outer_came)
    values = together(*inner.came, *outer_came, d_input, *placed)
    inner.came, outer_came, d_input = values[:2], values[2:count], values[count]
    outer.parts = values[count + 1 :]
    inner.finish()
    second.start()
    inner_came = [near.send(part, k) for k in range(1, half) for part in inner.parts]
    d_input_came.append(far.swap(d_input[width + width // 2 :]))
    if half == 2:
        outer.parts = list(spread_outer(*outer_came, 1 - at, outer.parts))
    count = len(inner_came)
    values = together(*inner_came, *d_input_came, *outer.parts)
    inner_came, d_input_came, outer.parts = (
        values[:count],
        values[count : count + 2],
        values[count + 2 :],
    )
    second.start()
    d_input = from_rows(d_input[:width], jnp.concatenate(d_input_came, 0))
    small = out_grad.shape[0], packed.shape[0], inner_grad.shape[0] - inner_main
    out_grad, packed, inner_b = cut(inner.parts[1], small)
    packed = [packed] + [cut(p, small)[1] for p in inner_came[1::2]]
    packed = by_device(packed).reshape(-1, D).astype(full)
    if half == 2:
        (outer_grad,) = outer.parts
        placed = spread_inner(*inner.parts, at, ())
        inner_grad, out_grad = spread_inner(*inner_came, 1 - at, placed)
    else:
        outer_grad = [jnp.concatenate(p, 0) for p in [outer.parts] + by_two(outer_came)]
        outer_grad = by_device(outer_grad).reshape(-1, D).astype(full)
        inner_grad = [jnp.concatenate([inner.parts[0], inner_b], 0)]
        out_grad = [out_grad]
        for first_part, other in by_two(inner_came):
            inner_grad.append(jnp.concatenate([first_part, cut(other, small)[2]], 0))
            out_grad.append(cut(other, small)[0])
        inner_grad = by_device(inner_grad).reshape(-1, D, D).astype(full)
        inner_grad = inner_grad.transpose(1, 0, 2).reshape(D, -1)
        out_grad = by_device(out_grad).reshape(-1, D).astype(full)
    d_input, inner_grad, out_grad, outer_grad, packed = together(
        d_input, inner_grad, out_grad, outer_grad, packed
    )
    heads_parts = second.parts[0]
    if half == 2:
        heads_came = near.send(heads_parts, 1)
        query_grad, key_grad, value_grad = spread_columns(
            heads_came, 1 - at, spread_columns(heads_parts, at, ())
        )
        biases = [p[D].astype(full) for p in (heads_parts, heads_came)]
        biases = jnp.where(at == 0, jnp.stack(biases), jnp.stack(biases[::-1]))
        query_bias_grad = biases[:, :cols].reshape(-1)
        value_bias_grad = biases[:, 2 * cols :].reshape(-1)
    else:
        heads_parts = by_device([heads_parts] + [near.send(heads_parts, k) for k in range(1, half)])
        query_grad, key_grad, value_grad = (
            jnp.concatenate([p[:, i * cols : (i + 1) * cols] for p in heads_parts], 1).astype(full)
            for i in range(3)
        )
        query_bias_grad, value_bias_grad = query_grad[D], value_grad[D]
        query_grad, key_grad, value_grad = query_grad[:D], key_grad[:D], value_grad[:D]
    return (
        result,
        d_input,
        query_grad,
        query_bias_grad,
        key_grad,
        value_grad,
        value_bias_grad,
        out_grad,
        packed[0],
        packed[1],
        packed[2],
        inner_grad,
        packed[6:10].reshape(-1),
        outer_grad,
        packed[3],
        packed[4],
        packed[5],
    )


def solution(mesh):
    tokens = P("rows", "seq", None)
    in_specs = (tokens,) + (P(),) * 15 + (P("rows"), P("rows", None, None), tokens)
    out_specs = (tokens, tokens) + (P(),) * 15
    return jax.shard_map(
        partial(per_device, mesh.shape["seq"], mesh.shape["rows"]),
        mesh=mesh,
        in_specs=in_specs,
        out_specs=out_specs,
        check_vma=False,
    )
```

```python
import functools
from functools import partial

import jax
import jax.numpy as jnp
from jax import lax
from jax.experimental import pallas as pl
from jax.experimental.pallas import tpu as pltpu
from jax.sharding import PartitionSpec as P

D = 768
HEADS = 12
HEAD = 64
BLOCK = 64
SETS = 8
CHIPS_Z = 4

EPSILON = 1e-05
NEG_FILL = -1e30

SHORT = pl.CostEstimate(flops=1 << 20, bytes_accessed=1 << 10, transcendentals=0)

NT = (((1,), (1,)), ((), ()))
NN = (((1,), (0,)), ((), ()))
TN = (((0,), (0,)), ((), ()))


def dot(left, right, dims):
    return lax.dot_general(left, right, dims, preferred_element_type=jnp.float32)


def head_groups(heads):
    groups, at = [], 0
    while at < heads:
        n = 2 if heads - at >= 2 else 1
        groups.append((at, n))
        at += n
    return groups


def lanes_of(at, n):
    return slice(at * HEAD, (at + n) * HEAD)


def diagonal(n, rows):
    row = lax.broadcasted_iota(jnp.int32, (n * rows, n * HEAD), 0) // rows
    lane = lax.broadcasted_iota(jnp.int32, (n * rows, n * HEAD), 1) // HEAD
    return (row == lane).astype(jnp.float32)


def spread_heads(block, diag, n):
    if n == 1:
        return block
    return jnp.concatenate([block] * n, 0) * diag.astype(block.dtype)


def fold_heads(full, diag, n):
    if n == 1:
        return full
    rows = full.shape[0] // n
    kept = full * diag
    out = kept[:rows]
    for h in range(1, n):
        out = out + kept[h * rows : (h + 1) * rows]
    return out


def rows_of(slot):
    return pl.ds(pl.multiple_of(slot * BLOCK, BLOCK), BLOCK)


def gather_rows(ref, slots, lanes):
    return jnp.concatenate([ref[rows_of(s), lanes] for s in slots], 0)


def as_row(column):
    n = column.shape[0]
    same = lax.broadcasted_iota(jnp.int32, (n, n), 0) == lax.broadcasted_iota(jnp.int32, (n, n), 1)
    return jnp.sum(jnp.where(same, column, 0.0), 0, keepdims=True)


def attend_kernel(
    heads,
    nb,
    abreast,
    key_at_ref,
    query_at_ref,
    q_ref,
    k_ref,
    v_ref,
    task_bias_ref,
    lead_bias_ref,
    o_ref,
    lse_ref,
):
    groups = head_groups(heads)
    scale = jnp.bfloat16(HEAD**-0.5)
    diags = {n: diagonal(n, BLOCK) for _, n in groups}

    def local(i, carry):
        work, scores, probs = [], [], []
        for u in range(abreast):
            t = abreast * i + u
            ks = [key_at_ref[t, b] for b in range(SETS)]
            work += [(t, ks, query_at_ref[t], lanes_of(at, n), n) for at, n in groups]
        for t, ks, qs, lanes, n in work:
            query = spread_heads(q_ref[rows_of(qs), lanes] * scale, diags[n], n)
            score = dot(query, gather_rows(k_ref, ks, lanes), NT)
            scores.append(score + task_bias_ref[pl.ds(t, 1), :])
        for score in scores:
            top = jnp.max(score, 1, keepdims=True)
            prob = jnp.exp(score - top)
            probs.append((prob.astype(jnp.bfloat16), top, jnp.sum(prob, 1, keepdims=True)))
        for (t, ks, qs, lanes, n), (prob, top, total) in zip(work, probs):
            out = dot(prob, gather_rows(v_ref, ks, lanes), NN) * (1.0 / total)
            out = fold_heads(out, diags[n], n)
            o_ref[rows_of(qs), lanes] = out.astype(jnp.bfloat16)
            lse_ref[qs, :, lanes] = as_row(top + jnp.log(total))
        return carry

    lax.fori_loop(0, (nb - 2) // abreast, local, 0)

    rows = 2 * BLOCK
    qs = query_at_ref[nb - 2]
    lead_rows = pl.ds(pl.multiple_of(qs * BLOCK, BLOCK), rows)
    scores, probs = [], []
    for at, n in groups:
        lanes = lanes_of(at, n)
        query = spread_heads(q_ref[lead_rows, lanes] * scale, diagonal(n, rows), n)
        scores.append(dot(query, k_ref[:, lanes], NT) + lead_bias_ref[...])
    for score in scores:
        top = jnp.max(score, 1, keepdims=True)
        prob = jnp.exp(score - top)
        probs.append((prob.astype(jnp.bfloat16), top, jnp.sum(prob, 1, keepdims=True)))
    for (at, n), (prob, top, total) in zip(groups, probs):
        lanes = lanes_of(at, n)
        out = dot(prob, v_ref[:, lanes], NN) * (1.0 / total)
        o_ref[lead_rows, lanes] = fold_heads(out, diagonal(n, rows), n).astype(jnp.bfloat16)
        lse = top + jnp.log(total)
        each = [as_row(lse[h * rows : (h + 1) * rows]) for h in range(n)]
        for b in range(2):
            part = slice(b * BLOCK, (b + 1) * BLOCK)
            lse_ref[qs + b, :, lanes] = jnp.concatenate([row[:, part] for row in each], 1)


def attend_back_kernel(
    heads,
    nb,
    abreast,
    pieces,
    key_at_ref,
    bias_at_ref,
    query_at_ref,
    places_ref,
    q_ref,
    k_ref,
    v_ref,
    o_ref,
    lse_ref,
    *rest,
):
    dq_ref, dk_ref, dv_ref, dk_acc, dv_acc, delta_ref, g_ref, bias_ref = rest[-8:]
    rows = nb * BLOCK // pieces
    for i in range(pieces):
        g_ref[i * rows : (i + 1) * rows, :] = rest[i][...]
    groups = head_groups(heads)
    diags = {n: diagonal(n, BLOCK) for _, n in groups}
    inside = lax.broadcasted_iota(jnp.int32, (BLOCK, 2 * HEAD), 0)
    for s in range(nb):
        valid = places_ref[s] * BLOCK + inside < places_ref[nb]
        bias_ref[s * BLOCK : (s + 1) * BLOCK, :] = jnp.where(valid, 0.0, NEG_FILL)
    every = nb * BLOCK
    bias_ref[every:, :] = jnp.full_like(bias_ref[every:, :], NEG_FILL)
    dk_acc[every:, :] = jnp.zeros_like(dk_acc[every:, :])
    dv_acc[every:, :] = jnp.zeros_like(dv_acc[every:, :])
    scale = HEAD**-0.5

    for at, n in groups:
        lanes = lanes_of(at, n)
        row = lax.broadcasted_iota(jnp.int32, (16, n * HEAD), 0)
        pick = row == lax.broadcasted_iota(jnp.int32, (16, n * HEAD), 1) // HEAD
        pick = pick.astype(jnp.float32).astype(jnp.bfloat16)
        for s in range(0, nb, 4):
            some = slice(s * BLOCK, (s + 4) * BLOCK)
            both = g_ref[some, lanes].astype(jnp.float32) * o_ref[some, lanes].astype(jnp.float32)
            high = both.astype(jnp.bfloat16)
            less = (both - high.astype(jnp.float32)).astype(jnp.bfloat16)
            delta = dot(pick, high, NT) + dot(pick, less, NT)
            for j in range(4):
                part = slice(j * BLOCK, (j + 1) * BLOCK)
                delta_ref[s + j, :, lanes] = jnp.concatenate(
                    [delta[h : h + 1, part] for h in range(n)], 1
                )

    both_rows = 2 * BLOCK
    lead = query_at_ref[nb - 2]
    lead_rows = pl.ds(pl.multiple_of(lead * BLOCK, BLOCK), both_rows)

    def lead_row(ref, lanes, n):
        first, second = ref[lead, :, lanes], ref[lead + 1, :, lanes]
        heads_of = [slice(h * HEAD, (h + 1) * HEAD) for h in range(n)]
        return jnp.concatenate([r[:, h] for h in heads_of for r in (first, second)], 1)

    for at, n in groups:
        lanes, diag = lanes_of(at, n), diagonal(n, both_rows)
        query = spread_heads(q_ref[lead_rows, lanes] * jnp.bfloat16(scale), diag, n)
        grad = spread_heads(g_ref[lead_rows, lanes], diag, n)
        score = dot(k_ref[:, lanes], query, NT)
        bias = jnp.concatenate([bias_ref[:every, :]] * n, 1)
        prob = jnp.exp(score + bias - lead_row(lse_ref, lanes, n))
        d_prob = dot(v_ref[:, lanes], grad, NT)
        d_score = (prob * (d_prob - lead_row(delta_ref, lanes, n))).astype(jnp.bfloat16)
        dv_acc[:every, lanes] = dot(prob.astype(jnp.bfloat16), grad, NN)
        dk_acc[:every, lanes] = dot(d_score, query, NN)
        d_query = fold_heads(dot(d_score, k_ref[:, lanes], TN), diag, n) * scale
        dq_ref[lead_rows, lanes] = d_query.astype(jnp.bfloat16)

    def several(i, carry):
        work, scores, probs, grads = [], [], [], []
        for u in range(abreast):
            t = abreast * i + u
            ks = [key_at_ref[t, b] for b in range(SETS)]
            bs = [bias_at_ref[t, b] for b in range(SETS)]
            work += [(ks, bs, query_at_ref[t], lanes_of(at, n), n) for at, n in groups]
        for ks, bs, qs, lanes, n in work:
            diag = diags[n]
            query = spread_heads(q_ref[rows_of(qs), lanes] * jnp.bfloat16(scale), diag, n)
            grad = spread_heads(g_ref[rows_of(qs), lanes], diag, n)
            keys = gather_rows(k_ref, ks, lanes)
            score = dot(keys, query, NT)
            d_prob = dot(gather_rows(v_ref, ks, lanes), grad, NT)
            scores.append((query, grad, keys, score, d_prob))
        for (ks, bs, qs, lanes, n), (query, grad, keys, score, d_prob) in zip(work, scores):
            bias = gather_rows(bias_ref, bs, slice(None))[:, : n * HEAD]
            prob = jnp.exp(score + bias - lse_ref[qs, :, lanes])
            d_score = (prob * (d_prob - delta_ref[qs, :, lanes])).astype(jnp.bfloat16)
            probs.append((prob.astype(jnp.bfloat16), d_score))
        for (query, grad, keys, _, _), (prob, d_score) in zip(scores, probs):
            grads.append((dot(prob, grad, NN), dot(d_score, query, NN), dot(d_score, keys, TN)))
        for (ks, bs, qs, lanes, n), (d_value, d_key, d_query) in zip(work, grads):
            before = [(dk_acc[rows_of(a), lanes], dv_acc[rows_of(a), lanes]) for a in bs]
            for j, a in enumerate(bs):
                part = slice(j * BLOCK, (j + 1) * BLOCK)
                dk_acc[rows_of(a), lanes] = before[j][0] + d_key[part]
                dv_acc[rows_of(a), lanes] = before[j][1] + d_value[part]
            d_query = fold_heads(d_query, diags[n], n) * scale
            dq_ref[rows_of(qs), lanes] = d_query.astype(jnp.bfloat16)
        return carry

    lax.fori_loop(0, (nb - 2) // abreast, several, 0)
    dk_ref[...] = dk_acc[: nb * BLOCK].astype(jnp.bfloat16)
    dv_ref[...] = dv_acc[: nb * BLOCK].astype(jnp.bfloat16)


VMEM = pl.BlockSpec(memory_space=pltpu.VMEM)
SMEM = pl.BlockSpec(memory_space=pltpu.SMEM)


def columns(array, at, width):
    if array.shape[1] == width or width % 128 == 0:
        return array, pl.BlockSpec((array.shape[0], width), lambda i: (0, at))
    array = array[:, at * width : (at + 1) * width]
    return array, pl.BlockSpec(array.shape, lambda i: (0, 0))


def attend(qkv, tables, heads, nb):
    key_at, _, query_at, _, task_bias, lead_bias = tables
    width = heads * HEAD
    operands, specs = zip(*[columns(qkv, i, width) for i in range(3)])
    return pl.pallas_call(
        partial(attend_kernel, heads, nb, 2),
        grid=(1,),
        out_shape=(
            jax.ShapeDtypeStruct((nb * BLOCK, width), jnp.bfloat16),
            jax.ShapeDtypeStruct((nb, 1, width), jnp.float32),
        ),
        in_specs=[SMEM] * 2 + list(specs) + [VMEM] * 2,
        out_specs=(VMEM, VMEM),
        compiler_params=pltpu.CompilerParams(vmem_limit_bytes=30 << 20),
        cost_estimate=pl.CostEstimate(
            flops=20_000_000_000, bytes_accessed=8 << 20, transcendentals=0
        ),
        name="attend",
    )(key_at, query_at, *operands, task_bias, lead_bias)


def attend_back(qkv, grads, context, lse, tables, heads, nb, held, at):
    key_at, bias_at, query_at, places, _, _ = tables
    total = context.shape[1]
    width = heads * HEAD
    parts = total // width
    operands, specs = zip(
        *[columns(qkv, i * parts + at, width) for i in range(3)], columns(context, at, width)
    )
    pieces, piece_specs = zip(*[columns(g, at, width) for g in grads])
    lse_spec = pl.BlockSpec((nb, 1, width), lambda i: (0, 0, at))
    out = jax.ShapeDtypeStruct((nb * BLOCK, total), jnp.bfloat16)
    out_spec = pl.BlockSpec((nb * BLOCK, width), lambda i: (0, at))
    count = 4 + len(operands) + 1 + len(pieces)
    abreast = 5 if (nb - 2) % 5 == 0 else 2
    return pl.pallas_call(
        partial(attend_back_kernel, heads, nb, abreast, len(pieces)),
        grid=(1,),
        out_shape=(out, out, out),
        in_specs=[SMEM] * 4
        + list(specs)
        + [lse_spec]
        + list(piece_specs)
        + [pl.BlockSpec(memory_space=pl.ANY)] * len(held),
        out_specs=(out_spec,) * 3,
        input_output_aliases={count + i: i for i in range(len(held))},
        scratch_shapes=[
            pltpu.VMEM(((nb + 1) * BLOCK, width), jnp.float32),
            pltpu.VMEM(((nb + 1) * BLOCK, width), jnp.float32),
            pltpu.VMEM((nb, 1, width), jnp.float32),
            pltpu.VMEM((nb * BLOCK, width), jnp.bfloat16),
            pltpu.VMEM(((nb + 1) * BLOCK, 2 * HEAD), jnp.float32),
        ],
        compiler_params=pltpu.CompilerParams(vmem_limit_bytes=52 << 20),
        cost_estimate=pl.CostEstimate(
            flops=15_000_000_000, bytes_accessed=6 << 20, transcendentals=0
        ),
        name="attend_back",
    )(key_at, bias_at, query_at, places, *operands, lse, *pieces, *held)


def block_tables(block_of_slot, doc, random_blocks):
    nb = random_blocks.shape[0]
    every = jnp.arange(nb, dtype=jnp.int32)
    slot_of_block = jnp.sum(
        jnp.where(block_of_slot[None, :] == every[:, None], every[None, :], 0), 1
    )
    ids = every[2:]
    before, after = ids - 1, ids + 1
    always_on = ids >= 0
    index = jnp.concatenate(
        [jnp.stack([ids * 0, ids * 0 + 1, before, ids, after], -1), random_blocks[2:]], -1
    )
    allowed = jnp.stack(
        [always_on, always_on, before >= 2, always_on, after < nb] + [always_on] * 3, -1
    )
    index = jnp.clip(index, 0, nb - 1)
    slots = jnp.sum(jnp.where(index[..., None] == block_of_slot, every, 0), -1)
    key_at = slots
    bias_at = jnp.where(allowed, slots, nb)
    query_at = jnp.concatenate([slot_of_block[2:], slot_of_block[:2]])
    inside = jnp.arange(BLOCK, dtype=jnp.int32)
    bias = jnp.where(block_of_slot[:, None] * BLOCK + inside < doc, 0.0, NEG_FILL)
    bias = bias.astype(jnp.float32)
    lead_bias = bias.reshape(1, -1)
    task_bias = (index[..., None] * BLOCK + inside < doc) & allowed[..., None]
    task_bias = jnp.where(task_bias, 0.0, NEG_FILL).astype(jnp.float32).reshape(nb - 2, -1)
    places = jnp.concatenate([block_of_slot, jnp.reshape(doc, (1,))])
    return key_at, bias_at, query_at, places, task_bias, lead_bias


TANH_SCALE = 0.7978845608028654
TANH_CUBE = 0.044715


def norm_rows(value):
    center = value - jnp.mean(value, -1, keepdims=True)
    scale = lax.rsqrt(jnp.mean(center * center, -1, keepdims=True) + EPSILON)
    return center * scale, scale


def norm_back(grad, normal, scale):
    return scale * (
        grad
        - jnp.mean(grad, -1, keepdims=True)
        - normal * jnp.mean(grad * normal, -1, keepdims=True)
    )


def feed_forward_kernel(
    chunk,
    few,
    pieces,
    mine_ref,
    x_ref,
    cot_own_ref,
    cot_came_ref,
    wo_ref,
    w1_hbm_ref,
    w2_hbm_ref,
    vec_ref,
    b1_ref,
    *refs,
):
    context_refs, refs = refs[:pieces], refs[pieces:]
    result_refs, refs = refs[:3], refs[3:]
    first_ref, active_out_ref, d_inner_out_ref, d_outer_ref, d_attended_ref = refs[:5]
    d_resid_ref, sums_ref, inner_sum_ref = refs[5:8]
    d_context_refs, refs = refs[8 : 8 + pieces], refs[8 + pieces :]
    w1_ref, w2_ref, active_ref, d_inner_ref, *refs = refs
    slope_ref, held_ref, normal_ref, scale_ref, result_ref, sems = refs
    cols = D // pieces
    first_step = pl.program_id(0) == 0
    tile = active_ref.shape[0]
    tokens_at = pl.ds(pl.multiple_of(pl.program_id(0) * tile, tile), tile)
    load_w1 = pltpu.make_async_copy(w1_hbm_ref, w1_ref, sems.at[0])
    load_w2 = pltpu.make_async_copy(w2_hbm_ref, w2_ref, sems.at[1])
    store_active = pltpu.make_async_copy(active_ref, active_out_ref.at[tokens_at, :], sems.at[2])
    store_d_inner = pltpu.make_async_copy(d_inner_ref, d_inner_out_ref.at[tokens_at, :], sems.at[3])
    low, full = jnp.bfloat16, jnp.float32
    tokens, hidden = active_ref.shape

    @pl.when(first_step)
    def _():
        load_w1.start()
        load_w2.start()
        sums_ref[...] = jnp.zeros_like(sums_ref)
        inner_sum_ref[...] = jnp.zeros_like(inner_sum_ref)

    bo, g1, s1, b2, g2, s2 = [vec_ref[i : i + 1, :] for i in range(6)]

    chunks = [slice(i, i + few) for i in range(0, tokens, few)]

    col_chunks = [slice(i, i + chunk) for i in range(0, hidden, chunk)]

    def add_sum(row, values):
        sums_ref[row : row + 1, :] += jnp.sum(values, 0, keepdims=True)

    def add_context(rows):
        parts = [
            dot(ref[rows, :], wo_ref[k * cols : (k + 1) * cols, :], NN)
            for k, ref in enumerate(context_refs)
        ]
        return sum(parts[1:], parts[0])

    for rows, attended in [(rows, add_context(rows)) for rows in chunks]:
        normal, scale = norm_rows(x_ref[rows, :].astype(full) + attended + bo)
        first = normal * g1 + s1
        normal_ref[rows, :] = normal
        scale_ref[rows, :] = jnp.broadcast_to(scale, (few, 128))
        held_ref[rows, :] = first
        first_ref[rows, :] = first.astype(low)

    @pl.when(first_step)
    def _():
        load_w1.wait()

    for cols_at, product in [(c, dot(first_ref[...], w1_ref[:, c], NN)) for c in col_chunks]:
        u = product + b1_ref[:1, cols_at]
        square = u * u
        tanh = jnp.tanh(u * (TANH_SCALE + (TANH_SCALE * TANH_CUBE) * square))
        share = 0.5 * tanh + 0.5
        active_ref[:, cols_at] = (u * share).astype(low)
        slope_ref[:, cols_at] = share + (0.5 * u) * (1.0 - tanh * tanh) * (
            TANH_SCALE + (3 * TANH_SCALE * TANH_CUBE) * square
        )

    store_active.start()

    @pl.when(first_step)
    def _():
        load_w2.wait()

    for rows, outer in [(rows, dot(active_ref[rows, :], w2_ref[...], NN)) for rows in chunks]:
        normal, scale = norm_rows(held_ref[rows, :] + outer + b2)
        result_ref[rows, :] = (normal * g2 + s2).astype(low)
        own = pl.program_id(0) == 0
        cot = jnp.where(own, cot_own_ref[0, rows, :], cot_came_ref[rows, :]).astype(full)
        d_second = norm_back(cot * g2, normal, scale)
        held_ref[rows, :] = d_second
        d_outer = d_second.astype(low)
        d_outer_ref[rows, :] = d_outer
        add_sum(3, d_outer.astype(full))
        add_sum(4, cot * normal)
        add_sum(5, cot)

    @pl.when(first_step)
    def _():
        result_refs[0][...] = result_ref[...]

    @pl.when(jnp.logical_not(first_step))
    def _():
        result_refs[1][...] = result_ref[: tile // 2, :]
        result_refs[2][...] = result_ref[tile // 2 :, :]

    for cols_at, product in [
        (c, dot(d_outer_ref[...], w2_ref[c, :], NT)) for c in col_chunks
    ]:
        d_inner = (product * slope_ref[:, cols_at]).astype(low)
        d_inner_ref[:, cols_at] = d_inner
        inner_sum_ref[:1, cols_at] += jnp.sum(d_inner.astype(full), 0, keepdims=True)

    store_d_inner.start()
    for rows, back in [(rows, dot(d_inner_ref[rows, :], w1_ref[...], NT)) for rows in chunks]:
        d_first = held_ref[rows, :] + back
        normal = normal_ref[rows, :]
        add_sum(1, d_first * normal)
        add_sum(2, d_first)
        d_resid = norm_back(d_first * g1, normal, scale_ref[rows, :1])
        d_resid_ref[rows, :] = d_resid
        d_attended = d_resid.astype(low)
        d_attended_ref[rows, :] = d_attended
        add_sum(0, d_attended.astype(full))
    for rows in chunks:
        for k, ref in enumerate(d_context_refs):
            part = dot(d_attended_ref[rows, :], wo_ref[k * cols : (k + 1) * cols, :], NT)
            ref[rows, :] = part.astype(low)
    store_active.wait()
    store_d_inner.wait()


def feed_forward(mine, x, cot, cot_came, context, wo, w1, w2, vec, b1):
    low, full = jnp.bfloat16, jnp.float32
    tile, hidden = cot_came.shape[0], w1.shape[1]
    tokens, cols = 2 * tile, context[0].shape[1]
    row = pl.BlockSpec((tile, D), lambda i, at: (i, 0))
    part = pl.BlockSpec((tile, cols), lambda i, at: (i, 0))
    there = pl.BlockSpec(memory_space=pl.ANY)
    shards = (tile, tile // 2, tile // 2)
    once = pl.Buffered(1)
    whole = lambda a: pl.BlockSpec(a.shape, lambda i, at: (0,) * a.ndim, pipeline_mode=once)
    shape = jax.ShapeDtypeStruct
    return pl.pallas_call(
        partial(feed_forward_kernel, 1024, 256, len(context)),
        grid_spec=pltpu.PrefetchScalarGridSpec(
            num_scalar_prefetch=1,
            grid=(tokens // tile,),
            in_specs=[
                row,
                pl.BlockSpec((1, tile, D), lambda i, at: (at[0], 0, 0), pipeline_mode=once),
            ]
            + [whole(cot_came), whole(wo), there, there, whole(vec), whole(b1)]
            + [part] * len(context),
            out_specs=[pl.BlockSpec((n, D), lambda i, at: (0, 0)) for n in shards]
            + [row, there, there, row, row, row]
            + [pl.BlockSpec((8, n), lambda i, at: (0, 0)) for n in (D, hidden)]
            + [part] * len(context),
            scratch_shapes=[
                pltpu.VMEM(w1.shape, low),
                pltpu.VMEM(w2.shape, low),
                pltpu.VMEM((tile, hidden), low),
                pltpu.VMEM((tile, hidden), low),
                pltpu.VMEM((tile, hidden), full),
                pltpu.VMEM((tile, D), full),
                pltpu.VMEM((tile, D), full),
                pltpu.VMEM((tile, 128), full),
                pltpu.VMEM((tile, D), low),
                pltpu.SemaphoreType.DMA((4,)),
            ],
        ),
        out_shape=[shape((n, D), low) for n in shards]
        + [
            shape((tokens, D), low),
            shape((tokens, hidden), low),
            shape((tokens, hidden), low),
            shape((tokens, D), low),
            shape((tokens, D), low),
            shape((tokens, D), full),
            shape((8, D), full),
            shape((8, hidden), full),
        ]
        + [shape((tokens, cols), low)] * len(context),
        compiler_params=pltpu.CompilerParams(vmem_limit_bytes=58 << 20),
        cost_estimate=pl.CostEstimate(
            flops=50_000_000_000, bytes_accessed=40 << 20, transcendentals=0
        ),
        name="feed_forward",
    )(jnp.reshape(mine, (1,)).astype(jnp.int32), x, cot, cot_came, wo, w1, w2, vec, b1, *context)


def wide_kernel(at_ref, left_ref, right_ref, *refs):
    *came_refs, out_ref, turned_ref = refs
    i = pl.program_id(0)

    @pl.when(i == 0)
    def _():
        turned_ref[...] = left_ref[...].T

    rows = out_ref.shape[0]
    some = pl.ds(pl.multiple_of(lax.rem(i, D // rows) * rows, rows), rows)
    out_ref[...] = add_came(dot(turned_ref[some, :], right_ref[...], NN), came_refs)


def add_came(total, came_refs):
    for ref in came_refs:
        total = total + ref[...].astype(jnp.float32)
    return total.astype(jnp.bfloat16)


def tall_kernel(at_ref, left_ref, right_ref, *refs):
    *came_refs, out_ref = refs
    out_ref[...] = add_came(dot(left_ref[...], right_ref[...], TN), came_refs)


def tall_product(left, right, half, count, tile, came=()):
    tokens, width = right.shape[0], left.shape[1]
    part = width // count
    per = part // tile
    return pl.pallas_call(
        tall_kernel,
        grid_spec=pltpu.PrefetchScalarGridSpec(
            num_scalar_prefetch=1,
            grid=(per,),
            in_specs=[
                pl.BlockSpec((tokens, tile), lambda i, at: (0, at[0] * per + i)),
                pl.BlockSpec((tokens, right.shape[1]), lambda i, at: (0, 0)),
            ]
            + [pl.BlockSpec((tile, right.shape[1]), lambda i, at: (i, 0))] * len(came),
            out_specs=pl.BlockSpec((tile, right.shape[1]), lambda i, at: (i, 0)),
        ),
        out_shape=jax.ShapeDtypeStruct((part, right.shape[1]), jnp.bfloat16),
        compiler_params=pltpu.CompilerParams(vmem_limit_bytes=48 << 20),
        cost_estimate=pl.CostEstimate(
            flops=2 * tokens * part * right.shape[1], bytes_accessed=8 << 20, transcendentals=0
        ),
        name="tall_product",
    )(jnp.reshape(half, (1,)).astype(jnp.int32), left, right, *came)


def wide_product(left, right, half, count, rows, came=()):
    tokens, width = right.shape
    part = width // count
    blocks, per = part // D, D // rows
    return pl.pallas_call(
        wide_kernel,
        grid_spec=pltpu.PrefetchScalarGridSpec(
            num_scalar_prefetch=1,
            grid=(blocks * per,),
            in_specs=[
                pl.BlockSpec((tokens, D), lambda i, at: (0, 0)),
                pl.BlockSpec((tokens, D), lambda i, at: (0, at[0] * blocks + i // per)),
            ]
            + [pl.BlockSpec((rows, D), lambda i, at: (i, 0))] * len(came),
            out_specs=pl.BlockSpec((rows, D), lambda i, at: (i, 0)),
            scratch_shapes=[pltpu.VMEM((D, tokens), jnp.bfloat16)],
        ),
        out_shape=jax.ShapeDtypeStruct((part, D), jnp.bfloat16),
        compiler_params=pltpu.CompilerParams(vmem_limit_bytes=48 << 20),
        cost_estimate=pl.CostEstimate(
            flops=2 * tokens * part * D, bytes_accessed=8 << 20, transcendentals=0
        ),
        name="wide_product",
    )(jnp.reshape(half, (1,)).astype(jnp.int32), left, right, *came)


def heads_kernel(x_ref, d_query_ref, d_key_ref, d_value_ref, out_ref, turned_ref):
    tokens, rows = x_ref.shape[0], turned_ref.shape[0]

    @pl.when(pl.program_id(0) == 0)
    def _():
        turned_ref[:D, :] = x_ref[...].T
        row = lax.broadcasted_iota(jnp.int32, (rows - D, tokens), 0)
        turned_ref[D:, :] = (row == 0).astype(jnp.float32).astype(jnp.bfloat16)

    for i, ref in enumerate((d_query_ref, d_key_ref, d_value_ref)):

        @pl.when(pl.program_id(0) == i)
        def _():
            out_ref[...] = dot(turned_ref[...], ref[...], NN).astype(jnp.bfloat16)


def heads_products(x, d_query, d_key, d_value):
    tokens, cols = d_query.shape
    rows = D + 32
    each = pl.BlockSpec((tokens, cols), lambda i: (0, 0))
    return pl.pallas_call(
        heads_kernel,
        grid=(3,),
        in_specs=[pl.BlockSpec((tokens, D), lambda i: (0, 0)), each, each, each],
        out_specs=pl.BlockSpec((rows, cols), lambda i: (0, i)),
        out_shape=jax.ShapeDtypeStruct((rows, 3 * cols), jnp.bfloat16),
        scratch_shapes=[pltpu.VMEM((rows, tokens), jnp.bfloat16)],
        compiler_params=pltpu.CompilerParams(vmem_limit_bytes=62 << 20),
        cost_estimate=pl.CostEstimate(
            flops=6 * tokens * rows * cols, bytes_accessed=8 << 20, transcendentals=0
        ),
        name="heads_products",
    )(x, d_query, d_key, d_value)


def inputs_kernel(at_ref, d_query_ref, d_key_ref, d_value_ref, wq_ref, wk_ref, wv_ref, *out_refs):
    total = dot(d_query_ref[...], wq_ref[...], NT)
    total = total + dot(d_key_ref[...], wk_ref[...], NT)
    total = (total + dot(d_value_ref[...], wv_ref[...], NT)).astype(jnp.bfloat16)
    per = pl.num_programs(0) // len(out_refs)
    for k, ref in enumerate(out_refs):

        @pl.when(pl.program_id(0) // per == k)
        def _():
            ref[...] = total


def inputs_products(grads, weights, at, count):
    tokens, cols = grads[0].shape
    tile = 512
    per = tokens // count // tile
    part = pl.BlockSpec((tile, cols), lambda i, at: (i, 0))
    weight = pl.BlockSpec((D, cols), lambda i, at: (0, at[0]), pipeline_mode=pl.Buffered(1))

    def place(k):
        return pl.BlockSpec((tile, D), lambda i, at: (jnp.clip(i - k * per, 0, per - 1), 0))

    return pl.pallas_call(
        inputs_kernel,
        grid_spec=pltpu.PrefetchScalarGridSpec(
            num_scalar_prefetch=1,
            grid=(count * per,),
            in_specs=[part] * 3 + [weight] * 3,
            out_specs=[place(k) for k in range(count)],
        ),
        out_shape=[jax.ShapeDtypeStruct((tokens // count, D), jnp.bfloat16)] * count,
        compiler_params=pltpu.CompilerParams(vmem_limit_bytes=60 << 20),
        cost_estimate=pl.CostEstimate(
            flops=24_000_000_000, bytes_accessed=8 << 20, transcendentals=0
        ),
        name="inputs_products",
    )(jnp.reshape(at, (1,)).astype(jnp.int32), *grads, *weights)


def spread_heads_kernel(at_ref, pool_ref, *refs):
    for i, ref in enumerate(refs[-3:]):

        @pl.when(pl.program_id(0) == i)
        def _():
            ref[...] = pool_ref[...].astype(jnp.float32)


def spread_columns(pool, half, held):
    cols = pool.shape[1] // 3
    shape = jax.ShapeDtypeStruct((D, D), jnp.float32)
    return pl.pallas_call(
        spread_heads_kernel,
        grid_spec=pltpu.PrefetchScalarGridSpec(
            num_scalar_prefetch=1,
            grid=(3,),
            in_specs=[pl.BlockSpec((D, cols), lambda i, at: (0, i))]
            + [pl.BlockSpec(memory_space=pl.ANY)] * len(held),
            out_specs=[pl.BlockSpec((D, cols), lambda i, at: (0, at[0]))] * 3,
        ),
        out_shape=[shape] * 3,
        input_output_aliases={2 + i: i for i in range(len(held))},
        compiler_params=pltpu.CompilerParams(vmem_limit_bytes=32 << 20),
        cost_estimate=SHORT,
        name="spread_columns",
    )(jnp.reshape(half, (1,)).astype(jnp.int32), pool, *held)


def spread_outer_kernel(at_ref, first_ref, second_ref, *refs):
    i, blocks = pl.program_id(0), pl.num_programs(0)

    @pl.when(i < blocks - 1)
    def _():
        refs[-1][...] = first_ref[...].astype(jnp.float32)

    @pl.when(i == blocks - 1)
    def _():
        refs[-1][...] = second_ref[...].astype(jnp.float32)


def spread_inner_kernel(at_ref, first_ref, second_ref, third_ref, *refs):
    inner_ref, out_ref = refs[-2:]
    i, blocks = pl.program_id(0), pl.num_programs(0) - 1

    @pl.when(i < blocks - 1)
    def _():
        inner_ref[...] = first_ref[...].astype(jnp.float32)

    @pl.when(i == blocks - 1)
    def _():
        inner_ref[...] = second_ref[...].astype(jnp.float32)

    @pl.when(i == blocks)
    def _():
        out_ref[...] = third_ref[...].astype(jnp.float32)


def spread_call(kernel, name, half, grid, operands, specs, out_shapes, out_specs, held):
    return pl.pallas_call(
        kernel,
        grid_spec=pltpu.PrefetchScalarGridSpec(
            num_scalar_prefetch=1,
            grid=grid,
            in_specs=specs + [pl.BlockSpec(memory_space=pl.ANY)] * len(held),
            out_specs=out_specs,
        ),
        out_shape=[jax.ShapeDtypeStruct(s, jnp.float32) for s in out_shapes],
        input_output_aliases={1 + len(operands) + i: i for i in range(len(held))},
        compiler_params=pltpu.CompilerParams(vmem_limit_bytes=32 << 20),
        cost_estimate=SHORT,
        name=name,
    )(jnp.reshape(half, (1,)).astype(jnp.int32), *operands, *held)


def spread_outer(first, second, half, held):
    rows = second.shape[0]
    blocks = first.shape[0] // rows + 1
    return spread_call(
        spread_outer_kernel,
        "spread_outer",
        half,
        (blocks,),
        (first, second),
        [
            pl.BlockSpec((rows, D), lambda i, at: (jnp.minimum(i, blocks - 2), 0)),
            pl.BlockSpec((rows, D), lambda i, at: (0, 0)),
        ],
        [(2 * rows * blocks, D)],
        [pl.BlockSpec((rows, D), lambda i, at: (at[0] * blocks + i, 0))],
        held,
    )


def spread_inner(first, mixed, half, held):
    rows = 256
    per = D // rows
    blocks = first.shape[0] // rows + 1
    wide = blocks // per
    out_rows = D // 2

    def inner_at(i, at):
        j = jnp.minimum(i, blocks - 1)
        return (j % per, at[0] * wide + j // per)

    return spread_call(
        spread_inner_kernel,
        "spread_inner",
        half,
        (blocks + 1,),
        (first, mixed, mixed),
        [
            pl.BlockSpec((rows, D), lambda i, at: (jnp.minimum(i, blocks - 2), 0)),
            pl.BlockSpec((rows, D), lambda i, at: (mixed.shape[0] // rows - 1, 0)),
            pl.BlockSpec((out_rows, D), lambda i, at: (0, 0)),
        ],
        [(D, 2 * wide * D), (D, D)],
        [
            pl.BlockSpec((rows, D), inner_at),
            pl.BlockSpec((out_rows, D), lambda i, at: (at[0], 0)),
        ],
        held,
    )


class Ring:
    def __init__(self, axis, size, at, perm):
        self.axis, self.size, self.at, self.perm = axis, size, at, perm

    def send(self, value, by):
        return lax.ppermute(value, self.axis, self.perm(by))


class Pairs:
    def __init__(self, seq, rows, masks, core):
        me = lax.axis_index("seq") * rows + lax.axis_index("rows")
        bits = [lax.rem(me // mask, 2) for mask in masks]
        self.bit = jnp.where(lax.rem(me // core, 2) == 0, bits[0], bits[1])
        self.perm = [(i, i ^ masks[i // core % 2]) for i in range(seq * rows)]

    def swap(self, value):
        return lax.ppermute(value, ("seq", "rows"), self.perm)

    def keep(self, value):
        part = value.shape[0] // 2
        return lax.dynamic_slice_in_dim(value, self.bit * part, part, 0)

    def give(self, value):
        part = value.shape[0] // 2
        return lax.dynamic_slice_in_dim(value, (1 - self.bit) * part, part, 0)

    def halved(self, value, came):
        return (self.keep(value).astype(jnp.float32) + came.astype(jnp.float32)).astype(value.dtype)

    def halve(self, value):
        return self.halved(value, self.swap(self.give(value)))

    def joined(self, value, came):
        first = jnp.where(self.bit == 0, value, came)
        second = jnp.where(self.bit == 0, came, value)
        return jnp.concatenate([first, second], 0)

    def join(self, value):
        return self.joined(value, self.swap(value))


def powers(step, count):
    masks = []
    while count > 1:
        masks.append(step)
        step, count = step * 2, count // 2
    return masks


def make_links(seq, rows):
    half = seq // 2
    deep = CHIPS_Z if rows % CHIPS_Z == 0 else 1
    wide = rows // deep
    s = lax.axis_index("seq")
    near = Ring(
        "seq",
        half,
        lax.rem(s, half),
        lambda by: [(i, i // half * half + (i + by) % half) for i in range(seq)],
    )

    def pairs(first, second=None):
        return Pairs(seq, rows, (first, second or first), rows)

    far_mask = half * rows
    y, z = powers(1, wide), powers(wide, deep)
    far = pairs(far_mask)
    inside = [pairs(mask) for mask in powers(rows, half)]
    main = [pairs(far_mask, y[0]), pairs(y[0], z[0]), pairs(z[0], far_mask)]
    side = [pairs(z[0]), pairs(far_mask), pairs(y[0])]
    last = [pairs(mask) for mask in y[1:] + z[1:]]
    return near, far, inside, [main, side], last


def in_step(values):
    return list(lax.optimization_barrier(tuple(values)))


def cut(value, sizes):
    out, at = [], 0
    for size in sizes:
        out.append(value[at : at + size])
        at += size
    return out


class HalveStep:
    def __init__(self, pairs):
        self.pairs = pairs

    def start(self, parts):
        return [pair.swap(pair.give(part)) for pair, part in zip(self.pairs, parts)]

    def finish(self, parts, came):
        return [pair.halved(*both) for pair, *both in zip(self.pairs, parts, came)]


class JoinStep:
    def __init__(self, pairs):
        self.pairs = pairs

    def start(self, parts):
        return [pair.swap(part) for pair, part in zip(self.pairs, parts)]

    def finish(self, parts, came):
        return [pair.joined(*both) for pair, *both in zip(self.pairs, parts, came)]


class SumStep:
    def __init__(self, pair):
        self.pair = pair

    def start(self, parts):
        return cut(self.pair.swap(jnp.concatenate(parts, 0)), [p.shape[0] for p in parts])

    def finish(self, parts, came):
        return [
            (p.astype(jnp.float32) + c.astype(jnp.float32)).astype(p.dtype)
            for p, c in zip(parts, came)
        ]


class Chain:
    def __init__(self, parts, steps):
        self.parts, self.steps, self.came = list(parts), list(steps), None

    def start(self):
        self.came = self.steps[0].start(self.parts)

    def finish(self, *after):
        came = in_step(list(self.came) + list(after))[: len(self.came)]
        self.parts = self.steps.pop(0).finish(self.parts, came)
        self.came = None

    def step(self, *after):
        if self.came is None:
            self.start()
        self.finish(*after)
        if self.steps:
            self.start()


def column_sum(values):
    return jnp.sum(values.astype(jnp.float32), 0)


def per_device(
    seq,
    rows,
    inputs,
    query_weight,
    query_bias,
    key_weight,
    value_weight,
    value_bias,
    output_weight,
    output_bias,
    first_gain,
    first_shift,
    inner_weight,
    inner_bias,
    outer_weight,
    outer_bias,
    second_gain,
    second_shift,
    doc_tokens,
    random_blocks,
    cotangent,
):
    low, full = jnp.bfloat16, jnp.float32
    near, far, inside, routes, last = make_links(seq, rows)
    main, side = routes
    half = seq // 2
    width = inputs.shape[1]
    tokens = 2 * width
    nb = random_blocks.shape[1]
    heads = HEADS // half
    cols = heads * HEAD
    mine, at = far.bit, near.at

    def own_and_other(array):
        own = lax.dynamic_index_in_dim(array, mine, 0, False)
        return own, lax.dynamic_index_in_dim(array, 1 - mine, 0, False)

    def from_rows(own, other):
        return jnp.where(mine == 0, jnp.stack([own, other]), jnp.stack([other, own]))

    def by_device(values):
        stacked = jnp.stack(values)
        order = lax.rem(at + half - jnp.arange(half), half)
        return jnp.take(stacked, order, axis=0) if half > 2 else jnp.where(at == 0, stacked, stacked[::-1])

    def by_two(values):
        return [values[i : i + 2] for i in range(0, len(values), 2)]

    x_own, x_other = own_and_other(inputs)
    x_came = far.swap(x_other)

    shards = []
    for k in range(half):
        own = mine * half + lax.rem(at + k, half)
        shards += [own, lax.rem(own + half, seq)]
    per_shard = width // BLOCK
    block_of_slot = (
        jnp.stack(shards)[:, None] * per_shard + jnp.arange(per_shard, dtype=jnp.int32)
    ).reshape(-1).astype(jnp.int32)
    doc = lax.dynamic_index_in_dim(doc_tokens, mine, 0, False)
    chosen = lax.dynamic_index_in_dim(random_blocks, mine, 0, False)
    tables = block_tables(block_of_slot, doc, chosen)

    def my_cols(weight):
        return lax.dynamic_slice_in_dim(weight, at * cols, cols, weight.ndim - 1)

    weights = (query_weight, key_weight, value_weight)
    w_qkv = jnp.concatenate([my_cols(w) for w in weights], 1)
    b_qkv = jnp.concatenate(
        [my_cols(query_bias), jnp.zeros((cols,), low), my_cols(value_bias)]
    ).astype(full)
    wo = jnp.concatenate(
        [
            lax.dynamic_slice_in_dim(
                output_weight, lax.rem(at + half - k, half) * cols, cols, 0
            )
            for k in range(half)
        ],
        0,
    )
    vec = jnp.stack(
        [output_bias, first_gain, first_shift, outer_bias, second_gain, second_shift]
    ).astype(full)
    vec = jnp.pad(vec, ((0, 2), (0, 0)))
    b1 = jnp.broadcast_to(inner_bias.astype(full), (8, inner_bias.shape[0]))

    x_came, w_qkv, b_qkv, wo, vec, b1, *tables = in_step(
        [x_came, w_qkv, b_qkv, wo, vec, b1, *tables]
    )
    x_parts = [x_own, x_came]
    for k in range(1, half):
        x_parts += [near.send(x_own, half - k), near.send(x_came, half - k)]
    x_all, cotangent = in_step([jnp.concatenate(x_parts, 0), cotangent])
    cot_came = far.swap(lax.dynamic_index_in_dim(cotangent, 1 - mine, 0, False))
    qkv = (dot(x_all, w_qkv, NN) + b_qkv).astype(low)
    qkv, cotangent = in_step([qkv, cotangent])
    heads_context, lse = attend(qkv, tables, heads, nb)
    heads_context, lse, cot_came = in_step([heads_context, lse, cot_came])
    context = [heads_context] + [
        near.send(heads_context[k * tokens : (k + 1) * tokens], k) for k in range(1, half)
    ]
    values = feed_forward(
        mine, x_all, cotangent, cot_came, context, wo, inner_weight, outer_weight, vec, b1
    )
    result, result_half, values = values[0], list(values[1:3]), values[3:]
    first_low, active, d_inner, d_outer, d_attended, d_resid, sums, inner_sum, *d_context = values
    heads_grad = [d_context[0]] + [near.send(d_context[k], half - k) for k in range(1, half)]

    packed = jnp.concatenate([sums[:6].reshape(-1), inner_sum[0]]).reshape(-1, D)
    packed = jnp.pad(packed, ((0, 256 - packed.shape[0]), (0, 0))).astype(low)

    def outer_product(part, k, came=()):
        return tall_product(active, d_outer, part, half, 768, came)

    def inner_product(part, k, came=()):
        return wide_product(first_low, d_inner, part, half, 768, came)

    def out_product(part, k, came=()):
        k = (half - k) % half
        if cols % 128:
            total = dot(context[k][:tokens], d_attended, TN)
            return sum([c.astype(full) for c in came], total).astype(low)
        return tall_product(context[k], d_attended, 0, 1, cols, came)

    def packed_part(part, k, came=()):
        size = 256 // half
        total = lax.dynamic_slice_in_dim(packed, part * size, size, 0).astype(full)
        return sum([c.astype(full) for c in came], total).astype(low)

    def give(product):
        return [product(lax.rem(at + k, half), k) for k in range(1, half)]

    def send(parts):
        return [near.send(part, k) for k, part in enumerate(parts, 1)]

    outer_give = give(outer_product)
    outer_give[0], first_low, d_attended = in_step([outer_give[0], first_low, d_attended])
    outer_came = send(outer_give)
    inner_came = send(give(inner_product))
    out_came = send(give(out_product))
    packed_came = send(give(packed_part))
    outer_grad = outer_product(at, 0, outer_came)
    outer_main = outer_grad.shape[0] * 3 // 4
    early = Chain([outer_grad[:outer_main], outer_grad[outer_main:]], [HalveStep([main[0], side[0]])])
    early.start()
    inner_came[0], out_came[0], packed_came[0], *early.parts = in_step(
        [inner_came[0], out_came[0], packed_came[0]] + early.parts
    )
    inner_grad = inner_product(at, 0, inner_came)
    out_grad = out_product(at, 0, out_came)
    packed = packed_part(at, 0, packed_came)
    inner_grad, out_grad, packed, *early.came = in_step(
        [inner_grad, out_grad, packed] + early.came
    )
    early.finish()
    inner_main = inner_grad.shape[0] * 5 // 6
    mixed = jnp.concatenate([out_grad, packed, inner_grad[inner_main:]], 0)
    rest = Chain([inner_grad[:inner_main], mixed], [HalveStep([main[0], side[0]])])
    heads_grad[0], *rest.parts = in_step([heads_grad[0]] + early.parts + rest.parts)
    early.parts, rest.parts = rest.parts[:2], rest.parts[2:]

    first_sizes = [
        (outer_main // 2, inner_main // 2),
        ((outer_grad.shape[0] - outer_main) // 2, mixed.shape[0] // 2),
    ]
    first = Chain([], [HalveStep([main[i], side[i]]) for i in (1, 2)])
    first.steps += [SumStep(pair) for pair in last]
    first.steps += [JoinStep([main[i], side[i]]) for i in (2, 1)]

    steps = cols // 128 if cols % 128 == 0 else 1
    d_qkv = ()
    result_came = []
    for k in range(steps):
        chain = first if first.parts else rest
        chain.start()
        if k == 2:
            result_half[0], d_query = in_step([result_half[0], d_qkv[0]])
            d_qkv = (d_query,) + d_qkv[1:]
            result_came.append(far.swap(result_half[0]))
        d_qkv = attend_back(
            qkv, heads_grad, heads_context, lse, tables, heads // steps, nb, d_qkv, k
        )
        d_query, d_key, d_value, *came = in_step(list(d_qkv) + chain.came + result_came)
        d_qkv = (d_query, d_key, d_value)
        chain.came, result_came = came[: len(chain.came)], came[len(chain.came) :]
        chain.finish()
        if chain is rest:
            first.parts = [
                jnp.concatenate([e, r], 0) for e, r in zip(early.parts, rest.parts)
            ]
        d_query, *first.parts = in_step([d_query] + first.parts)
        d_qkv = (d_query, d_key, d_value)

    while len(first.steps) > 3:
        first.start()
        first.finish()
    sums_at_last = first.steps.pop(0)
    last_came = sums_at_last.start(first.parts[1:])
    result_half[1:], d_query = in_step([*result_half[1:], d_query])[:-1], d_query
    result_came += [far.swap(piece) for piece in result_half[len(result_came) :]]
    if cols % 128 == 0:
        heads_part = heads_products(x_all, *d_qkv)
    else:
        sums_of = [jnp.pad(column_sum(d)[None, :], ((0, 31), (0, 0))) for d in d_qkv]
        heads_part = [
            jnp.concatenate([dot(x_all, d, TN), total], 0) for d, total in zip(d_qkv, sums_of)
        ]
        heads_part = jnp.concatenate(heads_part, 1).astype(low)
    heads_part, d_query, d_key, d_value, *came = in_step(
        [heads_part, d_query, d_key, d_value] + last_came + result_came
    )
    last_came, result_came = came[:1], came[1:]
    first.parts[0], heads_part = in_step([first.parts[0], heads_part])

    second = Chain([heads_part], [HalveStep([main[i]]) for i in range(3)])
    second.steps += [SumStep(pair) for pair in last]
    second.steps += [JoinStep([main[i]]) for i in (2, 1, 0)]
    second.start()
    last_came = sums_at_last.start(first.parts[:1]) + last_came
    if cols % 128 == 0:
        d_parts = list(inputs_products((d_query, d_key, d_value), weights, at, half))
    else:
        parts = zip((d_query, d_key, d_value), (my_cols(w) for w in weights))
        d_parts = sum(dot(d, w, NT) for d, w in parts).astype(low)
        d_parts = cut(d_parts, [tokens] * half)
    d_parts[0], *came = in_step([d_parts[0]] + last_came + second.came)
    first.parts, second.came = sums_at_last.finish(first.parts, came[:2]), came[2:]
    second.finish()

    def together(*beside):
        count = len(first.came or ())
        values = in_step(list(first.came or ()) + second.came + list(beside))
        if count:
            first.came = values[:count]
            first.finish()
        second.came = values[count : count + len(second.came)]
        second.finish()
        return values[len(values) - len(beside) :]

    second.start()
    first.start()
    d_came = [near.send(d_parts[k], k) for k in range(1, half)]
    d_came = together(*d_came)
    second.start()
    first.start()
    d_input = d_resid + d_parts[0].astype(full)
    for value in d_came:
        d_input = d_input + value.astype(full)
    d_input = d_input.astype(low)
    result = from_rows(result, jnp.concatenate(result_came, 0))
    d_input, result = together(d_input, result)
    for _ in last[:-1]:
        second.step()
    second.start()
    pieces = [p for share, size in zip(first.parts, first_sizes) for p in cut(share, size)]
    outer = Chain([pieces[0], pieces[2]], [JoinStep([main[0], side[0]])])
    inner = Chain([pieces[1], pieces[3]], [JoinStep([main[0], side[0]])])
    outer.start()
    d_input_came = [far.swap(d_input[width : width + width // 2])]
    values = together(*outer.came, *inner.parts, *d_input_came)
    outer.came, inner.parts, d_input_came = values[:2], values[2:4], values[4:]
    outer.finish()
    second.start()
    inner.start()
    outer_came = [near.send(part, k) for k in range(1, half) for part in outer.parts]
    placed = spread_outer(*outer.parts, at, ()) if half == 2 else outer.parts
    count = 2 + len(outer_came)
    values = together(*inner.came, *outer_came, d_input, *placed)
    inner.came, outer_came, d_input = values[:2], values[2:count], values[count]
    outer.parts = values[count + 1 :]
    inner.finish()
    second.start()
    inner_came = [near.send(part, k) for k in range(1, half) for part in inner.parts]
    d_input_came.append(far.swap(d_input[width + width // 2 :]))
    if half == 2:
        outer.parts = list(spread_outer(*outer_came, 1 - at, outer.parts))
    count = len(inner_came)
    values = together(*inner_came, *d_input_came, *outer.parts)
    inner_came, d_input_came, outer.parts = (
        values[:count],
        values[count : count + 2],
        values[count + 2 :],
    )
    second.start()
    d_input = from_rows(d_input[:width], jnp.concatenate(d_input_came, 0))
    small = out_grad.shape[0], packed.shape[0], inner_grad.shape[0] - inner_main
    out_grad, packed, inner_b = cut(inner.parts[1], small)
    packed = [packed] + [cut(p, small)[1] for p in inner_came[1::2]]
    packed = by_device(packed).reshape(-1, D).astype(full)
    if half == 2:
        (outer_grad,) = outer.parts
        placed = spread_inner(*inner.parts, at, ())
        inner_grad, out_grad = spread_inner(*inner_came, 1 - at, placed)
    else:
        outer_grad = [jnp.concatenate(p, 0) for p in [outer.parts] + by_two(outer_came)]
        outer_grad = by_device(outer_grad).reshape(-1, D).astype(full)
        inner_grad = [jnp.concatenate([inner.parts[0], inner_b], 0)]
        out_grad = [out_grad]
        for first_part, other in by_two(inner_came):
            inner_grad.append(jnp.concatenate([first_part, cut(other, small)[2]], 0))
            out_grad.append(cut(other, small)[0])
        inner_grad = by_device(inner_grad).reshape(-1, D, D).astype(full)
        inner_grad = inner_grad.transpose(1, 0, 2).reshape(D, -1)
        out_grad = by_device(out_grad).reshape(-1, D).astype(full)
    d_input, inner_grad, out_grad, outer_grad, packed = together(
        d_input, inner_grad, out_grad, outer_grad, packed
    )
    heads_parts = second.parts[0]
    if half == 2:
        heads_came = near.send(heads_parts, 1)
        query_grad, key_grad, value_grad = spread_columns(
            heads_came, 1 - at, spread_columns(heads_parts, at, ())
        )
        biases = [p[D].astype(full) for p in (heads_parts, heads_came)]
        biases = jnp.where(at == 0, jnp.stack(biases), jnp.stack(biases[::-1]))
        query_bias_grad = biases[:, :cols].reshape(-1)
        value_bias_grad = biases[:, 2 * cols :].reshape(-1)
    else:
        heads_parts = by_device([heads_parts] + [near.send(heads_parts, k) for k in range(1, half)])
        query_grad, key_grad, value_grad = (
            jnp.concatenate([p[:, i * cols : (i + 1) * cols] for p in heads_parts], 1).astype(full)
            for i in range(3)
        )
        query_bias_grad, value_bias_grad = query_grad[D], value_grad[D]
        query_grad, key_grad, value_grad = query_grad[:D], key_grad[:D], value_grad[:D]
    return (
        result,
        d_input,
        query_grad,
        query_bias_grad,
        key_grad,
        value_grad,
        value_bias_grad,
        out_grad,
        packed[0],
        packed[1],
        packed[2],
        inner_grad,
        packed[6:10].reshape(-1),
        outer_grad,
        packed[3],
        packed[4],
        packed[5],
    )


def solution(mesh):
    tokens = P("rows", "seq", None)
    in_specs = (tokens,) + (P(),) * 15 + (P("rows"), P("rows", None, None), tokens)
    out_specs = (tokens, tokens) + (P(),) * 15
    return jax.shard_map(
        partial(per_device, mesh.shape["seq"], mesh.shape["rows"]),
        mesh=mesh,
        in_specs=in_specs,
        out_specs=out_specs,
        check_vma=False,
    )
```

```python
import functools
from functools import partial

import jax
import jax.numpy as jnp
from jax import lax
from jax.experimental import pallas as pl
from jax.experimental.pallas import tpu as pltpu
from jax.sharding import PartitionSpec as P

D = 768
HEADS = 12
HEAD = 64
BLOCK = 64
SETS = 8
CHIPS_Z = 4

EPSILON = 1e-05
NEG_FILL = -1e30

SHORT = pl.CostEstimate(flops=1 << 20, bytes_accessed=1 << 10, transcendentals=0)

NT = (((1,), (1,)), ((), ()))
NN = (((1,), (0,)), ((), ()))
TN = (((0,), (0,)), ((), ()))


def dot(left, right, dims):
    return lax.dot_general(left, right, dims, preferred_element_type=jnp.float32)


def head_groups(heads):
    groups, at = [], 0
    while at < heads:
        n = 2 if heads - at >= 2 else 1
        groups.append((at, n))
        at += n
    return groups


def lanes_of(at, n):
    return slice(at * HEAD, (at + n) * HEAD)


def diagonal(n, rows):
    row = lax.broadcasted_iota(jnp.int32, (n * rows, n * HEAD), 0) // rows
    lane = lax.broadcasted_iota(jnp.int32, (n * rows, n * HEAD), 1) // HEAD
    return (row == lane).astype(jnp.float32)


def spread_heads(block, diag, n):
    if n == 1:
        return block
    return jnp.concatenate([block] * n, 0) * diag.astype(block.dtype)


def fold_heads(full, diag, n):
    if n == 1:
        return full
    rows = full.shape[0] // n
    kept = full * diag
    out = kept[:rows]
    for h in range(1, n):
        out = out + kept[h * rows : (h + 1) * rows]
    return out


def rows_of(slot):
    return pl.ds(pl.multiple_of(slot * BLOCK, BLOCK), BLOCK)


def gather_rows(ref, slots, lanes):
    return jnp.concatenate([ref[rows_of(s), lanes] for s in slots], 0)


def as_row(column):
    n = column.shape[0]
    same = lax.broadcasted_iota(jnp.int32, (n, n), 0) == lax.broadcasted_iota(jnp.int32, (n, n), 1)
    return jnp.sum(jnp.where(same, column, 0.0), 0, keepdims=True)


def attend_kernel(
    heads,
    nb,
    abreast,
    key_at_ref,
    query_at_ref,
    q_ref,
    k_ref,
    v_ref,
    task_bias_ref,
    lead_bias_ref,
    o_ref,
    lse_ref,
):
    groups = head_groups(heads)
    scale = jnp.bfloat16(HEAD**-0.5)
    diags = {n: diagonal(n, BLOCK) for _, n in groups}

    def local(i, carry):
        work, scores, probs = [], [], []
        for u in range(abreast):
            t = abreast * i + u
            ks = [key_at_ref[t, b] for b in range(SETS)]
            work += [(t, ks, query_at_ref[t], lanes_of(at, n), n) for at, n in groups]
        for t, ks, qs, lanes, n in work:
            query = spread_heads(q_ref[rows_of(qs), lanes] * scale, diags[n], n)
            score = dot(query, gather_rows(k_ref, ks, lanes), NT)
            scores.append(score + task_bias_ref[pl.ds(t, 1), :])
        for score in scores:
            top = jnp.max(score, 1, keepdims=True)
            prob = jnp.exp(score - top)
            probs.append((prob.astype(jnp.bfloat16), top, jnp.sum(prob, 1, keepdims=True)))
        for (t, ks, qs, lanes, n), (prob, top, total) in zip(work, probs):
            out = dot(prob, gather_rows(v_ref, ks, lanes), NN) * (1.0 / total)
            out = fold_heads(out, diags[n], n)
            o_ref[rows_of(qs), lanes] = out.astype(jnp.bfloat16)
            lse_ref[qs, :, lanes] = as_row(top + jnp.log(total))
        return carry

    lax.fori_loop(0, (nb - 2) // abreast, local, 0)

    rows = 2 * BLOCK
    qs = query_at_ref[nb - 2]
    lead_rows = pl.ds(pl.multiple_of(qs * BLOCK, BLOCK), rows)
    scores, probs = [], []
    for at, n in groups:
        lanes = lanes_of(at, n)
        query = spread_heads(q_ref[lead_rows, lanes] * scale, diagonal(n, rows), n)
        scores.append(dot(query, k_ref[:, lanes], NT) + lead_bias_ref[...])
    for score in scores:
        top = jnp.max(score, 1, keepdims=True)
        prob = jnp.exp(score - top)
        probs.append((prob.astype(jnp.bfloat16), top, jnp.sum(prob, 1, keepdims=True)))
    for (at, n), (prob, top, total) in zip(groups, probs):
        lanes = lanes_of(at, n)
        out = dot(prob, v_ref[:, lanes], NN) * (1.0 / total)
        o_ref[lead_rows, lanes] = fold_heads(out, diagonal(n, rows), n).astype(jnp.bfloat16)
        lse = top + jnp.log(total)
        each = [as_row(lse[h * rows : (h + 1) * rows]) for h in range(n)]
        for b in range(2):
            part = slice(b * BLOCK, (b + 1) * BLOCK)
            lse_ref[qs + b, :, lanes] = jnp.concatenate([row[:, part] for row in each], 1)


def attend_back_kernel(
    heads,
    nb,
    abreast,
    pieces,
    key_at_ref,
    bias_at_ref,
    query_at_ref,
    places_ref,
    q_ref,
    k_ref,
    v_ref,
    o_ref,
    lse_ref,
    *rest,
):
    dq_ref, dk_ref, dv_ref, dk_acc, dv_acc, delta_ref, g_ref, bias_ref = rest[-8:]
    rows = nb * BLOCK // pieces
    for i in range(pieces):
        g_ref[i * rows : (i + 1) * rows, :] = rest[i][...]
    groups = head_groups(heads)
    diags = {n: diagonal(n, BLOCK) for _, n in groups}
    inside = lax.broadcasted_iota(jnp.int32, (BLOCK, 2 * HEAD), 0)
    for s in range(nb):
        valid = places_ref[s] * BLOCK + inside < places_ref[nb]
        bias_ref[s * BLOCK : (s + 1) * BLOCK, :] = jnp.where(valid, 0.0, NEG_FILL)
    every = nb * BLOCK
    bias_ref[every:, :] = jnp.full_like(bias_ref[every:, :], NEG_FILL)
    dk_acc[every:, :] = jnp.zeros_like(dk_acc[every:, :])
    dv_acc[every:, :] = jnp.zeros_like(dv_acc[every:, :])
    scale = HEAD**-0.5

    for at, n in groups:
        lanes = lanes_of(at, n)
        row = lax.broadcasted_iota(jnp.int32, (16, n * HEAD), 0)
        pick = row == lax.broadcasted_iota(jnp.int32, (16, n * HEAD), 1) // HEAD
        pick = pick.astype(jnp.float32).astype(jnp.bfloat16)
        for s in range(0, nb, 4):
            some = slice(s * BLOCK, (s + 4) * BLOCK)
            both = g_ref[some, lanes].astype(jnp.float32) * o_ref[some, lanes].astype(jnp.float32)
            high = both.astype(jnp.bfloat16)
            less = (both - high.astype(jnp.float32)).astype(jnp.bfloat16)
            delta = dot(pick, high, NT) + dot(pick, less, NT)
            for j in range(4):
                part = slice(j * BLOCK, (j + 1) * BLOCK)
                delta_ref[s + j, :, lanes] = jnp.concatenate(
                    [delta[h : h + 1, part] for h in range(n)], 1
                )

    both_rows = 2 * BLOCK
    lead = query_at_ref[nb - 2]
    lead_rows = pl.ds(pl.multiple_of(lead * BLOCK, BLOCK), both_rows)

    def lead_row(ref, lanes, n):
        first, second = ref[lead, :, lanes], ref[lead + 1, :, lanes]
        heads_of = [slice(h * HEAD, (h + 1) * HEAD) for h in range(n)]
        return jnp.concatenate([r[:, h] for h in heads_of for r in (first, second)], 1)

    for at, n in groups:
        lanes, diag = lanes_of(at, n), diagonal(n, both_rows)
        query = spread_heads(q_ref[lead_rows, lanes] * jnp.bfloat16(scale), diag, n)
        grad = spread_heads(g_ref[lead_rows, lanes], diag, n)
        score = dot(k_ref[:, lanes], query, NT)
        bias = jnp.concatenate([bias_ref[:every, :]] * n, 1)
        prob = jnp.exp(score + bias - lead_row(lse_ref, lanes, n))
        d_prob = dot(v_ref[:, lanes], grad, NT)
        d_score = (prob * (d_prob - lead_row(delta_ref, lanes, n))).astype(jnp.bfloat16)
        dv_acc[:every, lanes] = dot(prob.astype(jnp.bfloat16), grad, NN)
        dk_acc[:every, lanes] = dot(d_score, query, NN)
        d_query = fold_heads(dot(d_score, k_ref[:, lanes], TN), diag, n) * scale
        dq_ref[lead_rows, lanes] = d_query.astype(jnp.bfloat16)

    def several(i, carry):
        work, scores, probs, grads = [], [], [], []
        for u in range(abreast):
            t = abreast * i + u
            ks = [key_at_ref[t, b] for b in range(SETS)]
            bs = [bias_at_ref[t, b] for b in range(SETS)]
            work += [(ks, bs, query_at_ref[t], lanes_of(at, n), n) for at, n in groups]
        for ks, bs, qs, lanes, n in work:
            diag = diags[n]
            query = spread_heads(q_ref[rows_of(qs), lanes] * jnp.bfloat16(scale), diag, n)
            grad = spread_heads(g_ref[rows_of(qs), lanes], diag, n)
            keys = gather_rows(k_ref, ks, lanes)
            score = dot(keys, query, NT)
            d_prob = dot(gather_rows(v_ref, ks, lanes), grad, NT)
            scores.append((query, grad, keys, score, d_prob))
        for (ks, bs, qs, lanes, n), (query, grad, keys, score, d_prob) in zip(work, scores):
            bias = gather_rows(bias_ref, bs, slice(None))[:, : n * HEAD]
            prob = jnp.exp(score + bias - lse_ref[qs, :, lanes])
            d_score = (prob * (d_prob - delta_ref[qs, :, lanes])).astype(jnp.bfloat16)
            probs.append((prob.astype(jnp.bfloat16), d_score))
        for (query, grad, keys, _, _), (prob, d_score) in zip(scores, probs):
            grads.append((dot(prob, grad, NN), dot(d_score, query, NN), dot(d_score, keys, TN)))
        for (ks, bs, qs, lanes, n), (d_value, d_key, d_query) in zip(work, grads):
            before = [(dk_acc[rows_of(a), lanes], dv_acc[rows_of(a), lanes]) for a in bs]
            for j, a in enumerate(bs):
                part = slice(j * BLOCK, (j + 1) * BLOCK)
                dk_acc[rows_of(a), lanes] = before[j][0] + d_key[part]
                dv_acc[rows_of(a), lanes] = before[j][1] + d_value[part]
            d_query = fold_heads(d_query, diags[n], n) * scale
            dq_ref[rows_of(qs), lanes] = d_query.astype(jnp.bfloat16)
        return carry

    lax.fori_loop(0, (nb - 2) // abreast, several, 0)
    dk_ref[...] = dk_acc[: nb * BLOCK].astype(jnp.bfloat16)
    dv_ref[...] = dv_acc[: nb * BLOCK].astype(jnp.bfloat16)


VMEM = pl.BlockSpec(memory_space=pltpu.VMEM)
SMEM = pl.BlockSpec(memory_space=pltpu.SMEM)


def columns(array, at, width):
    if array.shape[1] == width or width % 128 == 0:
        return array, pl.BlockSpec((array.shape[0], width), lambda i: (0, at))
    array = array[:, at * width : (at + 1) * width]
    return array, pl.BlockSpec(array.shape, lambda i: (0, 0))


def attend(qkv, tables, heads, nb):
    key_at, _, query_at, _, task_bias, lead_bias = tables
    width = heads * HEAD
    operands, specs = zip(*[columns(qkv, i, width) for i in range(3)])
    return pl.pallas_call(
        partial(attend_kernel, heads, nb, 2),
        grid=(1,),
        out_shape=(
            jax.ShapeDtypeStruct((nb * BLOCK, width), jnp.bfloat16),
            jax.ShapeDtypeStruct((nb, 1, width), jnp.float32),
        ),
        in_specs=[SMEM] * 2 + list(specs) + [VMEM] * 2,
        out_specs=(VMEM, VMEM),
        compiler_params=pltpu.CompilerParams(vmem_limit_bytes=30 << 20),
        cost_estimate=pl.CostEstimate(
            flops=2_000_000_000, bytes_accessed=8 << 20, transcendentals=0
        ),
        name="attend",
    )(key_at, query_at, *operands, task_bias, lead_bias)


def attend_back(qkv, grads, context, lse, tables, heads, nb, held, at):
    key_at, bias_at, query_at, places, _, _ = tables
    total = context.shape[1]
    width = heads * HEAD
    parts = total // width
    operands, specs = zip(
        *[columns(qkv, i * parts + at, width) for i in range(3)], columns(context, at, width)
    )
    pieces, piece_specs = zip(*[columns(g, at, width) for g in grads])
    lse_spec = pl.BlockSpec((nb, 1, width), lambda i: (0, 0, at))
    out = jax.ShapeDtypeStruct((nb * BLOCK, total), jnp.bfloat16)
    out_spec = pl.BlockSpec((nb * BLOCK, width), lambda i: (0, at))
    count = 4 + len(operands) + 1 + len(pieces)
    abreast = 5 if (nb - 2) % 5 == 0 else 2
    return pl.pallas_call(
        partial(attend_back_kernel, heads, nb, abreast, len(pieces)),
        grid=(1,),
        out_shape=(out, out, out),
        in_specs=[SMEM] * 4
        + list(specs)
        + [lse_spec]
        + list(piece_specs)
        + [pl.BlockSpec(memory_space=pl.ANY)] * len(held),
        out_specs=(out_spec,) * 3,
        input_output_aliases={count + i: i for i in range(len(held))},
        scratch_shapes=[
            pltpu.VMEM(((nb + 1) * BLOCK, width), jnp.float32),
            pltpu.VMEM(((nb + 1) * BLOCK, width), jnp.float32),
            pltpu.VMEM((nb, 1, width), jnp.float32),
            pltpu.VMEM((nb * BLOCK, width), jnp.bfloat16),
            pltpu.VMEM(((nb + 1) * BLOCK, 2 * HEAD), jnp.float32),
        ],
        compiler_params=pltpu.CompilerParams(vmem_limit_bytes=52 << 20),
        cost_estimate=pl.CostEstimate(
            flops=15_000_000_000, bytes_accessed=6 << 20, transcendentals=0
        ),
        name="attend_back",
    )(key_at, bias_at, query_at, places, *operands, lse, *pieces, *held)


def block_tables(block_of_slot, doc, random_blocks):
    nb = random_blocks.shape[0]
    every = jnp.arange(nb, dtype=jnp.int32)
    slot_of_block = jnp.sum(
        jnp.where(block_of_slot[None, :] == every[:, None], every[None, :], 0), 1
    )
    ids = every[2:]
    before, after = ids - 1, ids + 1
    always_on = ids >= 0
    index = jnp.concatenate(
        [jnp.stack([ids * 0, ids * 0 + 1, before, ids, after], -1), random_blocks[2:]], -1
    )
    allowed = jnp.stack(
        [always_on, always_on, before >= 2, always_on, after < nb] + [always_on] * 3, -1
    )
    index = jnp.clip(index, 0, nb - 1)
    slots = jnp.sum(jnp.where(index[..., None] == block_of_slot, every, 0), -1)
    key_at = slots
    bias_at = jnp.where(allowed, slots, nb)
    query_at = jnp.concatenate([slot_of_block[2:], slot_of_block[:2]])
    inside = jnp.arange(BLOCK, dtype=jnp.int32)
    bias = jnp.where(block_of_slot[:, None] * BLOCK + inside < doc, 0.0, NEG_FILL)
    bias = bias.astype(jnp.float32)
    lead_bias = bias.reshape(1, -1)
    task_bias = (index[..., None] * BLOCK + inside < doc) & allowed[..., None]
    task_bias = jnp.where(task_bias, 0.0, NEG_FILL).astype(jnp.float32).reshape(nb - 2, -1)
    places = jnp.concatenate([block_of_slot, jnp.reshape(doc, (1,))])
    return key_at, bias_at, query_at, places, task_bias, lead_bias


TANH_SCALE = 0.7978845608028654
TANH_CUBE = 0.044715


def norm_rows(value):
    center = value - jnp.mean(value, -1, keepdims=True)
    scale = lax.rsqrt(jnp.mean(center * center, -1, keepdims=True) + EPSILON)
    return center * scale, scale


def norm_back(grad, normal, scale):
    return scale * (
        grad
        - jnp.mean(grad, -1, keepdims=True)
        - normal * jnp.mean(grad * normal, -1, keepdims=True)
    )


def feed_forward_kernel(
    chunk,
    few,
    pieces,
    mine_ref,
    x_ref,
    cot_own_ref,
    cot_came_ref,
    wo_ref,
    w1_hbm_ref,
    w2_hbm_ref,
    vec_ref,
    b1_ref,
    *refs,
):
    context_refs, refs = refs[:pieces], refs[pieces:]
    result_refs, refs = refs[:3], refs[3:]
    first_ref, active_out_ref, d_inner_out_ref, d_outer_ref, d_attended_ref = refs[:5]
    d_resid_ref, sums_ref, inner_sum_ref = refs[5:8]
    d_context_refs, refs = refs[8 : 8 + pieces], refs[8 + pieces :]
    w1_ref, w2_ref, active_ref, d_inner_ref, *refs = refs
    slope_ref, held_ref, normal_ref, scale_ref, result_ref, sems = refs
    cols = D // pieces
    first_step = pl.program_id(0) == 0
    tile = active_ref.shape[0]
    tokens_at = pl.ds(pl.multiple_of(pl.program_id(0) * tile, tile), tile)
    load_w1 = pltpu.make_async_copy(w1_hbm_ref, w1_ref, sems.at[0])
    load_w2 = pltpu.make_async_copy(w2_hbm_ref, w2_ref, sems.at[1])
    store_active = pltpu.make_async_copy(active_ref, active_out_ref.at[tokens_at, :], sems.at[2])
    store_d_inner = pltpu.make_async_copy(d_inner_ref, d_inner_out_ref.at[tokens_at, :], sems.at[3])
    low, full = jnp.bfloat16, jnp.float32
    tokens, hidden = active_ref.shape

    @pl.when(first_step)
    def _():
        load_w1.start()
        load_w2.start()
        sums_ref[...] = jnp.zeros_like(sums_ref)
        inner_sum_ref[...] = jnp.zeros_like(inner_sum_ref)

    bo, g1, s1, b2, g2, s2 = [vec_ref[i : i + 1, :] for i in range(6)]

    chunks = [slice(i, i + few) for i in range(0, tokens, few)]

    def each_columns(body):
        def step(i, carry):
            body(pl.ds(pl.multiple_of(i * chunk, chunk), chunk))
            return carry

        lax.fori_loop(0, hidden // chunk, step, 0)

    def add_sum(row, values):
        sums_ref[row : row + 1, :] += jnp.sum(values, 0, keepdims=True)

    def add_context(rows):
        parts = [
            dot(ref[rows, :], wo_ref[k * cols : (k + 1) * cols, :], NN)
            for k, ref in enumerate(context_refs)
        ]
        return sum(parts[1:], parts[0])

    for rows, attended in [(rows, add_context(rows)) for rows in chunks]:
        normal, scale = norm_rows(x_ref[rows, :].astype(full) + attended + bo)
        first = normal * g1 + s1
        normal_ref[rows, :] = normal
        scale_ref[rows, :] = jnp.broadcast_to(scale, (few, 128))
        held_ref[rows, :] = first
        first_ref[rows, :] = first.astype(low)

    @pl.when(first_step)
    def _():
        load_w1.wait()

    @each_columns
    def _(cols):
        u = dot(first_ref[...], w1_ref[:, cols], NN) + b1_ref[:1, cols]
        square = u * u
        tanh = jnp.tanh(u * (TANH_SCALE + (TANH_SCALE * TANH_CUBE) * square))
        share = 0.5 * tanh + 0.5
        active_ref[:, cols] = (u * share).astype(low)
        slope_ref[:, cols] = share + (0.5 * u) * (1.0 - tanh * tanh) * (
            TANH_SCALE + (3 * TANH_SCALE * TANH_CUBE) * square
        )

    store_active.start()

    @pl.when(first_step)
    def _():
        load_w2.wait()

    for rows, outer in [(rows, dot(active_ref[rows, :], w2_ref[...], NN)) for rows in chunks]:
        normal, scale = norm_rows(held_ref[rows, :] + outer + b2)
        result_ref[rows, :] = (normal * g2 + s2).astype(low)
        own = pl.program_id(0) == 0
        cot = jnp.where(own, cot_own_ref[0, rows, :], cot_came_ref[rows, :]).astype(full)
        d_second = norm_back(cot * g2, normal, scale)
        held_ref[rows, :] = d_second
        d_outer = d_second.astype(low)
        d_outer_ref[rows, :] = d_outer
        add_sum(3, d_outer.astype(full))
        add_sum(4, cot * normal)
        add_sum(5, cot)

    @pl.when(first_step)
    def _():
        result_refs[0][...] = result_ref[...]

    @pl.when(jnp.logical_not(first_step))
    def _():
        result_refs[1][...] = result_ref[: tile // 2, :]
        result_refs[2][...] = result_ref[tile // 2 :, :]

    @each_columns
    def _(cols):
        d_inner = (dot(d_outer_ref[...], w2_ref[cols, :], NT) * slope_ref[:, cols]).astype(low)
        d_inner_ref[:, cols] = d_inner
        inner_sum_ref[:1, cols] += jnp.sum(d_inner.astype(full), 0, keepdims=True)

    store_d_inner.start()
    for rows, back in [(rows, dot(d_inner_ref[rows, :], w1_ref[...], NT)) for rows in chunks]:
        d_first = held_ref[rows, :] + back
        normal = normal_ref[rows, :]
        add_sum(1, d_first * normal)
        add_sum(2, d_first)
        d_resid = norm_back(d_first * g1, normal, scale_ref[rows, :1])
        d_resid_ref[rows, :] = d_resid
        d_attended = d_resid.astype(low)
        d_attended_ref[rows, :] = d_attended
        add_sum(0, d_attended.astype(full))
    for rows in chunks:
        for k, ref in enumerate(d_context_refs):
            part = dot(d_attended_ref[rows, :], wo_ref[k * cols : (k + 1) * cols, :], NT)
            ref[rows, :] = part.astype(low)
    store_active.wait()
    store_d_inner.wait()


def feed_forward(mine, x, cot, cot_came, context, wo, w1, w2, vec, b1):
    low, full = jnp.bfloat16, jnp.float32
    tile, hidden = cot_came.shape[0], w1.shape[1]
    tokens, cols = 2 * tile, context[0].shape[1]
    row = pl.BlockSpec((tile, D), lambda i, at: (i, 0))
    part = pl.BlockSpec((tile, cols), lambda i, at: (i, 0))
    there = pl.BlockSpec(memory_space=pl.ANY)
    shards = (tile, tile // 2, tile // 2)
    once = pl.Buffered(1)
    whole = lambda a: pl.BlockSpec(a.shape, lambda i, at: (0,) * a.ndim, pipeline_mode=once)
    shape = jax.ShapeDtypeStruct
    return pl.pallas_call(
        partial(feed_forward_kernel, 1024, 256, len(context)),
        grid_spec=pltpu.PrefetchScalarGridSpec(
            num_scalar_prefetch=1,
            grid=(tokens // tile,),
            in_specs=[
                row,
                pl.BlockSpec((1, tile, D), lambda i, at: (at[0], 0, 0), pipeline_mode=once),
            ]
            + [whole(cot_came), whole(wo), there, there, whole(vec), whole(b1)]
            + [part] * len(context),
            out_specs=[pl.BlockSpec((n, D), lambda i, at: (0, 0)) for n in shards]
            + [row, there, there, row, row, row]
            + [pl.BlockSpec((8, n), lambda i, at: (0, 0)) for n in (D, hidden)]
            + [part] * len(context),
            scratch_shapes=[
                pltpu.VMEM(w1.shape, low),
                pltpu.VMEM(w2.shape, low),
                pltpu.VMEM((tile, hidden), low),
                pltpu.VMEM((tile, hidden), low),
                pltpu.VMEM((tile, hidden), full),
                pltpu.VMEM((tile, D), full),
                pltpu.VMEM((tile, D), full),
                pltpu.VMEM((tile, 128), full),
                pltpu.VMEM((tile, D), low),
                pltpu.SemaphoreType.DMA((4,)),
            ],
        ),
        out_shape=[shape((n, D), low) for n in shards]
        + [
            shape((tokens, D), low),
            shape((tokens, hidden), low),
            shape((tokens, hidden), low),
            shape((tokens, D), low),
            shape((tokens, D), low),
            shape((tokens, D), full),
            shape((8, D), full),
            shape((8, hidden), full),
        ]
        + [shape((tokens, cols), low)] * len(context),
        compiler_params=pltpu.CompilerParams(vmem_limit_bytes=58 << 20),
        cost_estimate=pl.CostEstimate(
            flops=50_000_000_000, bytes_accessed=40 << 20, transcendentals=0
        ),
        name="feed_forward",
    )(jnp.reshape(mine, (1,)).astype(jnp.int32), x, cot, cot_came, wo, w1, w2, vec, b1, *context)


def wide_kernel(at_ref, left_ref, right_ref, *refs):
    *came_refs, out_ref, turned_ref = refs
    i = pl.program_id(0)

    @pl.when(i == 0)
    def _():
        turned_ref[...] = left_ref[...].T

    rows = out_ref.shape[0]
    some = pl.ds(pl.multiple_of(lax.rem(i, D // rows) * rows, rows), rows)
    out_ref[...] = add_came(dot(turned_ref[some, :], right_ref[...], NN), came_refs)


def add_came(total, came_refs):
    for ref in came_refs:
        total = total + ref[...].astype(jnp.float32)
    return total.astype(jnp.bfloat16)


def tall_kernel(at_ref, left_ref, right_ref, *refs):
    *came_refs, out_ref = refs
    out_ref[...] = add_came(dot(left_ref[...], right_ref[...], TN), came_refs)


def tall_product(left, right, half, count, tile, came=()):
    tokens, width = right.shape[0], left.shape[1]
    part = width // count
    per = part // tile
    return pl.pallas_call(
        tall_kernel,
        grid_spec=pltpu.PrefetchScalarGridSpec(
            num_scalar_prefetch=1,
            grid=(per,),
            in_specs=[
                pl.BlockSpec((tokens, tile), lambda i, at: (0, at[0] * per + i)),
                pl.BlockSpec((tokens, right.shape[1]), lambda i, at: (0, 0)),
            ]
            + [pl.BlockSpec((tile, right.shape[1]), lambda i, at: (i, 0))] * len(came),
            out_specs=pl.BlockSpec((tile, right.shape[1]), lambda i, at: (i, 0)),
        ),
        out_shape=jax.ShapeDtypeStruct((part, right.shape[1]), jnp.bfloat16),
        compiler_params=pltpu.CompilerParams(vmem_limit_bytes=48 << 20),
        cost_estimate=pl.CostEstimate(
            flops=2 * tokens * part * right.shape[1], bytes_accessed=8 << 20, transcendentals=0
        ),
        name="tall_product",
    )(jnp.reshape(half, (1,)).astype(jnp.int32), left, right, *came)


def wide_product(left, right, half, count, rows, came=()):
    tokens, width = right.shape
    part = width // count
    blocks, per = part // D, D // rows
    return pl.pallas_call(
        wide_kernel,
        grid_spec=pltpu.PrefetchScalarGridSpec(
            num_scalar_prefetch=1,
            grid=(blocks * per,),
            in_specs=[
                pl.BlockSpec((tokens, D), lambda i, at: (0, 0)),
                pl.BlockSpec((tokens, D), lambda i, at: (0, at[0] * blocks + i // per)),
            ]
            + [pl.BlockSpec((rows, D), lambda i, at: (i, 0))] * len(came),
            out_specs=pl.BlockSpec((rows, D), lambda i, at: (i, 0)),
            scratch_shapes=[pltpu.VMEM((D, tokens), jnp.bfloat16)],
        ),
        out_shape=jax.ShapeDtypeStruct((part, D), jnp.bfloat16),
        compiler_params=pltpu.CompilerParams(vmem_limit_bytes=48 << 20),
        cost_estimate=pl.CostEstimate(
            flops=2 * tokens * part * D, bytes_accessed=8 << 20, transcendentals=0
        ),
        name="wide_product",
    )(jnp.reshape(half, (1,)).astype(jnp.int32), left, right, *came)


def heads_kernel(x_ref, d_query_ref, d_key_ref, d_value_ref, out_ref, turned_ref):
    tokens, rows = x_ref.shape[0], turned_ref.shape[0]

    @pl.when(pl.program_id(0) == 0)
    def _():
        turned_ref[:D, :] = x_ref[...].T
        row = lax.broadcasted_iota(jnp.int32, (rows - D, tokens), 0)
        turned_ref[D:, :] = (row == 0).astype(jnp.float32).astype(jnp.bfloat16)

    for i, ref in enumerate((d_query_ref, d_key_ref, d_value_ref)):

        @pl.when(pl.program_id(0) == i)
        def _():
            out_ref[...] = dot(turned_ref[...], ref[...], NN).astype(jnp.bfloat16)


def heads_products(x, d_query, d_key, d_value):
    tokens, cols = d_query.shape
    rows = D + 32
    each = pl.BlockSpec((tokens, cols), lambda i: (0, 0))
    return pl.pallas_call(
        heads_kernel,
        grid=(3,),
        in_specs=[pl.BlockSpec((tokens, D), lambda i: (0, 0)), each, each, each],
        out_specs=pl.BlockSpec((rows, cols), lambda i: (0, i)),
        out_shape=jax.ShapeDtypeStruct((rows, 3 * cols), jnp.bfloat16),
        scratch_shapes=[pltpu.VMEM((rows, tokens), jnp.bfloat16)],
        compiler_params=pltpu.CompilerParams(vmem_limit_bytes=62 << 20),
        cost_estimate=pl.CostEstimate(
            flops=6 * tokens * rows * cols, bytes_accessed=8 << 20, transcendentals=0
        ),
        name="heads_products",
    )(x, d_query, d_key, d_value)


def inputs_kernel(at_ref, d_query_ref, d_key_ref, d_value_ref, wq_ref, wk_ref, wv_ref, *out_refs):
    total = dot(d_query_ref[...], wq_ref[...], NT)
    total = total + dot(d_key_ref[...], wk_ref[...], NT)
    total = (total + dot(d_value_ref[...], wv_ref[...], NT)).astype(jnp.bfloat16)
    per = pl.num_programs(0) // len(out_refs)
    for k, ref in enumerate(out_refs):

        @pl.when(pl.program_id(0) // per == k)
        def _():
            ref[...] = total


def inputs_products(grads, weights, at, count):
    tokens, cols = grads[0].shape
    tile = 512
    per = tokens // count // tile
    part = pl.BlockSpec((tile, cols), lambda i, at: (i, 0))
    weight = pl.BlockSpec((D, cols), lambda i, at: (0, at[0]), pipeline_mode=pl.Buffered(1))

    def place(k):
        return pl.BlockSpec((tile, D), lambda i, at: (jnp.clip(i - k * per, 0, per - 1), 0))

    return pl.pallas_call(
        inputs_kernel,
        grid_spec=pltpu.PrefetchScalarGridSpec(
            num_scalar_prefetch=1,
            grid=(count * per,),
            in_specs=[part] * 3 + [weight] * 3,
            out_specs=[place(k) for k in range(count)],
        ),
        out_shape=[jax.ShapeDtypeStruct((tokens // count, D), jnp.bfloat16)] * count,
        compiler_params=pltpu.CompilerParams(vmem_limit_bytes=60 << 20),
        cost_estimate=pl.CostEstimate(
            flops=24_000_000_000, bytes_accessed=8 << 20, transcendentals=0
        ),
        name="inputs_products",
    )(jnp.reshape(at, (1,)).astype(jnp.int32), *grads, *weights)


def spread_heads_kernel(at_ref, pool_ref, *refs):
    cols = refs[-1].shape[1]
    for i, ref in enumerate(refs[-3:]):
        ref[...] = pool_ref[:, i * cols : (i + 1) * cols].astype(jnp.float32)


def spread_columns(pool, half, held):
    cols = pool.shape[1] // 3
    return spread_call(
        spread_heads_kernel,
        "spread_columns",
        half,
        (1,),
        (pool,),
        [pl.BlockSpec((D, 3 * cols), lambda i, at: (0, 0))],
        [(D, D)] * 3,
        [pl.BlockSpec((D, cols), lambda i, at: (0, at[0]))] * 3,
        held,
    )


def spread_outer_kernel(at_ref, first_ref, second_ref, *refs):
    i, blocks = pl.program_id(0), pl.num_programs(0)

    @pl.when(i < blocks - 1)
    def _():
        refs[-1][...] = first_ref[...].astype(jnp.float32)

    @pl.when(i == blocks - 1)
    def _():
        refs[-1][...] = second_ref[...].astype(jnp.float32)


def spread_inner_kernel(at_ref, first_ref, second_ref, third_ref, *refs):
    inner_ref, out_ref = refs[-2:]
    i, blocks = pl.program_id(0), pl.num_programs(0) - 1

    @pl.when(i < blocks - 1)
    def _():
        inner_ref[...] = first_ref[...].astype(jnp.float32)

    @pl.when(i == blocks - 1)
    def _():
        inner_ref[...] = second_ref[...].astype(jnp.float32)

    @pl.when(i == blocks)
    def _():
        out_ref[...] = third_ref[...].astype(jnp.float32)


def spread_call(kernel, name, half, grid, operands, specs, out_shapes, out_specs, held):
    return pl.pallas_call(
        kernel,
        grid_spec=pltpu.PrefetchScalarGridSpec(
            num_scalar_prefetch=1,
            grid=grid,
            in_specs=specs + [pl.BlockSpec(memory_space=pl.ANY)] * len(held),
            out_specs=out_specs,
        ),
        out_shape=[jax.ShapeDtypeStruct(s, jnp.float32) for s in out_shapes],
        input_output_aliases={1 + len(operands) + i: i for i in range(len(held))},
        compiler_params=pltpu.CompilerParams(vmem_limit_bytes=32 << 20),
        cost_estimate=SHORT,
        name=name,
    )(jnp.reshape(half, (1,)).astype(jnp.int32), *operands, *held)


def spread_outer(first, second, half, held):
    rows = second.shape[0]
    blocks = first.shape[0] // rows + 1
    return spread_call(
        spread_outer_kernel,
        "spread_outer",
        half,
        (blocks,),
        (first, second),
        [
            pl.BlockSpec((rows, D), lambda i, at: (jnp.minimum(i, blocks - 2), 0)),
            pl.BlockSpec((rows, D), lambda i, at: (0, 0)),
        ],
        [(2 * rows * blocks, D)],
        [pl.BlockSpec((rows, D), lambda i, at: (at[0] * blocks + i, 0))],
        held,
    )


def spread_inner(first, mixed, half, held):
    rows = 256
    per = D // rows
    blocks = first.shape[0] // rows + 1
    wide = blocks // per
    out_rows = D // 2

    def inner_at(i, at):
        j = jnp.minimum(i, blocks - 1)
        return (j % per, at[0] * wide + j // per)

    return spread_call(
        spread_inner_kernel,
        "spread_inner",
        half,
        (blocks + 1,),
        (first, mixed, mixed),
        [
            pl.BlockSpec((rows, D), lambda i, at: (jnp.minimum(i, blocks - 2), 0)),
            pl.BlockSpec((rows, D), lambda i, at: (mixed.shape[0] // rows - 1, 0)),
            pl.BlockSpec((out_rows, D), lambda i, at: (0, 0)),
        ],
        [(D, 2 * wide * D), (D, D)],
        [
            pl.BlockSpec((rows, D), inner_at),
            pl.BlockSpec((out_rows, D), lambda i, at: (at[0], 0)),
        ],
        held,
    )


class Ring:
    def __init__(self, axis, size, at, perm):
        self.axis, self.size, self.at, self.perm = axis, size, at, perm

    def send(self, value, by):
        return lax.ppermute(value, self.axis, self.perm(by))


class Pairs:
    def __init__(self, seq, rows, masks, core):
        me = lax.axis_index("seq") * rows + lax.axis_index("rows")
        bits = [lax.rem(me // mask, 2) for mask in masks]
        self.bit = jnp.where(lax.rem(me // core, 2) == 0, bits[0], bits[1])
        self.perm = [(i, i ^ masks[i // core % 2]) for i in range(seq * rows)]

    def swap(self, value):
        return lax.ppermute(value, ("seq", "rows"), self.perm)

    def keep(self, value):
        part = value.shape[0] // 2
        return lax.dynamic_slice_in_dim(value, self.bit * part, part, 0)

    def give(self, value):
        part = value.shape[0] // 2
        return lax.dynamic_slice_in_dim(value, (1 - self.bit) * part, part, 0)

    def halved(self, value, came):
        return (self.keep(value).astype(jnp.float32) + came.astype(jnp.float32)).astype(value.dtype)

    def halve(self, value):
        return self.halved(value, self.swap(self.give(value)))

    def joined(self, value, came):
        first = jnp.where(self.bit == 0, value, came)
        second = jnp.where(self.bit == 0, came, value)
        return jnp.concatenate([first, second], 0)

    def join(self, value):
        return self.joined(value, self.swap(value))


def powers(step, count):
    masks = []
    while count > 1:
        masks.append(step)
        step, count = step * 2, count // 2
    return masks


def make_links(seq, rows):
    half = seq // 2
    deep = CHIPS_Z if rows % CHIPS_Z == 0 else 1
    wide = rows // deep
    s = lax.axis_index("seq")
    near = Ring(
        "seq",
        half,
        lax.rem(s, half),
        lambda by: [(i, i // half * half + (i + by) % half) for i in range(seq)],
    )

    def pairs(first, second=None):
        return Pairs(seq, rows, (first, second or first), rows)

    far_mask = half * rows
    y, z = powers(1, wide), powers(wide, deep)
    far = pairs(far_mask)
    inside = [pairs(mask) for mask in powers(rows, half)]
    main = [pairs(far_mask, y[0]), pairs(y[0], z[0]), pairs(z[0], far_mask)]
    side = [pairs(z[0]), pairs(far_mask), pairs(y[0])]
    last = [pairs(mask) for mask in y[1:] + z[1:]]
    return near, far, inside, [main, side], last


def in_step(values):
    return list(lax.optimization_barrier(tuple(values)))


def cut(value, sizes):
    out, at = [], 0
    for size in sizes:
        out.append(value[at : at + size])
        at += size
    return out


class HalveStep:
    def __init__(self, pairs):
        self.pairs = pairs

    def start(self, parts):
        return [pair.swap(pair.give(part)) for pair, part in zip(self.pairs, parts)]

    def finish(self, parts, came):
        return [pair.halved(*both) for pair, *both in zip(self.pairs, parts, came)]


class JoinStep:
    def __init__(self, pairs):
        self.pairs = pairs

    def start(self, parts):
        return [pair.swap(part) for pair, part in zip(self.pairs, parts)]

    def finish(self, parts, came):
        return [pair.joined(*both) for pair, *both in zip(self.pairs, parts, came)]


class SumStep:
    def __init__(self, pair):
        self.pair = pair

    def start(self, parts):
        return cut(self.pair.swap(jnp.concatenate(parts, 0)), [p.shape[0] for p in parts])

    def finish(self, parts, came):
        return [
            (p.astype(jnp.float32) + c.astype(jnp.float32)).astype(p.dtype)
            for p, c in zip(parts, came)
        ]


class Chain:
    def __init__(self, parts, steps):
        self.parts, self.steps, self.came = list(parts), list(steps), None

    def start(self):
        self.came = self.steps[0].start(self.parts)

    def finish(self, *after):
        came = in_step(list(self.came) + list(after))[: len(self.came)]
        self.parts = self.steps.pop(0).finish(self.parts, came)
        self.came = None

    def step(self, *after):
        if self.came is None:
            self.start()
        self.finish(*after)
        if self.steps:
            self.start()


def column_sum(values):
    return jnp.sum(values.astype(jnp.float32), 0)


def per_device(
    seq,
    rows,
    inputs,
    query_weight,
    query_bias,
    key_weight,
    value_weight,
    value_bias,
    output_weight,
    output_bias,
    first_gain,
    first_shift,
    inner_weight,
    inner_bias,
    outer_weight,
    outer_bias,
    second_gain,
    second_shift,
    doc_tokens,
    random_blocks,
    cotangent,
):
    low, full = jnp.bfloat16, jnp.float32
    near, far, inside, routes, last = make_links(seq, rows)
    main, side = routes
    half = seq // 2
    width = inputs.shape[1]
    tokens = 2 * width
    nb = random_blocks.shape[1]
    heads = HEADS // half
    cols = heads * HEAD
    mine, at = far.bit, near.at

    def own_and_other(array):
        own = lax.dynamic_index_in_dim(array, mine, 0, False)
        return own, lax.dynamic_index_in_dim(array, 1 - mine, 0, False)

    def from_rows(own, other):
        return jnp.where(mine == 0, jnp.stack([own, other]), jnp.stack([other, own]))

    def by_device(values):
        stacked = jnp.stack(values)
        order = lax.rem(at + half - jnp.arange(half), half)
        return jnp.take(stacked, order, axis=0) if half > 2 else jnp.where(at == 0, stacked, stacked[::-1])

    def by_two(values):
        return [values[i : i + 2] for i in range(0, len(values), 2)]

    x_own, x_other = own_and_other(inputs)
    x_came = far.swap(x_other)

    shards = []
    for k in range(half):
        own = mine * half + lax.rem(at + k, half)
        shards += [own, lax.rem(own + half, seq)]
    per_shard = width // BLOCK
    block_of_slot = (
        jnp.stack(shards)[:, None] * per_shard + jnp.arange(per_shard, dtype=jnp.int32)
    ).reshape(-1).astype(jnp.int32)
    doc = lax.dynamic_index_in_dim(doc_tokens, mine, 0, False)
    chosen = lax.dynamic_index_in_dim(random_blocks, mine, 0, False)
    tables = block_tables(block_of_slot, doc, chosen)

    def my_cols(weight):
        return lax.dynamic_slice_in_dim(weight, at * cols, cols, weight.ndim - 1)

    weights = (query_weight, key_weight, value_weight)
    w_qkv = jnp.concatenate([my_cols(w) for w in weights], 1)
    b_qkv = jnp.concatenate(
        [my_cols(query_bias), jnp.zeros((cols,), low), my_cols(value_bias)]
    ).astype(full)
    wo = jnp.concatenate(
        [
            lax.dynamic_slice_in_dim(
                output_weight, lax.rem(at + half - k, half) * cols, cols, 0
            )
            for k in range(half)
        ],
        0,
    )
    vec = jnp.stack(
        [output_bias, first_gain, first_shift, outer_bias, second_gain, second_shift]
    ).astype(full)
    vec = jnp.pad(vec, ((0, 2), (0, 0)))
    b1 = jnp.broadcast_to(inner_bias.astype(full), (8, inner_bias.shape[0]))

    x_came, cotangent, w_qkv, b_qkv, wo, vec, b1, *tables = in_step(
        [x_came, cotangent, w_qkv, b_qkv, wo, vec, b1, *tables]
    )
    cot_came = far.swap(lax.dynamic_index_in_dim(cotangent, 1 - mine, 0, False))
    x_parts = [x_own, x_came]
    for k in range(1, half):
        x_parts += [near.send(x_own, half - k), near.send(x_came, half - k)]
    x_all = jnp.concatenate(x_parts, 0)
    qkv = (dot(x_all, w_qkv, NN) + b_qkv).astype(low)
    heads_context, lse = attend(qkv, tables, heads, nb)
    heads_context, lse, cot_came = in_step([heads_context, lse, cot_came])
    context = [heads_context] + [
        near.send(heads_context[k * tokens : (k + 1) * tokens], k) for k in range(1, half)
    ]
    values = feed_forward(
        mine, x_all, cotangent, cot_came, context, wo, inner_weight, outer_weight, vec, b1
    )
    result, result_half, values = values[0], list(values[1:3]), values[3:]
    first_low, active, d_inner, d_outer, d_attended, d_resid, sums, inner_sum, *d_context = values
    heads_grad = [d_context[0]] + [near.send(d_context[k], half - k) for k in range(1, half)]

    packed = jnp.concatenate([sums[:6].reshape(-1), inner_sum[0]]).reshape(-1, D)
    packed = jnp.pad(packed, ((0, 256 - packed.shape[0]), (0, 0))).astype(low)

    def outer_product(part, k, came=()):
        return tall_product(active, d_outer, part, half, 768, came)

    def inner_product(part, k, came=()):
        return wide_product(first_low, d_inner, part, half, 768, came)

    def out_product(part, k, came=()):
        k = (half - k) % half
        if cols % 128:
            total = dot(context[k][:tokens], d_attended, TN)
            return sum([c.astype(full) for c in came], total).astype(low)
        return tall_product(context[k], d_attended, 0, 1, cols, came)

    def packed_part(part, k, came=()):
        size = 256 // half
        total = lax.dynamic_slice_in_dim(packed, part * size, size, 0).astype(full)
        return sum([c.astype(full) for c in came], total).astype(low)

    def give(product):
        return [product(lax.rem(at + k, half), k) for k in range(1, half)]

    def send(parts):
        return [near.send(part, k) for k, part in enumerate(parts, 1)]

    outer_give = give(outer_product)
    outer_give[0], first_low, d_attended = in_step([outer_give[0], first_low, d_attended])
    outer_came = send(outer_give)
    inner_came = send(give(inner_product))
    out_came = send(give(out_product))
    packed_came = send(give(packed_part))
    outer_grad = outer_product(at, 0, outer_came)
    outer_main = outer_grad.shape[0] * 3 // 4
    early = Chain([outer_grad[:outer_main], outer_grad[outer_main:]], [HalveStep([main[0], side[0]])])
    early.start()
    inner_came[0], out_came[0], packed_came[0], *early.parts = in_step(
        [inner_came[0], out_came[0], packed_came[0]] + early.parts
    )
    inner_grad = inner_product(at, 0, inner_came)
    out_grad = out_product(at, 0, out_came)
    packed = packed_part(at, 0, packed_came)
    inner_grad, out_grad, packed, *early.came = in_step(
        [inner_grad, out_grad, packed] + early.came
    )
    early.finish()
    inner_main = inner_grad.shape[0] * 5 // 6
    mixed = jnp.concatenate([out_grad, packed, inner_grad[inner_main:]], 0)
    rest = Chain([inner_grad[:inner_main], mixed], [HalveStep([main[0], side[0]])])
    heads_grad[0], *rest.parts = in_step([heads_grad[0]] + early.parts + rest.parts)
    early.parts, rest.parts = rest.parts[:2], rest.parts[2:]

    first_sizes = [
        (outer_main // 2, inner_main // 2),
        ((outer_grad.shape[0] - outer_main) // 2, mixed.shape[0] // 2),
    ]
    first = Chain([], [HalveStep([main[i], side[i]]) for i in (1, 2)])
    first.steps += [SumStep(pair) for pair in last]
    first.steps += [JoinStep([main[i], side[i]]) for i in (2, 1)]

    steps = cols // 128 if cols % 128 == 0 else 1
    d_qkv = ()
    result_came = []
    for k in range(steps):
        chain = first if first.parts else rest
        chain.start()
        if k == 2:
            result_half[0], d_query = in_step([result_half[0], d_qkv[0]])
            d_qkv = (d_query,) + d_qkv[1:]
            result_came.append(far.swap(result_half[0]))
        d_qkv = attend_back(
            qkv, heads_grad, heads_context, lse, tables, heads // steps, nb, d_qkv, k
        )
        d_query, d_key, d_value, *came = in_step(list(d_qkv) + chain.came + result_came)
        d_qkv = (d_query, d_key, d_value)
        chain.came, result_came = came[: len(chain.came)], came[len(chain.came) :]
        chain.finish()
        if chain is rest:
            first.parts = [
                jnp.concatenate([e, r], 0) for e, r in zip(early.parts, rest.parts)
            ]
        d_query, *first.parts = in_step([d_query] + first.parts)
        d_qkv = (d_query, d_key, d_value)

    while len(first.steps) > 3:
        first.start()
        first.finish()
    sums_at_last = first.steps.pop(0)
    some = first.parts[0].shape[0] // 4 // 8 * 8
    main_parts = [first.parts[0][:some], first.parts[0][some:]]
    last_came = sums_at_last.start([main_parts[0], first.parts[1]])
    result_half[1:], d_query = in_step([*result_half[1:], d_query])[:-1], d_query
    result_came += [far.swap(piece) for piece in result_half[len(result_came) :]]
    if cols % 128 == 0:
        heads_part = heads_products(x_all, *d_qkv)
    else:
        sums_of = [jnp.pad(column_sum(d)[None, :], ((0, 31), (0, 0))) for d in d_qkv]
        heads_part = [
            jnp.concatenate([dot(x_all, d, TN), total], 0) for d, total in zip(d_qkv, sums_of)
        ]
        heads_part = jnp.concatenate(heads_part, 1).astype(low)
    heads_part, d_query, d_key, d_value, *came = in_step(
        [heads_part, d_query, d_key, d_value] + last_came + result_came
    )
    last_came, result_came = came[:2], came[2:]
    main_parts[1], heads_part = in_step([main_parts[1], heads_part])

    second = Chain([heads_part], [HalveStep([main[i]]) for i in range(3)])
    second.steps += [SumStep(pair) for pair in last]
    second.steps += [JoinStep([main[i]]) for i in (2, 1, 0)]
    second.start()
    last_came += sums_at_last.start(main_parts[1:])
    if cols % 128 == 0:
        d_parts = list(inputs_products((d_query, d_key, d_value), weights, at, half))
    else:
        parts = zip((d_query, d_key, d_value), (my_cols(w) for w in weights))
        d_parts = sum(dot(d, w, NT) for d, w in parts).astype(low)
        d_parts = cut(d_parts, [tokens] * half)
    d_parts[0], *came = in_step([d_parts[0]] + last_came + second.came)
    second.came = came[3:]
    sums = sums_at_last.finish([main_parts[0], first.parts[1], main_parts[1]], came[:3])
    first.parts = [jnp.concatenate([sums[0], sums[2]], 0), sums[1]]
    second.finish()

    def together(*beside):
        count = len(first.came or ())
        values = in_step(list(first.came or ()) + second.came + list(beside))
        if count:
            first.came = values[:count]
            first.finish()
        second.came = values[count : count + len(second.came)]
        second.finish()
        return values[len(values) - len(beside) :]

    second.start()
    first.start()
    d_came = [near.send(d_parts[k], k) for k in range(1, half)]
    d_came = together(*d_came)
    second.start()
    first.start()
    d_input = d_resid + d_parts[0].astype(full)
    for value in d_came:
        d_input = d_input + value.astype(full)
    d_input = d_input.astype(low)
    result = from_rows(result, jnp.concatenate(result_came, 0))
    d_input, result = together(d_input, result)
    for _ in last[:-1]:
        second.step()
    second.start()
    pieces = [p for share, size in zip(first.parts, first_sizes) for p in cut(share, size)]
    outer = Chain([pieces[0], pieces[2]], [JoinStep([main[0], side[0]])])
    inner = Chain([pieces[1], pieces[3]], [JoinStep([main[0], side[0]])])
    outer.start()
    d_input_came = [far.swap(d_input[width : width + width // 2])]
    values = together(*outer.came, *inner.parts, *d_input_came)
    outer.came, inner.parts, d_input_came = values[:2], values[2:4], values[4:]
    outer.finish()
    second.start()
    inner.start()
    outer_came = [near.send(part, k) for k in range(1, half) for part in outer.parts]
    placed = spread_outer(*outer.parts, at, ()) if half == 2 else outer.parts
    count = 2 + len(outer_came)
    values = together(*inner.came, *outer_came, d_input, *placed)
    inner.came, outer_came, d_input = values[:2], values[2:count], values[count]
    outer.parts = values[count + 1 :]
    inner.finish()
    second.start()
    inner_came = [near.send(part, k) for k in range(1, half) for part in inner.parts]
    d_input_came.append(far.swap(d_input[width + width // 2 :]))
    if half == 2:
        outer.parts = list(spread_outer(*outer_came, 1 - at, outer.parts))
    count = len(inner_came)
    values = together(*inner_came, *d_input_came, *outer.parts)
    inner_came, d_input_came, outer.parts = (
        values[:count],
        values[count : count + 2],
        values[count + 2 :],
    )
    second.start()
    d_input = from_rows(d_input[:width], jnp.concatenate(d_input_came, 0))
    small = out_grad.shape[0], packed.shape[0], inner_grad.shape[0] - inner_main
    out_grad, packed, inner_b = cut(inner.parts[1], small)
    packed = [packed] + [cut(p, small)[1] for p in inner_came[1::2]]
    packed = by_device(packed).reshape(-1, D).astype(full)
    if half == 2:
        (outer_grad,) = outer.parts
        placed = spread_inner(*inner.parts, at, ())
        inner_grad, out_grad = spread_inner(*inner_came, 1 - at, placed)
    else:
        outer_grad = [jnp.concatenate(p, 0) for p in [outer.parts] + by_two(outer_came)]
        outer_grad = by_device(outer_grad).reshape(-1, D).astype(full)
        inner_grad = [jnp.concatenate([inner.parts[0], inner_b], 0)]
        out_grad = [out_grad]
        for first_part, other in by_two(inner_came):
            inner_grad.append(jnp.concatenate([first_part, cut(other, small)[2]], 0))
            out_grad.append(cut(other, small)[0])
        inner_grad = by_device(inner_grad).reshape(-1, D, D).astype(full)
        inner_grad = inner_grad.transpose(1, 0, 2).reshape(D, -1)
        out_grad = by_device(out_grad).reshape(-1, D).astype(full)
    d_input, inner_grad, out_grad, outer_grad, packed = together(
        d_input, inner_grad, out_grad, outer_grad, packed
    )
    heads_parts = second.parts[0]
    if half == 2:
        heads_came = near.send(heads_parts, 1)
        query_grad, key_grad, value_grad = spread_columns(
            heads_came, 1 - at, spread_columns(heads_parts, at, ())
        )
        biases = [p[D].astype(full) for p in (heads_parts, heads_came)]
        biases = jnp.where(at == 0, jnp.stack(biases), jnp.stack(biases[::-1]))
        query_bias_grad = biases[:, :cols].reshape(-1)
        value_bias_grad = biases[:, 2 * cols :].reshape(-1)
    else:
        heads_parts = by_device([heads_parts] + [near.send(heads_parts, k) for k in range(1, half)])
        query_grad, key_grad, value_grad = (
            jnp.concatenate([p[:, i * cols : (i + 1) * cols] for p in heads_parts], 1).astype(full)
            for i in range(3)
        )
        query_bias_grad, value_bias_grad = query_grad[D], value_grad[D]
        query_grad, key_grad, value_grad = query_grad[:D], key_grad[:D], value_grad[:D]
    return (
        result,
        d_input,
        query_grad,
        query_bias_grad,
        key_grad,
        value_grad,
        value_bias_grad,
        out_grad,
        packed[0],
        packed[1],
        packed[2],
        inner_grad,
        packed[6:10].reshape(-1),
        outer_grad,
        packed[3],
        packed[4],
        packed[5],
    )


def solution(mesh):
    tokens = P("rows", "seq", None)
    in_specs = (tokens,) + (P(),) * 15 + (P("rows"), P("rows", None, None), tokens)
    out_specs = (tokens, tokens) + (P(),) * 15
    return jax.shard_map(
        partial(per_device, mesh.shape["seq"], mesh.shape["rows"]),
        mesh=mesh,
        in_specs=in_specs,
        out_specs=out_specs,
        check_vma=False,
    )
```

```python
import functools
from functools import partial

import jax
import jax.numpy as jnp
from jax import lax
from jax.experimental import pallas as pl
from jax.experimental.pallas import tpu as pltpu
from jax.sharding import PartitionSpec as P

D = 768
HEADS = 12
HEAD = 64
BLOCK = 64
SETS = 8
CHIPS_Z = 4

EPSILON = 1e-05
NEG_FILL = -1e30

SHORT = pl.CostEstimate(flops=1 << 20, bytes_accessed=1 << 10, transcendentals=0)

NT = (((1,), (1,)), ((), ()))
NN = (((1,), (0,)), ((), ()))
TN = (((0,), (0,)), ((), ()))


def dot(left, right, dims):
    return lax.dot_general(left, right, dims, preferred_element_type=jnp.float32)


def head_groups(heads):
    groups, at = [], 0
    while at < heads:
        n = 2 if heads - at >= 2 else 1
        groups.append((at, n))
        at += n
    return groups


def lanes_of(at, n):
    return slice(at * HEAD, (at + n) * HEAD)


def diagonal(n, rows):
    row = lax.broadcasted_iota(jnp.int32, (n * rows, n * HEAD), 0) // rows
    lane = lax.broadcasted_iota(jnp.int32, (n * rows, n * HEAD), 1) // HEAD
    return (row == lane).astype(jnp.float32)


def spread_heads(block, diag, n):
    if n == 1:
        return block
    return jnp.concatenate([block] * n, 0) * diag.astype(block.dtype)


def fold_heads(full, diag, n):
    if n == 1:
        return full
    rows = full.shape[0] // n
    kept = full * diag
    out = kept[:rows]
    for h in range(1, n):
        out = out + kept[h * rows : (h + 1) * rows]
    return out


def rows_of(slot):
    return pl.ds(pl.multiple_of(slot * BLOCK, BLOCK), BLOCK)


def gather_rows(ref, slots, lanes):
    return jnp.concatenate([ref[rows_of(s), lanes] for s in slots], 0)


def as_row(column):
    n = column.shape[0]
    same = lax.broadcasted_iota(jnp.int32, (n, n), 0) == lax.broadcasted_iota(jnp.int32, (n, n), 1)
    return jnp.sum(jnp.where(same, column, 0.0), 0, keepdims=True)


def attend_kernel(
    heads,
    nb,
    abreast,
    key_at_ref,
    query_at_ref,
    q_ref,
    k_ref,
    v_ref,
    task_bias_ref,
    lead_bias_ref,
    o_ref,
    lse_ref,
):
    groups = head_groups(heads)
    scale = jnp.bfloat16(HEAD**-0.5)
    diags = {n: diagonal(n, BLOCK) for _, n in groups}

    def local(i, carry):
        work, scores, probs = [], [], []
        for u in range(abreast):
            t = abreast * i + u
            ks = [key_at_ref[t, b] for b in range(SETS)]
            work += [(t, ks, query_at_ref[t], lanes_of(at, n), n) for at, n in groups]
        for t, ks, qs, lanes, n in work:
            query = spread_heads(q_ref[rows_of(qs), lanes] * scale, diags[n], n)
            score = dot(query, gather_rows(k_ref, ks, lanes), NT)
            scores.append(score + task_bias_ref[pl.ds(t, 1), :])
        for score in scores:
            top = jnp.max(score, 1, keepdims=True)
            prob = jnp.exp(score - top)
            probs.append((prob.astype(jnp.bfloat16), top, jnp.sum(prob, 1, keepdims=True)))
        for (t, ks, qs, lanes, n), (prob, top, total) in zip(work, probs):
            out = dot(prob, gather_rows(v_ref, ks, lanes), NN) * (1.0 / total)
            out = fold_heads(out, diags[n], n)
            o_ref[rows_of(qs), lanes] = out.astype(jnp.bfloat16)
            lse_ref[qs, :, lanes] = as_row(top + jnp.log(total))
        return carry

    lax.fori_loop(0, (nb - 2) // abreast, local, 0)

    rows = 2 * BLOCK
    qs = query_at_ref[nb - 2]
    lead_rows = pl.ds(pl.multiple_of(qs * BLOCK, BLOCK), rows)
    scores, probs = [], []
    for at, n in groups:
        lanes = lanes_of(at, n)
        query = spread_heads(q_ref[lead_rows, lanes] * scale, diagonal(n, rows), n)
        scores.append(dot(query, k_ref[:, lanes], NT) + lead_bias_ref[...])
    for score in scores:
        top = jnp.max(score, 1, keepdims=True)
        prob = jnp.exp(score - top)
        probs.append((prob.astype(jnp.bfloat16), top, jnp.sum(prob, 1, keepdims=True)))
    for (at, n), (prob, top, total) in zip(groups, probs):
        lanes = lanes_of(at, n)
        out = dot(prob, v_ref[:, lanes], NN) * (1.0 / total)
        o_ref[lead_rows, lanes] = fold_heads(out, diagonal(n, rows), n).astype(jnp.bfloat16)
        lse = top + jnp.log(total)
        each = [as_row(lse[h * rows : (h + 1) * rows]) for h in range(n)]
        for b in range(2):
            part = slice(b * BLOCK, (b + 1) * BLOCK)
            lse_ref[qs + b, :, lanes] = jnp.concatenate([row[:, part] for row in each], 1)


def attend_back_kernel(
    heads,
    nb,
    abreast,
    pieces,
    key_at_ref,
    bias_at_ref,
    query_at_ref,
    places_ref,
    q_ref,
    k_ref,
    v_ref,
    o_ref,
    lse_ref,
    *rest,
):
    dq_ref, dk_ref, dv_ref, dk_acc, dv_acc, delta_ref, g_ref, bias_ref = rest[-8:]
    rows = nb * BLOCK // pieces
    for i in range(pieces):
        g_ref[i * rows : (i + 1) * rows, :] = rest[i][...]
    groups = head_groups(heads)
    diags = {n: diagonal(n, BLOCK) for _, n in groups}
    inside = lax.broadcasted_iota(jnp.int32, (BLOCK, 2 * HEAD), 0)
    for s in range(nb):
        valid = places_ref[s] * BLOCK + inside < places_ref[nb]
        bias_ref[s * BLOCK : (s + 1) * BLOCK, :] = jnp.where(valid, 0.0, NEG_FILL)
    every = nb * BLOCK
    bias_ref[every:, :] = jnp.full_like(bias_ref[every:, :], NEG_FILL)
    dk_acc[every:, :] = jnp.zeros_like(dk_acc[every:, :])
    dv_acc[every:, :] = jnp.zeros_like(dv_acc[every:, :])
    scale = HEAD**-0.5

    for at, n in groups:
        lanes = lanes_of(at, n)
        row = lax.broadcasted_iota(jnp.int32, (16, n * HEAD), 0)
        pick = row == lax.broadcasted_iota(jnp.int32, (16, n * HEAD), 1) // HEAD
        pick = pick.astype(jnp.float32).astype(jnp.bfloat16)
        for s in range(0, nb, 4):
            some = slice(s * BLOCK, (s + 4) * BLOCK)
            both = g_ref[some, lanes].astype(jnp.float32) * o_ref[some, lanes].astype(jnp.float32)
            high = both.astype(jnp.bfloat16)
            less = (both - high.astype(jnp.float32)).astype(jnp.bfloat16)
            delta = dot(pick, high, NT) + dot(pick, less, NT)
            for j in range(4):
                part = slice(j * BLOCK, (j + 1) * BLOCK)
                delta_ref[s + j, :, lanes] = jnp.concatenate(
                    [delta[h : h + 1, part] for h in range(n)], 1
                )

    both_rows = 2 * BLOCK
    lead = query_at_ref[nb - 2]
    lead_rows = pl.ds(pl.multiple_of(lead * BLOCK, BLOCK), both_rows)

    def lead_row(ref, lanes, n):
        first, second = ref[lead, :, lanes], ref[lead + 1, :, lanes]
        heads_of = [slice(h * HEAD, (h + 1) * HEAD) for h in range(n)]
        return jnp.concatenate([r[:, h] for h in heads_of for r in (first, second)], 1)

    for at, n in groups:
        lanes, diag = lanes_of(at, n), diagonal(n, both_rows)
        query = spread_heads(q_ref[lead_rows, lanes] * jnp.bfloat16(scale), diag, n)
        grad = spread_heads(g_ref[lead_rows, lanes], diag, n)
        score = dot(k_ref[:, lanes], query, NT)
        bias = jnp.concatenate([bias_ref[:every, :]] * n, 1)
        prob = jnp.exp(score + bias - lead_row(lse_ref, lanes, n))
        d_prob = dot(v_ref[:, lanes], grad, NT)
        d_score = (prob * (d_prob - lead_row(delta_ref, lanes, n))).astype(jnp.bfloat16)
        dv_acc[:every, lanes] = dot(prob.astype(jnp.bfloat16), grad, NN)
        dk_acc[:every, lanes] = dot(d_score, query, NN)
        d_query = fold_heads(dot(d_score, k_ref[:, lanes], TN), diag, n) * scale
        dq_ref[lead_rows, lanes] = d_query.astype(jnp.bfloat16)

    def several(i, carry):
        work, scores, probs, grads = [], [], [], []
        for u in range(abreast):
            t = abreast * i + u
            ks = [key_at_ref[t, b] for b in range(SETS)]
            bs = [bias_at_ref[t, b] for b in range(SETS)]
            work += [(ks, bs, query_at_ref[t], lanes_of(at, n), n) for at, n in groups]
        for ks, bs, qs, lanes, n in work:
            diag = diags[n]
            query = spread_heads(q_ref[rows_of(qs), lanes] * jnp.bfloat16(scale), diag, n)
            grad = spread_heads(g_ref[rows_of(qs), lanes], diag, n)
            keys = gather_rows(k_ref, ks, lanes)
            score = dot(keys, query, NT)
            d_prob = dot(gather_rows(v_ref, ks, lanes), grad, NT)
            scores.append((query, grad, keys, score, d_prob))
        for (ks, bs, qs, lanes, n), (query, grad, keys, score, d_prob) in zip(work, scores):
            bias = gather_rows(bias_ref, bs, slice(None))[:, : n * HEAD]
            prob = jnp.exp(score + bias - lse_ref[qs, :, lanes])
            d_score = (prob * (d_prob - delta_ref[qs, :, lanes])).astype(jnp.bfloat16)
            probs.append((prob.astype(jnp.bfloat16), d_score))
        for (query, grad, keys, _, _), (prob, d_score) in zip(scores, probs):
            grads.append((dot(prob, grad, NN), dot(d_score, query, NN), dot(d_score, keys, TN)))
        for (ks, bs, qs, lanes, n), (d_value, d_key, d_query) in zip(work, grads):
            before = [(dk_acc[rows_of(a), lanes], dv_acc[rows_of(a), lanes]) for a in bs]
            for j, a in enumerate(bs):
                part = slice(j * BLOCK, (j + 1) * BLOCK)
                dk_acc[rows_of(a), lanes] = before[j][0] + d_key[part]
                dv_acc[rows_of(a), lanes] = before[j][1] + d_value[part]
            d_query = fold_heads(d_query, diags[n], n) * scale
            dq_ref[rows_of(qs), lanes] = d_query.astype(jnp.bfloat16)
        return carry

    lax.fori_loop(0, (nb - 2) // abreast, several, 0)
    dk_ref[...] = dk_acc[: nb * BLOCK].astype(jnp.bfloat16)
    dv_ref[...] = dv_acc[: nb * BLOCK].astype(jnp.bfloat16)


VMEM = pl.BlockSpec(memory_space=pltpu.VMEM)
SMEM = pl.BlockSpec(memory_space=pltpu.SMEM)


def columns(array, at, width):
    if array.shape[1] == width or width % 128 == 0:
        return array, pl.BlockSpec((array.shape[0], width), lambda i: (0, at))
    array = array[:, at * width : (at + 1) * width]
    return array, pl.BlockSpec(array.shape, lambda i: (0, 0))


def attend(qkv, tables, heads, nb):
    key_at, _, query_at, _, task_bias, lead_bias = tables
    width = heads * HEAD
    operands, specs = zip(*[columns(qkv, i, width) for i in range(3)])
    return pl.pallas_call(
        partial(attend_kernel, heads, nb, 2),
        grid=(1,),
        out_shape=(
            jax.ShapeDtypeStruct((nb * BLOCK, width), jnp.bfloat16),
            jax.ShapeDtypeStruct((nb, 1, width), jnp.float32),
        ),
        in_specs=[SMEM] * 2 + list(specs) + [VMEM] * 2,
        out_specs=(VMEM, VMEM),
        compiler_params=pltpu.CompilerParams(vmem_limit_bytes=30 << 20),
        cost_estimate=pl.CostEstimate(
            flops=2_000_000_000, bytes_accessed=8 << 20, transcendentals=0
        ),
        name="attend",
    )(key_at, query_at, *operands, task_bias, lead_bias)


def attend_back(qkv, grads, context, lse, tables, heads, nb, held, at):
    key_at, bias_at, query_at, places, _, _ = tables
    total = context.shape[1]
    width = heads * HEAD
    parts = total // width
    operands, specs = zip(
        *[columns(qkv, i * parts + at, width) for i in range(3)], columns(context, at, width)
    )
    pieces, piece_specs = zip(*[columns(g, at, width) for g in grads])
    lse_spec = pl.BlockSpec((nb, 1, width), lambda i: (0, 0, at))
    out = jax.ShapeDtypeStruct((nb * BLOCK, total), jnp.bfloat16)
    out_spec = pl.BlockSpec((nb * BLOCK, width), lambda i: (0, at))
    count = 4 + len(operands) + 1 + len(pieces)
    abreast = 5 if (nb - 2) % 5 == 0 else 2
    return pl.pallas_call(
        partial(attend_back_kernel, heads, nb, abreast, len(pieces)),
        grid=(1,),
        out_shape=(out, out, out),
        in_specs=[SMEM] * 4
        + list(specs)
        + [lse_spec]
        + list(piece_specs)
        + [pl.BlockSpec(memory_space=pl.ANY)] * len(held),
        out_specs=(out_spec,) * 3,
        input_output_aliases={count + i: i for i in range(len(held))},
        scratch_shapes=[
            pltpu.VMEM(((nb + 1) * BLOCK, width), jnp.float32),
            pltpu.VMEM(((nb + 1) * BLOCK, width), jnp.float32),
            pltpu.VMEM((nb, 1, width), jnp.float32),
            pltpu.VMEM((nb * BLOCK, width), jnp.bfloat16),
            pltpu.VMEM(((nb + 1) * BLOCK, 2 * HEAD), jnp.float32),
        ],
        compiler_params=pltpu.CompilerParams(vmem_limit_bytes=52 << 20),
        cost_estimate=pl.CostEstimate(
            flops=15_000_000_000, bytes_accessed=6 << 20, transcendentals=0
        ),
        name="attend_back",
    )(key_at, bias_at, query_at, places, *operands, lse, *pieces, *held)


def block_tables(block_of_slot, doc, random_blocks):
    nb = random_blocks.shape[0]
    every = jnp.arange(nb, dtype=jnp.int32)
    slot_of_block = jnp.sum(
        jnp.where(block_of_slot[None, :] == every[:, None], every[None, :], 0), 1
    )
    ids = every[2:]
    before, after = ids - 1, ids + 1
    always_on = ids >= 0
    index = jnp.concatenate(
        [jnp.stack([ids * 0, ids * 0 + 1, before, ids, after], -1), random_blocks[2:]], -1
    )
    allowed = jnp.stack(
        [always_on, always_on, before >= 2, always_on, after < nb] + [always_on] * 3, -1
    )
    index = jnp.clip(index, 0, nb - 1)
    slots = jnp.sum(jnp.where(index[..., None] == block_of_slot, every, 0), -1)
    key_at = slots
    bias_at = jnp.where(allowed, slots, nb)
    query_at = jnp.concatenate([slot_of_block[2:], slot_of_block[:2]])
    inside = jnp.arange(BLOCK, dtype=jnp.int32)
    bias = jnp.where(block_of_slot[:, None] * BLOCK + inside < doc, 0.0, NEG_FILL)
    bias = bias.astype(jnp.float32)
    lead_bias = bias.reshape(1, -1)
    task_bias = (index[..., None] * BLOCK + inside < doc) & allowed[..., None]
    task_bias = jnp.where(task_bias, 0.0, NEG_FILL).astype(jnp.float32).reshape(nb - 2, -1)
    places = jnp.concatenate([block_of_slot, jnp.reshape(doc, (1,))])
    return key_at, bias_at, query_at, places, task_bias, lead_bias


TANH_SCALE = 0.7978845608028654
TANH_CUBE = 0.044715


def norm_rows(value):
    center = value - jnp.mean(value, -1, keepdims=True)
    scale = lax.rsqrt(jnp.mean(center * center, -1, keepdims=True) + EPSILON)
    return center * scale, scale


def norm_back(grad, normal, scale):
    return scale * (
        grad
        - jnp.mean(grad, -1, keepdims=True)
        - normal * jnp.mean(grad * normal, -1, keepdims=True)
    )


def feed_forward_kernel(
    chunk,
    few,
    pieces,
    mine_ref,
    x_ref,
    cot_own_ref,
    cot_came_ref,
    wo_ref,
    w1_hbm_ref,
    w2_hbm_ref,
    vec_ref,
    b1_ref,
    *refs,
):
    context_refs, refs = refs[:pieces], refs[pieces:]
    result_refs, refs = refs[:3], refs[3:]
    first_ref, active_out_ref, d_inner_out_ref, d_outer_ref, d_attended_ref = refs[:5]
    d_resid_ref, sums_ref, inner_sum_ref = refs[5:8]
    d_context_refs, refs = refs[8 : 8 + pieces], refs[8 + pieces :]
    w1_ref, w2_ref, active_ref, d_inner_ref, *refs = refs
    slope_ref, held_ref, normal_ref, scale_ref, result_ref, sems = refs
    cols = D // pieces
    first_step = pl.program_id(0) == 0
    tile = active_ref.shape[0]
    tokens_at = pl.ds(pl.multiple_of(pl.program_id(0) * tile, tile), tile)
    load_w1 = pltpu.make_async_copy(w1_hbm_ref, w1_ref, sems.at[0])
    load_w2 = pltpu.make_async_copy(w2_hbm_ref, w2_ref, sems.at[1])
    store_active = pltpu.make_async_copy(active_ref, active_out_ref.at[tokens_at, :], sems.at[2])
    store_d_inner = pltpu.make_async_copy(d_inner_ref, d_inner_out_ref.at[tokens_at, :], sems.at[3])
    low, full = jnp.bfloat16, jnp.float32
    tokens, hidden = active_ref.shape

    @pl.when(first_step)
    def _():
        load_w1.start()
        load_w2.start()
        sums_ref[...] = jnp.zeros_like(sums_ref)
        inner_sum_ref[...] = jnp.zeros_like(inner_sum_ref)

    bo, g1, s1, b2, g2, s2 = [vec_ref[i : i + 1, :] for i in range(6)]

    chunks = [slice(i, i + few) for i in range(0, tokens, few)]

    def each_columns(body):
        def step(i, carry):
            body(pl.ds(pl.multiple_of(i * chunk, chunk), chunk))
            return carry

        lax.fori_loop(0, hidden // chunk, step, 0)

    def add_sum(row, values):
        sums_ref[row : row + 1, :] += jnp.sum(values, 0, keepdims=True)

    def add_context(rows):
        parts = [
            dot(ref[rows, :], wo_ref[k * cols : (k + 1) * cols, :], NN)
            for k, ref in enumerate(context_refs)
        ]
        return sum(parts[1:], parts[0])

    for rows, attended in [(rows, add_context(rows)) for rows in chunks]:
        normal, scale = norm_rows(x_ref[rows, :].astype(full) + attended + bo)
        first = normal * g1 + s1
        normal_ref[rows, :] = normal
        scale_ref[rows, :] = jnp.broadcast_to(scale, (few, 128))
        held_ref[rows, :] = first
        first_ref[rows, :] = first.astype(low)

    @pl.when(first_step)
    def _():
        load_w1.wait()

    @each_columns
    def _(cols):
        u = dot(first_ref[...], w1_ref[:, cols], NN) + b1_ref[:1, cols]
        square = u * u
        tanh = jnp.tanh(u * (TANH_SCALE + (TANH_SCALE * TANH_CUBE) * square))
        share = 0.5 * tanh + 0.5
        active_ref[:, cols] = (u * share).astype(low)
        slope_ref[:, cols] = share + (0.5 * u) * (1.0 - tanh * tanh) * (
            TANH_SCALE + (3 * TANH_SCALE * TANH_CUBE) * square
        )

    store_active.start()

    @pl.when(first_step)
    def _():
        load_w2.wait()

    for rows, outer in [(rows, dot(active_ref[rows, :], w2_ref[...], NN)) for rows in chunks]:
        normal, scale = norm_rows(held_ref[rows, :] + outer + b2)
        result_ref[rows, :] = (normal * g2 + s2).astype(low)
        own = pl.program_id(0) == 0
        cot = jnp.where(own, cot_own_ref[0, rows, :], cot_came_ref[rows, :]).astype(full)
        d_second = norm_back(cot * g2, normal, scale)
        held_ref[rows, :] = d_second
        d_outer = d_second.astype(low)
        d_outer_ref[rows, :] = d_outer
        add_sum(3, d_outer.astype(full))
        add_sum(4, cot * normal)
        add_sum(5, cot)

    @pl.when(first_step)
    def _():
        result_refs[0][...] = result_ref[...]

    @pl.when(jnp.logical_not(first_step))
    def _():
        result_refs[1][...] = result_ref[: tile // 2, :]
        result_refs[2][...] = result_ref[tile // 2 :, :]

    @each_columns
    def _(cols):
        d_inner = (dot(d_outer_ref[...], w2_ref[cols, :], NT) * slope_ref[:, cols]).astype(low)
        d_inner_ref[:, cols] = d_inner
        inner_sum_ref[:1, cols] += jnp.sum(d_inner.astype(full), 0, keepdims=True)

    store_d_inner.start()
    for rows, back in [(rows, dot(d_inner_ref[rows, :], w1_ref[...], NT)) for rows in chunks]:
        d_first = held_ref[rows, :] + back
        normal = normal_ref[rows, :]
        add_sum(1, d_first * normal)
        add_sum(2, d_first)
        d_resid = norm_back(d_first * g1, normal, scale_ref[rows, :1])
        d_resid_ref[rows, :] = d_resid
        d_attended = d_resid.astype(low)
        d_attended_ref[rows, :] = d_attended
        add_sum(0, d_attended.astype(full))
    for rows in chunks:
        for k, ref in enumerate(d_context_refs):
            part = dot(d_attended_ref[rows, :], wo_ref[k * cols : (k + 1) * cols, :], NT)
            ref[rows, :] = part.astype(low)
    store_active.wait()
    store_d_inner.wait()


def feed_forward(mine, x, cot, cot_came, context, wo, w1, w2, vec, b1):
    low, full = jnp.bfloat16, jnp.float32
    tile, hidden = cot_came.shape[0], w1.shape[1]
    tokens, cols = 2 * tile, context[0].shape[1]
    row = pl.BlockSpec((tile, D), lambda i, at: (i, 0))
    part = pl.BlockSpec((tile, cols), lambda i, at: (i, 0))
    there = pl.BlockSpec(memory_space=pl.ANY)
    shards = (tile, tile // 2, tile // 2)
    once = pl.Buffered(1)
    whole = lambda a: pl.BlockSpec(a.shape, lambda i, at: (0,) * a.ndim, pipeline_mode=once)
    shape = jax.ShapeDtypeStruct
    return pl.pallas_call(
        partial(feed_forward_kernel, 1024, 256, len(context)),
        grid_spec=pltpu.PrefetchScalarGridSpec(
            num_scalar_prefetch=1,
            grid=(tokens // tile,),
            in_specs=[
                row,
                pl.BlockSpec((1, tile, D), lambda i, at: (at[0], 0, 0), pipeline_mode=once),
            ]
            + [whole(cot_came), whole(wo), there, there, whole(vec), whole(b1)]
            + [part] * len(context),
            out_specs=[pl.BlockSpec((n, D), lambda i, at: (0, 0)) for n in shards]
            + [row, there, there, row, row, row]
            + [pl.BlockSpec((8, n), lambda i, at: (0, 0)) for n in (D, hidden)]
            + [part] * len(context),
            scratch_shapes=[
                pltpu.VMEM(w1.shape, low),
                pltpu.VMEM(w2.shape, low),
                pltpu.VMEM((tile, hidden), low),
                pltpu.VMEM((tile, hidden), low),
                pltpu.VMEM((tile, hidden), full),
                pltpu.VMEM((tile, D), full),
                pltpu.VMEM((tile, D), full),
                pltpu.VMEM((tile, 128), full),
                pltpu.VMEM((tile, D), low),
                pltpu.SemaphoreType.DMA((4,)),
            ],
        ),
        out_shape=[shape((n, D), low) for n in shards]
        + [
            shape((tokens, D), low),
            shape((tokens, hidden), low),
            shape((tokens, hidden), low),
            shape((tokens, D), low),
            shape((tokens, D), low),
            shape((tokens, D), full),
            shape((8, D), full),
            shape((8, hidden), full),
        ]
        + [shape((tokens, cols), low)] * len(context),
        compiler_params=pltpu.CompilerParams(vmem_limit_bytes=50 << 20),
        cost_estimate=pl.CostEstimate(
            flops=50_000_000_000, bytes_accessed=40 << 20, transcendentals=0
        ),
        name="feed_forward",
    )(jnp.reshape(mine, (1,)).astype(jnp.int32), x, cot, cot_came, wo, w1, w2, vec, b1, *context)


def wide_kernel(at_ref, left_ref, right_ref, *refs):
    *came_refs, out_ref, turned_ref = refs
    i = pl.program_id(0)

    @pl.when(i == 0)
    def _():
        turned_ref[...] = left_ref[...].T

    rows = out_ref.shape[0]
    some = pl.ds(pl.multiple_of(lax.rem(i, D // rows) * rows, rows), rows)
    out_ref[...] = add_came(dot(turned_ref[some, :], right_ref[...], NN), came_refs)


def add_came(total, came_refs):
    for ref in came_refs:
        total = total + ref[...].astype(jnp.float32)
    return total.astype(jnp.bfloat16)


def tall_kernel(at_ref, left_ref, right_ref, *refs):
    *came_refs, out_ref = refs
    out_ref[...] = add_came(dot(left_ref[...], right_ref[...], TN), came_refs)


def tall_product(left, right, half, count, tile, came=()):
    tokens, width = right.shape[0], left.shape[1]
    part = width // count
    per = part // tile
    return pl.pallas_call(
        tall_kernel,
        grid_spec=pltpu.PrefetchScalarGridSpec(
            num_scalar_prefetch=1,
            grid=(per,),
            in_specs=[
                pl.BlockSpec((tokens, tile), lambda i, at: (0, at[0] * per + i)),
                pl.BlockSpec((tokens, right.shape[1]), lambda i, at: (0, 0)),
            ]
            + [pl.BlockSpec((tile, right.shape[1]), lambda i, at: (i, 0))] * len(came),
            out_specs=pl.BlockSpec((tile, right.shape[1]), lambda i, at: (i, 0)),
        ),
        out_shape=jax.ShapeDtypeStruct((part, right.shape[1]), jnp.bfloat16),
        compiler_params=pltpu.CompilerParams(vmem_limit_bytes=48 << 20),
        cost_estimate=pl.CostEstimate(
            flops=2 * tokens * part * right.shape[1], bytes_accessed=8 << 20, transcendentals=0
        ),
        name="tall_product",
    )(jnp.reshape(half, (1,)).astype(jnp.int32), left, right, *came)


def wide_product(left, right, half, count, rows, came=()):
    tokens, width = right.shape
    part = width // count
    blocks, per = part // D, D // rows
    return pl.pallas_call(
        wide_kernel,
        grid_spec=pltpu.PrefetchScalarGridSpec(
            num_scalar_prefetch=1,
            grid=(blocks * per,),
            in_specs=[
                pl.BlockSpec((tokens, D), lambda i, at: (0, 0)),
                pl.BlockSpec((tokens, D), lambda i, at: (0, at[0] * blocks + i // per)),
            ]
            + [pl.BlockSpec((rows, D), lambda i, at: (i, 0))] * len(came),
            out_specs=pl.BlockSpec((rows, D), lambda i, at: (i, 0)),
            scratch_shapes=[pltpu.VMEM((D, tokens), jnp.bfloat16)],
        ),
        out_shape=jax.ShapeDtypeStruct((part, D), jnp.bfloat16),
        compiler_params=pltpu.CompilerParams(vmem_limit_bytes=48 << 20),
        cost_estimate=pl.CostEstimate(
            flops=2 * tokens * part * D, bytes_accessed=8 << 20, transcendentals=0
        ),
        name="wide_product",
    )(jnp.reshape(half, (1,)).astype(jnp.int32), left, right, *came)


def heads_kernel(x_ref, d_query_ref, d_key_ref, d_value_ref, out_ref, turned_ref):
    tokens, rows = x_ref.shape[0], turned_ref.shape[0]

    @pl.when(pl.program_id(0) == 0)
    def _():
        turned_ref[:D, :] = x_ref[...].T
        row = lax.broadcasted_iota(jnp.int32, (rows - D, tokens), 0)
        turned_ref[D:, :] = (row == 0).astype(jnp.float32).astype(jnp.bfloat16)

    for i, ref in enumerate((d_query_ref, d_key_ref, d_value_ref)):

        @pl.when(pl.program_id(0) == i)
        def _():
            out_ref[...] = dot(turned_ref[...], ref[...], NN).astype(jnp.bfloat16)


def heads_products(x, d_query, d_key, d_value):
    tokens, cols = d_query.shape
    rows = D + 32
    each = pl.BlockSpec((tokens, cols), lambda i: (0, 0))
    return pl.pallas_call(
        heads_kernel,
        grid=(3,),
        in_specs=[pl.BlockSpec((tokens, D), lambda i: (0, 0)), each, each, each],
        out_specs=pl.BlockSpec((rows, cols), lambda i: (0, i)),
        out_shape=jax.ShapeDtypeStruct((rows, 3 * cols), jnp.bfloat16),
        scratch_shapes=[pltpu.VMEM((rows, tokens), jnp.bfloat16)],
        compiler_params=pltpu.CompilerParams(vmem_limit_bytes=62 << 20),
        cost_estimate=pl.CostEstimate(
            flops=6 * tokens * rows * cols, bytes_accessed=8 << 20, transcendentals=0
        ),
        name="heads_products",
    )(x, d_query, d_key, d_value)


def inputs_kernel(at_ref, d_query_ref, d_key_ref, d_value_ref, wq_ref, wk_ref, wv_ref, *out_refs):
    total = dot(d_query_ref[...], wq_ref[...], NT)
    total = total + dot(d_key_ref[...], wk_ref[...], NT)
    total = (total + dot(d_value_ref[...], wv_ref[...], NT)).astype(jnp.bfloat16)
    per = pl.num_programs(0) // len(out_refs)
    for k, ref in enumerate(out_refs):

        @pl.when(pl.program_id(0) // per == k)
        def _():
            ref[...] = total


def inputs_products(grads, weights, at, count):
    tokens, cols = grads[0].shape
    tile = 512
    per = tokens // count // tile
    part = pl.BlockSpec((tile, cols), lambda i, at: (i, 0))
    weight = pl.BlockSpec((D, cols), lambda i, at: (0, at[0]), pipeline_mode=pl.Buffered(1))

    def place(k):
        return pl.BlockSpec((tile, D), lambda i, at: (jnp.clip(i - k * per, 0, per - 1), 0))

    return pl.pallas_call(
        inputs_kernel,
        grid_spec=pltpu.PrefetchScalarGridSpec(
            num_scalar_prefetch=1,
            grid=(count * per,),
            in_specs=[part] * 3 + [weight] * 3,
            out_specs=[place(k) for k in range(count)],
        ),
        out_shape=[jax.ShapeDtypeStruct((tokens // count, D), jnp.bfloat16)] * count,
        compiler_params=pltpu.CompilerParams(vmem_limit_bytes=60 << 20),
        cost_estimate=pl.CostEstimate(
            flops=24_000_000_000, bytes_accessed=8 << 20, transcendentals=0
        ),
        name="inputs_products",
    )(jnp.reshape(at, (1,)).astype(jnp.int32), *grads, *weights)


def spread_heads_kernel(at_ref, pool_ref, *refs):
    cols = refs[-1].shape[1]
    for i, ref in enumerate(refs[-3:]):
        ref[...] = pool_ref[:, i * cols : (i + 1) * cols].astype(jnp.float32)


def spread_columns(pool, half, held):
    cols = pool.shape[1] // 3
    return spread_call(
        spread_heads_kernel,
        "spread_columns",
        half,
        (1,),
        (pool,),
        [pl.BlockSpec((D, 3 * cols), lambda i, at: (0, 0))],
        [(D, D)] * 3,
        [pl.BlockSpec((D, cols), lambda i, at: (0, at[0]))] * 3,
        held,
    )


OUT_STEPS = 3


def spread_outer_kernel(at_ref, first_ref, second_ref, *refs):
    i, blocks = pl.program_id(0), pl.num_programs(0)

    @pl.when(i < blocks - 1)
    def _():
        refs[-1][...] = first_ref[...].astype(jnp.float32)

    @pl.when(i == blocks - 1)
    def _():
        refs[-1][...] = second_ref[...].astype(jnp.float32)


def spread_inner_kernel(at_ref, first_ref, second_ref, third_ref, *refs):
    inner_ref, out_ref = refs[-2:]
    i, blocks = pl.program_id(0), pl.num_programs(0) - OUT_STEPS

    @pl.when(i < blocks - 1)
    def _():
        inner_ref[...] = first_ref[...].astype(jnp.float32)

    @pl.when(i == blocks - 1)
    def _():
        inner_ref[...] = second_ref[...].astype(jnp.float32)

    @pl.when(i >= blocks)
    def _():
        out_ref[...] = third_ref[...].astype(jnp.float32)


def spread_call(kernel, name, half, grid, operands, specs, out_shapes, out_specs, held):
    return pl.pallas_call(
        kernel,
        grid_spec=pltpu.PrefetchScalarGridSpec(
            num_scalar_prefetch=1,
            grid=grid,
            in_specs=specs + [pl.BlockSpec(memory_space=pl.ANY)] * len(held),
            out_specs=out_specs,
        ),
        out_shape=[jax.ShapeDtypeStruct(s, jnp.float32) for s in out_shapes],
        input_output_aliases={1 + len(operands) + i: i for i in range(len(held))},
        compiler_params=pltpu.CompilerParams(vmem_limit_bytes=32 << 20),
        cost_estimate=SHORT,
        name=name,
    )(jnp.reshape(half, (1,)).astype(jnp.int32), *operands, *held)


def spread_outer(first, second, half, held):
    rows = second.shape[0]
    blocks = first.shape[0] // rows + 1
    return spread_call(
        spread_outer_kernel,
        "spread_outer",
        half,
        (blocks,),
        (first, second),
        [
            pl.BlockSpec((rows, D), lambda i, at: (jnp.minimum(i, blocks - 2), 0)),
            pl.BlockSpec((rows, D), lambda i, at: (0, 0)),
        ],
        [(2 * rows * blocks, D)],
        [pl.BlockSpec((rows, D), lambda i, at: (at[0] * blocks + i, 0))],
        held,
    )


def spread_inner(first, mixed, half, held):
    rows = 256
    per = D // rows
    blocks = first.shape[0] // rows + 1
    wide = blocks // per
    out_rows = D // 2 // OUT_STEPS
    skip = rows // out_rows

    def inner_at(i, at):
        j = jnp.minimum(i, blocks - 1)
        return (j % per, at[0] * wide + j // per)

    return spread_call(
        spread_inner_kernel,
        "spread_inner",
        half,
        (blocks + OUT_STEPS,),
        (first, mixed, mixed),
        [
            pl.BlockSpec((rows, D), lambda i, at: (jnp.minimum(i, blocks - 2), 0)),
            pl.BlockSpec((rows, D), lambda i, at: (0, 0)),
            pl.BlockSpec((out_rows, D), lambda i, at: (skip + jnp.maximum(i - blocks, 0), 0)),
        ],
        [(D, 2 * wide * D), (D, D)],
        [
            pl.BlockSpec((rows, D), inner_at),
            pl.BlockSpec(
                (out_rows, D), lambda i, at: (at[0] * OUT_STEPS + jnp.maximum(i - blocks, 0), 0)
            ),
        ],
        held,
    )


class Ring:
    def __init__(self, axis, size, at, perm):
        self.axis, self.size, self.at, self.perm = axis, size, at, perm

    def send(self, value, by):
        return lax.ppermute(value, self.axis, self.perm(by))


class Pairs:
    def __init__(self, seq, rows, masks, core):
        me = lax.axis_index("seq") * rows + lax.axis_index("rows")
        bits = [lax.rem(me // mask, 2) for mask in masks]
        self.bit = jnp.where(lax.rem(me // core, 2) == 0, bits[0], bits[1])
        self.perm = [(i, i ^ masks[i // core % 2]) for i in range(seq * rows)]

    def swap(self, value):
        return lax.ppermute(value, ("seq", "rows"), self.perm)

    def keep(self, value):
        part = value.shape[0] // 2
        return lax.dynamic_slice_in_dim(value, self.bit * part, part, 0)

    def give(self, value):
        part = value.shape[0] // 2
        return lax.dynamic_slice_in_dim(value, (1 - self.bit) * part, part, 0)

    def halved(self, value, came):
        return (self.keep(value).astype(jnp.float32) + came.astype(jnp.float32)).astype(value.dtype)

    def halve(self, value):
        return self.halved(value, self.swap(self.give(value)))

    def joined(self, value, came):
        first = jnp.where(self.bit == 0, value, came)
        second = jnp.where(self.bit == 0, came, value)
        return jnp.concatenate([first, second], 0)

    def join(self, value):
        return self.joined(value, self.swap(value))


def powers(step, count):
    masks = []
    while count > 1:
        masks.append(step)
        step, count = step * 2, count // 2
    return masks


def make_links(seq, rows):
    half = seq // 2
    deep = CHIPS_Z if rows % CHIPS_Z == 0 else 1
    wide = rows // deep
    s = lax.axis_index("seq")
    near = Ring(
        "seq",
        half,
        lax.rem(s, half),
        lambda by: [(i, i // half * half + (i + by) % half) for i in range(seq)],
    )

    def pairs(first, second=None):
        return Pairs(seq, rows, (first, second or first), rows)

    far_mask = half * rows
    y, z = powers(1, wide), powers(wide, deep)
    far = pairs(far_mask)
    inside = [pairs(mask) for mask in powers(rows, half)]
    main = [pairs(far_mask, y[0]), pairs(y[0], z[0]), pairs(z[0], far_mask)]
    side = [pairs(z[0]), pairs(far_mask), pairs(y[0])]
    last = [pairs(mask) for mask in y[1:] + z[1:]]
    return near, far, inside, [main, side], last


def in_step(values):
    return list(lax.optimization_barrier(tuple(values)))


def cut(value, sizes):
    out, at = [], 0
    for size in sizes:
        out.append(value[at : at + size])
        at += size
    return out


class HalveStep:
    def __init__(self, pairs):
        self.pairs = pairs

    def start(self, parts):
        return [pair.swap(pair.give(part)) for pair, part in zip(self.pairs, parts)]

    def finish(self, parts, came):
        return [pair.halved(*both) for pair, *both in zip(self.pairs, parts, came)]


class JoinStep:
    def __init__(self, pairs):
        self.pairs = pairs

    def start(self, parts):
        return [pair.swap(part) for pair, part in zip(self.pairs, parts)]

    def finish(self, parts, came):
        return [pair.joined(*both) for pair, *both in zip(self.pairs, parts, came)]


class SumStep:
    def __init__(self, pair):
        self.pair = pair

    def start(self, parts):
        return cut(self.pair.swap(jnp.concatenate(parts, 0)), [p.shape[0] for p in parts])

    def finish(self, parts, came):
        return [
            (p.astype(jnp.float32) + c.astype(jnp.float32)).astype(p.dtype)
            for p, c in zip(parts, came)
        ]


class Chain:
    def __init__(self, parts, steps):
        self.parts, self.steps, self.came = list(parts), list(steps), None

    def start(self):
        self.came = self.steps[0].start(self.parts)

    def finish(self, *after):
        came = in_step(list(self.came) + list(after))[: len(self.came)]
        self.parts = self.steps.pop(0).finish(self.parts, came)
        self.came = None

    def step(self, *after):
        if self.came is None:
            self.start()
        self.finish(*after)
        if self.steps:
            self.start()


def column_sum(values):
    return jnp.sum(values.astype(jnp.float32), 0)


def per_device(
    seq,
    rows,
    inputs,
    query_weight,
    query_bias,
    key_weight,
    value_weight,
    value_bias,
    output_weight,
    output_bias,
    first_gain,
    first_shift,
    inner_weight,
    inner_bias,
    outer_weight,
    outer_bias,
    second_gain,
    second_shift,
    doc_tokens,
    random_blocks,
    cotangent,
):
    low, full = jnp.bfloat16, jnp.float32
    near, far, inside, routes, last = make_links(seq, rows)
    main, side = routes
    half = seq // 2
    width = inputs.shape[1]
    tokens = 2 * width
    nb = random_blocks.shape[1]
    heads = HEADS // half
    cols = heads * HEAD
    mine, at = far.bit, near.at

    def own_and_other(array):
        own = lax.dynamic_index_in_dim(array, mine, 0, False)
        return own, lax.dynamic_index_in_dim(array, 1 - mine, 0, False)

    def from_rows(own, other):
        return jnp.where(mine == 0, jnp.stack([own, other]), jnp.stack([other, own]))

    def by_device(values):
        stacked = jnp.stack(values)
        order = lax.rem(at + half - jnp.arange(half), half)
        return jnp.take(stacked, order, axis=0) if half > 2 else jnp.where(at == 0, stacked, stacked[::-1])

    def by_two(values):
        return [values[i : i + 2] for i in range(0, len(values), 2)]

    x_own, x_other = own_and_other(inputs)
    x_came = far.swap(x_other)

    shards = []
    for k in range(half):
        own = mine * half + lax.rem(at + k, half)
        shards += [own, lax.rem(own + half, seq)]
    per_shard = width // BLOCK
    block_of_slot = (
        jnp.stack(shards)[:, None] * per_shard + jnp.arange(per_shard, dtype=jnp.int32)
    ).reshape(-1).astype(jnp.int32)
    doc = lax.dynamic_index_in_dim(doc_tokens, mine, 0, False)
    chosen = lax.dynamic_index_in_dim(random_blocks, mine, 0, False)
    tables = block_tables(block_of_slot, doc, chosen)

    def my_cols(weight):
        return lax.dynamic_slice_in_dim(weight, at * cols, cols, weight.ndim - 1)

    weights = (query_weight, key_weight, value_weight)
    w_qkv = jnp.concatenate([my_cols(w) for w in weights], 1)
    b_qkv = jnp.concatenate(
        [my_cols(query_bias), jnp.zeros((cols,), low), my_cols(value_bias)]
    ).astype(full)
    wo = jnp.concatenate(
        [
            lax.dynamic_slice_in_dim(
                output_weight, lax.rem(at + half - k, half) * cols, cols, 0
            )
            for k in range(half)
        ],
        0,
    )
    vec = jnp.stack(
        [output_bias, first_gain, first_shift, outer_bias, second_gain, second_shift]
    ).astype(full)
    vec = jnp.pad(vec, ((0, 2), (0, 0)))
    b1 = jnp.broadcast_to(inner_bias.astype(full), (8, inner_bias.shape[0]))

    x_came, cotangent, w_qkv, b_qkv, wo, vec, b1, *tables = in_step(
        [x_came, cotangent, w_qkv, b_qkv, wo, vec, b1, *tables]
    )
    cot_came = far.swap(lax.dynamic_index_in_dim(cotangent, 1 - mine, 0, False))
    x_parts = [x_own, x_came]
    for k in range(1, half):
        x_parts += [near.send(x_own, half - k), near.send(x_came, half - k)]
    x_all = jnp.concatenate(x_parts, 0)
    qkv = (dot(x_all, w_qkv, NN) + b_qkv).astype(low)
    heads_context, lse = attend(qkv, tables, heads, nb)
    heads_context, lse, cot_came = in_step([heads_context, lse, cot_came])
    context = [heads_context] + [
        near.send(heads_context[k * tokens : (k + 1) * tokens], k) for k in range(1, half)
    ]
    values = feed_forward(
        mine, x_all, cotangent, cot_came, context, wo, inner_weight, outer_weight, vec, b1
    )
    result, result_half, values = values[0], list(values[1:3]), values[3:]
    first_low, active, d_inner, d_outer, d_attended, d_resid, sums, inner_sum, *d_context = values
    heads_grad = [d_context[0]] + [near.send(d_context[k], half - k) for k in range(1, half)]

    packed = jnp.concatenate([sums[:6].reshape(-1), inner_sum[0]]).reshape(-1, D)
    packed = jnp.pad(packed, ((0, 128 - packed.shape[0]), (0, 0))).astype(low)

    def outer_product(part, k, came=()):
        return tall_product(active, d_outer, part, half, 768, came)

    def inner_product(part, k, came=()):
        return wide_product(first_low, d_inner, part, half, 768, came)

    def out_product(part, k, came=()):
        k = (half - k) % half
        if cols % 128:
            total = dot(context[k][:tokens], d_attended, TN)
            return sum([c.astype(full) for c in came], total).astype(low)
        return tall_product(context[k], d_attended, 0, 1, cols, came)

    def packed_part(part, k, came=()):
        size = 128 // half
        total = lax.dynamic_slice_in_dim(packed, part * size, size, 0).astype(full)
        return sum([c.astype(full) for c in came], total).astype(low)

    def give(product):
        return [product(lax.rem(at + k, half), k) for k in range(1, half)]

    def send(parts):
        return [near.send(part, k) for k, part in enumerate(parts, 1)]

    outer_give = give(outer_product)
    outer_give[0], first_low, d_attended = in_step([outer_give[0], first_low, d_attended])
    outer_came = send(outer_give)
    inner_came = send(give(inner_product))
    out_came = send(give(out_product))
    packed_came = send(give(packed_part))
    outer_grad = outer_product(at, 0, outer_came)
    outer_main = outer_grad.shape[0] * 3 // 4
    early = Chain([outer_grad[:outer_main], outer_grad[outer_main:]], [HalveStep([main[0], side[0]])])
    early.start()
    inner_came[0], out_came[0], packed_came[0], *early.parts = in_step(
        [inner_came[0], out_came[0], packed_came[0]] + early.parts
    )
    inner_grad = inner_product(at, 0, inner_came)
    out_grad = out_product(at, 0, out_came)
    packed = packed_part(at, 0, packed_came)
    inner_grad, out_grad, packed, *early.came = in_step(
        [inner_grad, out_grad, packed] + early.came
    )
    early.finish()
    inner_main = inner_grad.shape[0] * 5 // 6
    mixed = jnp.concatenate([inner_grad[inner_main:], out_grad, packed], 0)
    rest = Chain([inner_grad[:inner_main], mixed], [HalveStep([main[0], side[0]])])
    heads_grad[0], *rest.parts = in_step([heads_grad[0]] + early.parts + rest.parts)
    early.parts, rest.parts = rest.parts[:2], rest.parts[2:]

    first_sizes = [
        (outer_main // 2, inner_main // 2),
        ((outer_grad.shape[0] - outer_main) // 2, mixed.shape[0] // 2),
    ]
    first = Chain([], [HalveStep([main[i], side[i]]) for i in (1, 2)])
    first.steps += [SumStep(pair) for pair in last]
    first.steps += [JoinStep([main[i], side[i]]) for i in (2, 1)]

    steps = cols // 128 if cols % 128 == 0 else 1
    d_qkv = ()
    result_came = []
    for k in range(steps):
        chain = first if first.parts else rest
        chain.start()
        if k == 2:
            result_half[0], d_query = in_step([result_half[0], d_qkv[0]])
            d_qkv = (d_query,) + d_qkv[1:]
            result_came.append(far.swap(result_half[0]))
        d_qkv = attend_back(
            qkv, heads_grad, heads_context, lse, tables, heads // steps, nb, d_qkv, k
        )
        d_query, d_key, d_value, *came = in_step(list(d_qkv) + chain.came + result_came)
        d_qkv = (d_query, d_key, d_value)
        chain.came, result_came = came[: len(chain.came)], came[len(chain.came) :]
        chain.finish()
        if chain is rest:
            first.parts = [
                jnp.concatenate([e, r], 0) for e, r in zip(early.parts, rest.parts)
            ]
        d_query, *first.parts = in_step([d_query] + first.parts)
        d_qkv = (d_query, d_key, d_value)

    while len(first.steps) > 3:
        first.start()
        first.finish()
    sums_at_last = first.steps.pop(0)
    some = first.parts[0].shape[0] // 4 // 8 * 8
    main_parts = [first.parts[0][:some], first.parts[0][some:]]
    last_came = sums_at_last.start([main_parts[0], first.parts[1]])
    result_half[1:], d_query = in_step([*result_half[1:], d_query])[:-1], d_query
    result_came += [far.swap(piece) for piece in result_half[len(result_came) :]]
    if cols % 128 == 0:
        heads_part = heads_products(x_all, *d_qkv)
    else:
        sums_of = [jnp.pad(column_sum(d)[None, :], ((0, 31), (0, 0))) for d in d_qkv]
        heads_part = [
            jnp.concatenate([dot(x_all, d, TN), total], 0) for d, total in zip(d_qkv, sums_of)
        ]
        heads_part = jnp.concatenate(heads_part, 1).astype(low)
    heads_part, d_query, d_key, d_value, *came = in_step(
        [heads_part, d_query, d_key, d_value] + last_came + result_came
    )
    last_came, result_came = came[:2], came[2:]
    main_parts[1], heads_part = in_step([main_parts[1], heads_part])

    second = Chain([heads_part], [HalveStep([main[i]]) for i in range(3)])
    second.steps += [SumStep(pair) for pair in last]
    second.steps += [JoinStep([main[i]]) for i in (2, 1, 0)]
    second.start()
    last_came += sums_at_last.start(main_parts[1:])
    if cols % 128 == 0:
        d_parts = list(inputs_products((d_query, d_key, d_value), weights, at, half))
    else:
        parts = zip((d_query, d_key, d_value), (my_cols(w) for w in weights))
        d_parts = sum(dot(d, w, NT) for d, w in parts).astype(low)
        d_parts = cut(d_parts, [tokens] * half)
    d_parts[0], *came = in_step([d_parts[0]] + last_came + second.came)
    second.came = came[3:]
    sums = sums_at_last.finish([main_parts[0], first.parts[1], main_parts[1]], came[:3])
    first.parts = [jnp.concatenate([sums[0], sums[2]], 0), sums[1]]
    second.finish()

    def together(*beside):
        count = len(first.came or ())
        values = in_step(list(first.came or ()) + second.came + list(beside))
        if count:
            first.came = values[:count]
            first.finish()
        second.came = values[count : count + len(second.came)]
        second.finish()
        return values[len(values) - len(beside) :]

    second.start()
    first.start()
    d_came = [near.send(d_parts[k], k) for k in range(1, half)]
    d_came = together(*d_came)
    second.start()
    first.start()
    d_input = d_resid + d_parts[0].astype(full)
    for value in d_came:
        d_input = d_input + value.astype(full)
    d_input = d_input.astype(low)
    result = from_rows(result, jnp.concatenate(result_came, 0))
    d_input, result = together(d_input, result)
    for _ in last[:-1]:
        second.step()
    second.start()
    pieces = [p for share, size in zip(first.parts, first_sizes) for p in cut(share, size)]
    outer = Chain([pieces[0], pieces[2]], [JoinStep([main[0], side[0]])])
    inner = Chain([pieces[1], pieces[3]], [JoinStep([main[0], side[0]])])
    outer.start()
    d_input_came = [far.swap(d_input[width : width + width // 2])]
    values = together(*outer.came, *inner.parts, *d_input_came)
    outer.came, inner.parts, d_input_came = values[:2], values[2:4], values[4:]
    outer.finish()
    second.start()
    inner.start()
    outer_came = [near.send(part, k) for k in range(1, half) for part in outer.parts]
    placed = spread_outer(*outer.parts, at, ()) if half == 2 else outer.parts
    count = 2 + len(outer_came)
    values = together(*inner.came, *outer_came, d_input, *placed)
    inner.came, outer_came, d_input = values[:2], values[2:count], values[count]
    outer.parts = values[count + 1 :]
    inner.finish()
    second.start()
    inner_came = [near.send(part, k) for k in range(1, half) for part in inner.parts]
    d_input_came.append(far.swap(d_input[width + width // 2 :]))
    if half == 2:
        outer.parts = list(spread_outer(*outer_came, 1 - at, outer.parts))
    count = len(inner_came)
    values = together(*inner_came, *d_input_came, *outer.parts)
    inner_came, d_input_came, outer.parts = (
        values[:count],
        values[count : count + 2],
        values[count + 2 :],
    )
    second.start()
    d_input = from_rows(d_input[:width], jnp.concatenate(d_input_came, 0))
    small = inner_grad.shape[0] - inner_main, out_grad.shape[0], packed.shape[0]
    inner_b, out_grad, packed = cut(inner.parts[1], small)
    packed = [packed] + [cut(p, small)[2] for p in inner_came[1::2]]
    packed = by_device(packed).reshape(-1, D).astype(full)
    if half == 2:
        (outer_grad,) = outer.parts
        placed = spread_inner(*inner.parts, at, ())
        inner_grad, out_grad = spread_inner(*inner_came, 1 - at, placed)
    else:
        outer_grad = [jnp.concatenate(p, 0) for p in [outer.parts] + by_two(outer_came)]
        outer_grad = by_device(outer_grad).reshape(-1, D).astype(full)
        inner_grad = [jnp.concatenate([inner.parts[0], inner_b], 0)]
        out_grad = [out_grad]
        for first_part, other in by_two(inner_came):
            inner_grad.append(jnp.concatenate([first_part, cut(other, small)[0]], 0))
            out_grad.append(cut(other, small)[1])
        inner_grad = by_device(inner_grad).reshape(-1, D, D).astype(full)
        inner_grad = inner_grad.transpose(1, 0, 2).reshape(D, -1)
        out_grad = by_device(out_grad).reshape(-1, D).astype(full)
    small_grads = [packed[i] for i in range(6)] + [packed[6:10].reshape(-1)]
    d_input, inner_grad, out_grad, outer_grad, *small_grads = together(
        d_input, inner_grad, out_grad, outer_grad, *small_grads
    )
    heads_parts = second.parts[0]
    if half == 2:
        heads_came = near.send(heads_parts, 1)
        query_grad, key_grad, value_grad = spread_columns(
            heads_came, 1 - at, spread_columns(heads_parts, at, ())
        )
        biases = [p[D].astype(full) for p in (heads_parts, heads_came)]
        biases = jnp.where(at == 0, jnp.stack(biases), jnp.stack(biases[::-1]))
        query_bias_grad = biases[:, :cols].reshape(-1)
        value_bias_grad = biases[:, 2 * cols :].reshape(-1)
    else:
        heads_parts = by_device([heads_parts] + [near.send(heads_parts, k) for k in range(1, half)])
        query_grad, key_grad, value_grad = (
            jnp.concatenate([p[:, i * cols : (i + 1) * cols] for p in heads_parts], 1).astype(full)
            for i in range(3)
        )
        query_bias_grad, value_bias_grad = query_grad[D], value_grad[D]
        query_grad, key_grad, value_grad = query_grad[:D], key_grad[:D], value_grad[:D]
    return (
        result,
        d_input,
        query_grad,
        query_bias_grad,
        key_grad,
        value_grad,
        value_bias_grad,
        out_grad,
        *small_grads[:3],
        inner_grad,
        small_grads[6],
        outer_grad,
        *small_grads[3:6],
    )


def solution(mesh):
    tokens = P("rows", "seq", None)
    in_specs = (tokens,) + (P(),) * 15 + (P("rows"), P("rows", None, None), tokens)
    out_specs = (tokens, tokens) + (P(),) * 15
    return jax.shard_map(
        partial(per_device, mesh.shape["seq"], mesh.shape["rows"]),
        mesh=mesh,
        in_specs=in_specs,
        out_specs=out_specs,
        check_vma=False,
    )
```

```python
import functools
from functools import partial

import jax
import jax.numpy as jnp
from jax import lax
from jax.experimental import pallas as pl
from jax.experimental.pallas import tpu as pltpu
from jax.sharding import PartitionSpec as P

D = 768
HEADS = 12
HEAD = 64
BLOCK = 64
SETS = 8
CHIPS_Z = 4

EPSILON = 1e-05
NEG_FILL = -1e30

SHORT = pl.CostEstimate(flops=1 << 20, bytes_accessed=1 << 10, transcendentals=0)

NT = (((1,), (1,)), ((), ()))
NN = (((1,), (0,)), ((), ()))
TN = (((0,), (0,)), ((), ()))


def dot(left, right, dims):
    return lax.dot_general(left, right, dims, preferred_element_type=jnp.float32)


def head_groups(heads):
    groups, at = [], 0
    while at < heads:
        n = 2 if heads - at >= 2 else 1
        groups.append((at, n))
        at += n
    return groups


def lanes_of(at, n):
    return slice(at * HEAD, (at + n) * HEAD)


def diagonal(n, rows):
    row = lax.broadcasted_iota(jnp.int32, (n * rows, n * HEAD), 0) // rows
    lane = lax.broadcasted_iota(jnp.int32, (n * rows, n * HEAD), 1) // HEAD
    return (row == lane).astype(jnp.float32)


def spread_heads(block, diag, n):
    if n == 1:
        return block
    return jnp.concatenate([block] * n, 0) * diag.astype(block.dtype)


def fold_heads(full, diag, n):
    if n == 1:
        return full
    rows = full.shape[0] // n
    kept = full * diag
    out = kept[:rows]
    for h in range(1, n):
        out = out + kept[h * rows : (h + 1) * rows]
    return out


def rows_of(slot):
    return pl.ds(pl.multiple_of(slot * BLOCK, BLOCK), BLOCK)


def gather_rows(ref, slots, lanes):
    return jnp.concatenate([ref[rows_of(s), lanes] for s in slots], 0)


def as_row(column):
    n = column.shape[0]
    same = lax.broadcasted_iota(jnp.int32, (n, n), 0) == lax.broadcasted_iota(jnp.int32, (n, n), 1)
    return jnp.sum(jnp.where(same, column, 0.0), 0, keepdims=True)


def attend_kernel(
    heads,
    nb,
    abreast,
    key_at_ref,
    query_at_ref,
    q_ref,
    k_ref,
    v_ref,
    task_bias_ref,
    lead_bias_ref,
    o_ref,
    lse_ref,
):
    groups = head_groups(heads)
    scale = jnp.bfloat16(HEAD**-0.5)
    diags = {n: diagonal(n, BLOCK) for _, n in groups}

    def local(i, carry):
        work, scores, probs = [], [], []
        for u in range(abreast):
            t = abreast * i + u
            ks = [key_at_ref[t, b] for b in range(SETS)]
            work += [(t, ks, query_at_ref[t], lanes_of(at, n), n) for at, n in groups]
        for t, ks, qs, lanes, n in work:
            query = spread_heads(q_ref[rows_of(qs), lanes] * scale, diags[n], n)
            score = dot(query, gather_rows(k_ref, ks, lanes), NT)
            scores.append(score + task_bias_ref[pl.ds(t, 1), :])
        for score in scores:
            top = jnp.max(score, 1, keepdims=True)
            prob = jnp.exp(score - top)
            probs.append((prob.astype(jnp.bfloat16), top, jnp.sum(prob, 1, keepdims=True)))
        for (t, ks, qs, lanes, n), (prob, top, total) in zip(work, probs):
            out = dot(prob, gather_rows(v_ref, ks, lanes), NN) * (1.0 / total)
            out = fold_heads(out, diags[n], n)
            o_ref[rows_of(qs), lanes] = out.astype(jnp.bfloat16)
            lse_ref[qs, :, lanes] = as_row(top + jnp.log(total))
        return carry

    lax.fori_loop(0, (nb - 2) // abreast, local, 0)

    rows = 2 * BLOCK
    qs = query_at_ref[nb - 2]
    lead_rows = pl.ds(pl.multiple_of(qs * BLOCK, BLOCK), rows)
    scores, probs = [], []
    for at, n in groups:
        lanes = lanes_of(at, n)
        query = spread_heads(q_ref[lead_rows, lanes] * scale, diagonal(n, rows), n)
        scores.append(dot(query, k_ref[:, lanes], NT) + lead_bias_ref[...])
    for score in scores:
        top = jnp.max(score, 1, keepdims=True)
        prob = jnp.exp(score - top)
        probs.append((prob.astype(jnp.bfloat16), top, jnp.sum(prob, 1, keepdims=True)))
    for (at, n), (prob, top, total) in zip(groups, probs):
        lanes = lanes_of(at, n)
        out = dot(prob, v_ref[:, lanes], NN) * (1.0 / total)
        o_ref[lead_rows, lanes] = fold_heads(out, diagonal(n, rows), n).astype(jnp.bfloat16)
        lse = top + jnp.log(total)
        each = [as_row(lse[h * rows : (h + 1) * rows]) for h in range(n)]
        for b in range(2):
            part = slice(b * BLOCK, (b + 1) * BLOCK)
            lse_ref[qs + b, :, lanes] = jnp.concatenate([row[:, part] for row in each], 1)


def attend_back_kernel(
    heads,
    nb,
    abreast,
    pieces,
    key_at_ref,
    bias_at_ref,
    query_at_ref,
    places_ref,
    q_ref,
    k_ref,
    v_ref,
    o_ref,
    lse_ref,
    *rest,
):
    dq_ref, dk_ref, dv_ref, dk_acc, dv_acc, delta_ref, g_ref, bias_ref = rest[-8:]
    rows = nb * BLOCK // pieces
    for i in range(pieces):
        g_ref[i * rows : (i + 1) * rows, :] = rest[i][...]
    groups = head_groups(heads)
    diags = {n: diagonal(n, BLOCK) for _, n in groups}
    inside = lax.broadcasted_iota(jnp.int32, (BLOCK, 2 * HEAD), 0)
    for s in range(nb):
        valid = places_ref[s] * BLOCK + inside < places_ref[nb]
        bias_ref[s * BLOCK : (s + 1) * BLOCK, :] = jnp.where(valid, 0.0, NEG_FILL)
    every = nb * BLOCK
    bias_ref[every:, :] = jnp.full_like(bias_ref[every:, :], NEG_FILL)
    dk_acc[every:, :] = jnp.zeros_like(dk_acc[every:, :])
    dv_acc[every:, :] = jnp.zeros_like(dv_acc[every:, :])
    scale = HEAD**-0.5

    for at, n in groups:
        lanes = lanes_of(at, n)
        row = lax.broadcasted_iota(jnp.int32, (16, n * HEAD), 0)
        pick = row == lax.broadcasted_iota(jnp.int32, (16, n * HEAD), 1) // HEAD
        pick = pick.astype(jnp.float32).astype(jnp.bfloat16)
        for s in range(0, nb, 4):
            some = slice(s * BLOCK, (s + 4) * BLOCK)
            both = g_ref[some, lanes].astype(jnp.float32) * o_ref[some, lanes].astype(jnp.float32)
            high = both.astype(jnp.bfloat16)
            less = (both - high.astype(jnp.float32)).astype(jnp.bfloat16)
            delta = dot(pick, high, NT) + dot(pick, less, NT)
            for j in range(4):
                part = slice(j * BLOCK, (j + 1) * BLOCK)
                delta_ref[s + j, :, lanes] = jnp.concatenate(
                    [delta[h : h + 1, part] for h in range(n)], 1
                )

    both_rows = 2 * BLOCK
    lead = query_at_ref[nb - 2]
    lead_rows = pl.ds(pl.multiple_of(lead * BLOCK, BLOCK), both_rows)

    def lead_row(ref, lanes, n):
        first, second = ref[lead, :, lanes], ref[lead + 1, :, lanes]
        heads_of = [slice(h * HEAD, (h + 1) * HEAD) for h in range(n)]
        return jnp.concatenate([r[:, h] for h in heads_of for r in (first, second)], 1)

    for at, n in groups:
        lanes, diag = lanes_of(at, n), diagonal(n, both_rows)
        query = spread_heads(q_ref[lead_rows, lanes] * jnp.bfloat16(scale), diag, n)
        grad = spread_heads(g_ref[lead_rows, lanes], diag, n)
        score = dot(k_ref[:, lanes], query, NT)
        bias = jnp.concatenate([bias_ref[:every, :]] * n, 1)
        prob = jnp.exp(score + bias - lead_row(lse_ref, lanes, n))
        d_prob = dot(v_ref[:, lanes], grad, NT)
        d_score = (prob * (d_prob - lead_row(delta_ref, lanes, n))).astype(jnp.bfloat16)
        dv_acc[:every, lanes] = dot(prob.astype(jnp.bfloat16), grad, NN)
        dk_acc[:every, lanes] = dot(d_score, query, NN)
        d_query = fold_heads(dot(d_score, k_ref[:, lanes], TN), diag, n) * scale
        dq_ref[lead_rows, lanes] = d_query.astype(jnp.bfloat16)

    def several(i, carry):
        work, scores, probs, grads = [], [], [], []
        for u in range(abreast):
            t = abreast * i + u
            ks = [key_at_ref[t, b] for b in range(SETS)]
            bs = [bias_at_ref[t, b] for b in range(SETS)]
            work += [(ks, bs, query_at_ref[t], lanes_of(at, n), n) for at, n in groups]
        for ks, bs, qs, lanes, n in work:
            diag = diags[n]
            query = spread_heads(q_ref[rows_of(qs), lanes] * jnp.bfloat16(scale), diag, n)
            grad = spread_heads(g_ref[rows_of(qs), lanes], diag, n)
            keys = gather_rows(k_ref, ks, lanes)
            score = dot(keys, query, NT)
            d_prob = dot(gather_rows(v_ref, ks, lanes), grad, NT)
            scores.append((query, grad, keys, score, d_prob))
        for (ks, bs, qs, lanes, n), (query, grad, keys, score, d_prob) in zip(work, scores):
            bias = gather_rows(bias_ref, bs, slice(None))[:, : n * HEAD]
            prob = jnp.exp(score + bias - lse_ref[qs, :, lanes])
            d_score = (prob * (d_prob - delta_ref[qs, :, lanes])).astype(jnp.bfloat16)
            probs.append((prob.astype(jnp.bfloat16), d_score))
        for (query, grad, keys, _, _), (prob, d_score) in zip(scores, probs):
            grads.append((dot(prob, grad, NN), dot(d_score, query, NN), dot(d_score, keys, TN)))
        for (ks, bs, qs, lanes, n), (d_value, d_key, d_query) in zip(work, grads):
            before = [(dk_acc[rows_of(a), lanes], dv_acc[rows_of(a), lanes]) for a in bs]
            for j, a in enumerate(bs):
                part = slice(j * BLOCK, (j + 1) * BLOCK)
                dk_acc[rows_of(a), lanes] = before[j][0] + d_key[part]
                dv_acc[rows_of(a), lanes] = before[j][1] + d_value[part]
            d_query = fold_heads(d_query, diags[n], n) * scale
            dq_ref[rows_of(qs), lanes] = d_query.astype(jnp.bfloat16)
        return carry

    lax.fori_loop(0, (nb - 2) // abreast, several, 0)
    dk_ref[...] = dk_acc[: nb * BLOCK].astype(jnp.bfloat16)
    dv_ref[...] = dv_acc[: nb * BLOCK].astype(jnp.bfloat16)


VMEM = pl.BlockSpec(memory_space=pltpu.VMEM)
SMEM = pl.BlockSpec(memory_space=pltpu.SMEM)


def columns(array, at, width):
    if array.shape[1] == width or width % 128 == 0:
        return array, pl.BlockSpec((array.shape[0], width), lambda i: (0, at))
    array = array[:, at * width : (at + 1) * width]
    return array, pl.BlockSpec(array.shape, lambda i: (0, 0))


def attend(qkv, tables, heads, nb):
    key_at, _, query_at, _, task_bias, lead_bias = tables
    width = heads * HEAD
    operands, specs = zip(*[columns(qkv, i, width) for i in range(3)])
    return pl.pallas_call(
        partial(attend_kernel, heads, nb, 2),
        grid=(1,),
        out_shape=(
            jax.ShapeDtypeStruct((nb * BLOCK, width), jnp.bfloat16),
            jax.ShapeDtypeStruct((nb, 1, width), jnp.float32),
        ),
        in_specs=[SMEM] * 2 + list(specs) + [VMEM] * 2,
        out_specs=(VMEM, VMEM),
        compiler_params=pltpu.CompilerParams(vmem_limit_bytes=30 << 20),
        cost_estimate=pl.CostEstimate(
            flops=2_000_000_000, bytes_accessed=8 << 20, transcendentals=0
        ),
        name="attend",
    )(key_at, query_at, *operands, task_bias, lead_bias)


def attend_back(qkv, grads, context, lse, tables, heads, nb, held, at):
    key_at, bias_at, query_at, places, _, _ = tables
    total = context.shape[1]
    width = heads * HEAD
    parts = total // width
    operands, specs = zip(
        *[columns(qkv, i * parts + at, width) for i in range(3)], columns(context, at, width)
    )
    pieces, piece_specs = zip(*[columns(g, at, width) for g in grads])
    lse_spec = pl.BlockSpec((nb, 1, width), lambda i: (0, 0, at))
    out = jax.ShapeDtypeStruct((nb * BLOCK, total), jnp.bfloat16)
    out_spec = pl.BlockSpec((nb * BLOCK, width), lambda i: (0, at))
    count = 4 + len(operands) + 1 + len(pieces)
    abreast = 5 if (nb - 2) % 5 == 0 else 2
    return pl.pallas_call(
        partial(attend_back_kernel, heads, nb, abreast, len(pieces)),
        grid=(1,),
        out_shape=(out, out, out),
        in_specs=[SMEM] * 4
        + list(specs)
        + [lse_spec]
        + list(piece_specs)
        + [pl.BlockSpec(memory_space=pl.ANY)] * len(held),
        out_specs=(out_spec,) * 3,
        input_output_aliases={count + i: i for i in range(len(held))},
        scratch_shapes=[
            pltpu.VMEM(((nb + 1) * BLOCK, width), jnp.float32),
            pltpu.VMEM(((nb + 1) * BLOCK, width), jnp.float32),
            pltpu.VMEM((nb, 1, width), jnp.float32),
            pltpu.VMEM((nb * BLOCK, width), jnp.bfloat16),
            pltpu.VMEM(((nb + 1) * BLOCK, 2 * HEAD), jnp.float32),
        ],
        compiler_params=pltpu.CompilerParams(vmem_limit_bytes=52 << 20),
        cost_estimate=pl.CostEstimate(
            flops=15_000_000_000, bytes_accessed=6 << 20, transcendentals=0
        ),
        name="attend_back",
    )(key_at, bias_at, query_at, places, *operands, lse, *pieces, *held)


def block_tables(block_of_slot, doc, random_blocks):
    nb = random_blocks.shape[0]
    every = jnp.arange(nb, dtype=jnp.int32)
    slot_of_block = jnp.sum(
        jnp.where(block_of_slot[None, :] == every[:, None], every[None, :], 0), 1
    )
    ids = every[2:]
    before, after = ids - 1, ids + 1
    always_on = ids >= 0
    index = jnp.concatenate(
        [jnp.stack([ids * 0, ids * 0 + 1, before, ids, after], -1), random_blocks[2:]], -1
    )
    allowed = jnp.stack(
        [always_on, always_on, before >= 2, always_on, after < nb] + [always_on] * 3, -1
    )
    index = jnp.clip(index, 0, nb - 1)
    slots = jnp.sum(jnp.where(index[..., None] == block_of_slot, every, 0), -1)
    key_at = slots
    bias_at = jnp.where(allowed, slots, nb)
    query_at = jnp.concatenate([slot_of_block[2:], slot_of_block[:2]])
    inside = jnp.arange(BLOCK, dtype=jnp.int32)
    bias = jnp.where(block_of_slot[:, None] * BLOCK + inside < doc, 0.0, NEG_FILL)
    bias = bias.astype(jnp.float32)
    lead_bias = bias.reshape(1, -1)
    task_bias = (index[..., None] * BLOCK + inside < doc) & allowed[..., None]
    task_bias = jnp.where(task_bias, 0.0, NEG_FILL).astype(jnp.float32).reshape(nb - 2, -1)
    places = jnp.concatenate([block_of_slot, jnp.reshape(doc, (1,))])
    return key_at, bias_at, query_at, places, task_bias, lead_bias


TANH_SCALE = 0.7978845608028654
TANH_CUBE = 0.044715


def norm_rows(value):
    center = value - jnp.mean(value, -1, keepdims=True)
    scale = lax.rsqrt(jnp.mean(center * center, -1, keepdims=True) + EPSILON)
    return center * scale, scale


def norm_back(grad, normal, scale):
    return scale * (
        grad
        - jnp.mean(grad, -1, keepdims=True)
        - normal * jnp.mean(grad * normal, -1, keepdims=True)
    )


def feed_forward_kernel(
    chunk,
    few,
    pieces,
    mine_ref,
    x_ref,
    cot_own_ref,
    cot_came_ref,
    wo_ref,
    w1_hbm_ref,
    w2_hbm_ref,
    vec_ref,
    b1_ref,
    *refs,
):
    context_refs, refs = refs[:pieces], refs[pieces:]
    result_refs, refs = refs[:3], refs[3:]
    first_ref, active_out_ref, d_inner_out_ref, d_outer_ref, d_attended_ref = refs[:5]
    d_resid_ref, sums_ref, inner_sum_ref = refs[5:8]
    d_context_refs, refs = refs[8 : 8 + pieces], refs[8 + pieces :]
    w1_ref, w2_ref, active_ref, d_inner_ref, *refs = refs
    slope_ref, held_ref, normal_ref, scale_ref, result_ref, sems = refs
    cols = D // pieces
    first_step = pl.program_id(0) == 0
    tile = active_ref.shape[0]
    tokens_at = pl.ds(pl.multiple_of(pl.program_id(0) * tile, tile), tile)
    load_w1 = pltpu.make_async_copy(w1_hbm_ref, w1_ref, sems.at[0])
    load_w2 = pltpu.make_async_copy(w2_hbm_ref, w2_ref, sems.at[1])
    store_active = pltpu.make_async_copy(active_ref, active_out_ref.at[tokens_at, :], sems.at[2])
    store_d_inner = pltpu.make_async_copy(d_inner_ref, d_inner_out_ref.at[tokens_at, :], sems.at[3])
    low, full = jnp.bfloat16, jnp.float32
    tokens, hidden = active_ref.shape

    @pl.when(first_step)
    def _():
        load_w1.start()
        load_w2.start()
        sums_ref[...] = jnp.zeros_like(sums_ref)
        inner_sum_ref[...] = jnp.zeros_like(inner_sum_ref)

    bo, g1, s1, b2, g2, s2 = [vec_ref[i : i + 1, :] for i in range(6)]

    chunks = [slice(i, i + few) for i in range(0, tokens, few)]

    def each_columns(body):
        def step(i, carry):
            body(pl.ds(pl.multiple_of(i * chunk, chunk), chunk))
            return carry

        lax.fori_loop(0, hidden // chunk, step, 0)

    def add_sum(row, values):
        sums_ref[row : row + 1, :] += jnp.sum(values, 0, keepdims=True)

    def add_context(rows):
        parts = [
            dot(ref[rows, :], wo_ref[k * cols : (k + 1) * cols, :], NN)
            for k, ref in enumerate(context_refs)
        ]
        return sum(parts[1:], parts[0])

    for rows, attended in [(rows, add_context(rows)) for rows in chunks]:
        normal, scale = norm_rows(x_ref[rows, :].astype(full) + attended + bo)
        first = normal * g1 + s1
        normal_ref[rows, :] = normal
        scale_ref[rows, :] = jnp.broadcast_to(scale, (few, 128))
        held_ref[rows, :] = first
        first_ref[rows, :] = first.astype(low)

    @pl.when(first_step)
    def _():
        load_w1.wait()

    @each_columns
    def _(cols):
        u = dot(first_ref[...], w1_ref[:, cols], NN) + b1_ref[:1, cols]
        square = u * u
        tanh = jnp.tanh(u * (TANH_SCALE + (TANH_SCALE * TANH_CUBE) * square))
        share = 0.5 * tanh + 0.5
        active_ref[:, cols] = (u * share).astype(low)
        slope_ref[:, cols] = share + (0.5 * u) * (1.0 - tanh * tanh) * (
            TANH_SCALE + (3 * TANH_SCALE * TANH_CUBE) * square
        )

    store_active.start()

    @pl.when(first_step)
    def _():
        load_w2.wait()

    for rows, outer in [(rows, dot(active_ref[rows, :], w2_ref[...], NN)) for rows in chunks]:
        normal, scale = norm_rows(held_ref[rows, :] + outer + b2)
        result_ref[rows, :] = (normal * g2 + s2).astype(low)
        own = pl.program_id(0) == 0
        cot = jnp.where(own, cot_own_ref[0, rows, :], cot_came_ref[rows, :]).astype(full)
        d_second = norm_back(cot * g2, normal, scale)
        held_ref[rows, :] = d_second
        d_outer = d_second.astype(low)
        d_outer_ref[rows, :] = d_outer
        add_sum(3, d_outer.astype(full))
        add_sum(4, cot * normal)
        add_sum(5, cot)

    @pl.when(first_step)
    def _():
        result_refs[0][...] = result_ref[...]

    @pl.when(jnp.logical_not(first_step))
    def _():
        result_refs[1][...] = result_ref[: tile // 2, :]
        result_refs[2][...] = result_ref[tile // 2 :, :]

    @each_columns
    def _(cols):
        d_inner = (dot(d_outer_ref[...], w2_ref[cols, :], NT) * slope_ref[:, cols]).astype(low)
        d_inner_ref[:, cols] = d_inner
        inner_sum_ref[:1, cols] += jnp.sum(d_inner.astype(full), 0, keepdims=True)

    store_d_inner.start()
    for rows, back in [(rows, dot(d_inner_ref[rows, :], w1_ref[...], NT)) for rows in chunks]:
        d_first = held_ref[rows, :] + back
        normal = normal_ref[rows, :]
        add_sum(1, d_first * normal)
        add_sum(2, d_first)
        d_resid = norm_back(d_first * g1, normal, scale_ref[rows, :1])
        d_resid_ref[rows, :] = d_resid
        d_attended = d_resid.astype(low)
        d_attended_ref[rows, :] = d_attended
        add_sum(0, d_attended.astype(full))
    for rows in chunks:
        for k, ref in enumerate(d_context_refs):
            part = dot(d_attended_ref[rows, :], wo_ref[k * cols : (k + 1) * cols, :], NT)
            ref[rows, :] = part.astype(low)
    store_active.wait()
    store_d_inner.wait()


def feed_forward(mine, x, cot, cot_came, context, wo, w1, w2, vec, b1):
    low, full = jnp.bfloat16, jnp.float32
    tile, hidden = cot_came.shape[0], w1.shape[1]
    tokens, cols = 2 * tile, context[0].shape[1]
    row = pl.BlockSpec((tile, D), lambda i, at: (i, 0))
    part = pl.BlockSpec((tile, cols), lambda i, at: (i, 0))
    there = pl.BlockSpec(memory_space=pl.ANY)
    shards = (tile, tile // 2, tile // 2)
    once = pl.Buffered(1)
    whole = lambda a: pl.BlockSpec(a.shape, lambda i, at: (0,) * a.ndim, pipeline_mode=once)
    shape = jax.ShapeDtypeStruct
    return pl.pallas_call(
        partial(feed_forward_kernel, 1024, 256, len(context)),
        grid_spec=pltpu.PrefetchScalarGridSpec(
            num_scalar_prefetch=1,
            grid=(tokens // tile,),
            in_specs=[
                row,
                pl.BlockSpec((1, tile, D), lambda i, at: (at[0], 0, 0), pipeline_mode=once),
            ]
            + [whole(cot_came), whole(wo), there, there, whole(vec), whole(b1)]
            + [part] * len(context),
            out_specs=[pl.BlockSpec((n, D), lambda i, at: (0, 0)) for n in shards]
            + [row, there, there, row, row, row]
            + [pl.BlockSpec((8, n), lambda i, at: (0, 0)) for n in (D, hidden)]
            + [part] * len(context),
            scratch_shapes=[
                pltpu.VMEM(w1.shape, low),
                pltpu.VMEM(w2.shape, low),
                pltpu.VMEM((tile, hidden), low),
                pltpu.VMEM((tile, hidden), low),
                pltpu.VMEM((tile, hidden), full),
                pltpu.VMEM((tile, D), full),
                pltpu.VMEM((tile, D), full),
                pltpu.VMEM((tile, 128), full),
                pltpu.VMEM((tile, D), low),
                pltpu.SemaphoreType.DMA((4,)),
            ],
        ),
        out_shape=[shape((n, D), low) for n in shards]
        + [
            shape((tokens, D), low),
            shape((tokens, hidden), low),
            shape((tokens, hidden), low),
            shape((tokens, D), low),
            shape((tokens, D), low),
            shape((tokens, D), full),
            shape((8, D), full),
            shape((8, hidden), full),
        ]
        + [shape((tokens, cols), low)] * len(context),
        compiler_params=pltpu.CompilerParams(vmem_limit_bytes=50 << 20),
        cost_estimate=pl.CostEstimate(
            flops=50_000_000_000, bytes_accessed=40 << 20, transcendentals=0
        ),
        name="feed_forward",
    )(jnp.reshape(mine, (1,)).astype(jnp.int32), x, cot, cot_came, wo, w1, w2, vec, b1, *context)


def wide_kernel(at_ref, left_ref, right_ref, *refs):
    *came_refs, out_ref, turned_ref = refs
    i = pl.program_id(0)

    @pl.when(i == 0)
    def _():
        turned_ref[...] = left_ref[...].T

    rows = out_ref.shape[0]
    some = pl.ds(pl.multiple_of(lax.rem(i, D // rows) * rows, rows), rows)
    out_ref[...] = add_came(dot(turned_ref[some, :], right_ref[...], NN), came_refs)


def add_came(total, came_refs):
    for ref in came_refs:
        total = total + ref[...].astype(jnp.float32)
    return total.astype(jnp.bfloat16)


def tall_kernel(at_ref, left_ref, right_ref, *refs):
    *came_refs, out_ref = refs
    out_ref[...] = add_came(dot(left_ref[...], right_ref[...], TN), came_refs)


def tall_product(left, right, half, count, tile, came=()):
    tokens, width = right.shape[0], left.shape[1]
    part = width // count
    per = part // tile
    return pl.pallas_call(
        tall_kernel,
        grid_spec=pltpu.PrefetchScalarGridSpec(
            num_scalar_prefetch=1,
            grid=(per,),
            in_specs=[
                pl.BlockSpec((tokens, tile), lambda i, at: (0, at[0] * per + i)),
                pl.BlockSpec((tokens, right.shape[1]), lambda i, at: (0, 0)),
            ]
            + [pl.BlockSpec((tile, right.shape[1]), lambda i, at: (i, 0))] * len(came),
            out_specs=pl.BlockSpec((tile, right.shape[1]), lambda i, at: (i, 0)),
        ),
        out_shape=jax.ShapeDtypeStruct((part, right.shape[1]), jnp.bfloat16),
        compiler_params=pltpu.CompilerParams(vmem_limit_bytes=48 << 20),
        cost_estimate=pl.CostEstimate(
            flops=2 * tokens * part * right.shape[1], bytes_accessed=8 << 20, transcendentals=0
        ),
        name="tall_product",
    )(jnp.reshape(half, (1,)).astype(jnp.int32), left, right, *came)


def wide_product(left, right, half, count, rows, came=()):
    tokens, width = right.shape
    part = width // count
    blocks, per = part // D, D // rows
    return pl.pallas_call(
        wide_kernel,
        grid_spec=pltpu.PrefetchScalarGridSpec(
            num_scalar_prefetch=1,
            grid=(blocks * per,),
            in_specs=[
                pl.BlockSpec((tokens, D), lambda i, at: (0, 0)),
                pl.BlockSpec((tokens, D), lambda i, at: (0, at[0] * blocks + i // per)),
            ]
            + [pl.BlockSpec((rows, D), lambda i, at: (i, 0))] * len(came),
            out_specs=pl.BlockSpec((rows, D), lambda i, at: (i, 0)),
            scratch_shapes=[pltpu.VMEM((D, tokens), jnp.bfloat16)],
        ),
        out_shape=jax.ShapeDtypeStruct((part, D), jnp.bfloat16),
        compiler_params=pltpu.CompilerParams(vmem_limit_bytes=48 << 20),
        cost_estimate=pl.CostEstimate(
            flops=2 * tokens * part * D, bytes_accessed=8 << 20, transcendentals=0
        ),
        name="wide_product",
    )(jnp.reshape(half, (1,)).astype(jnp.int32), left, right, *came)


def heads_kernel(
    bit_ref, x_ref, d_query_ref, d_key_ref, d_value_ref, give_ref, keep_ref, turned_ref
):
    tokens, rows = x_ref.shape[0], turned_ref.shape[0]

    @pl.when(pl.program_id(0) == 0)
    def _():
        turned_ref[:D, :] = x_ref[...].T
        row = lax.broadcasted_iota(jnp.int32, (rows - D, tokens), 0)
        turned_ref[D:, :] = (row == 0).astype(jnp.float32).astype(jnp.bfloat16)

    for i, ref in enumerate((d_query_ref, d_key_ref, d_value_ref)):

        @pl.when(pl.program_id(0) == i)
        def _():
            total = dot(turned_ref[...], ref[...], NN).astype(jnp.bfloat16)
            first, second = total[: rows // 2], total[rows // 2 :]
            low_bit = bit_ref[0] == 0
            give_ref[...] = jnp.where(low_bit, second, first)
            keep_ref[...] = jnp.where(low_bit, first, second)


def heads_products(x, d_query, d_key, d_value, bit):
    tokens, cols = d_query.shape
    rows = D + 32
    each = pl.BlockSpec((tokens, cols), lambda i, at: (0, 0))
    part = pl.BlockSpec((rows // 2, cols), lambda i, at: (0, i))
    return pl.pallas_call(
        heads_kernel,
        grid_spec=pltpu.PrefetchScalarGridSpec(
            num_scalar_prefetch=1,
            grid=(3,),
            in_specs=[pl.BlockSpec((tokens, D), lambda i, at: (0, 0)), each, each, each],
            out_specs=[part, part],
            scratch_shapes=[pltpu.VMEM((rows, tokens), jnp.bfloat16)],
        ),
        out_shape=[jax.ShapeDtypeStruct((rows // 2, 3 * cols), jnp.bfloat16)] * 2,
        compiler_params=pltpu.CompilerParams(vmem_limit_bytes=62 << 20),
        cost_estimate=pl.CostEstimate(
            flops=6 * tokens * rows * cols, bytes_accessed=8 << 20, transcendentals=0
        ),
        name="heads_products",
    )(jnp.reshape(bit, (1,)).astype(jnp.int32), x, d_query, d_key, d_value)


def inputs_kernel(at_ref, d_query_ref, d_key_ref, d_value_ref, wq_ref, wk_ref, wv_ref, *out_refs):
    total = dot(d_query_ref[...], wq_ref[...], NT)
    total = total + dot(d_key_ref[...], wk_ref[...], NT)
    total = (total + dot(d_value_ref[...], wv_ref[...], NT)).astype(jnp.bfloat16)
    per = pl.num_programs(0) // len(out_refs)
    for k, ref in enumerate(out_refs):

        @pl.when(pl.program_id(0) // per == k)
        def _():
            ref[...] = total


def inputs_products(grads, weights, at, count):
    tokens, cols = grads[0].shape
    tile = 512
    per = tokens // count // tile
    part = pl.BlockSpec((tile, cols), lambda i, at: (i, 0))
    weight = pl.BlockSpec((D, cols), lambda i, at: (0, at[0]), pipeline_mode=pl.Buffered(1))

    def place(k):
        return pl.BlockSpec((tile, D), lambda i, at: (jnp.clip(i - k * per, 0, per - 1), 0))

    return pl.pallas_call(
        inputs_kernel,
        grid_spec=pltpu.PrefetchScalarGridSpec(
            num_scalar_prefetch=1,
            grid=(count * per,),
            in_specs=[part] * 3 + [weight] * 3,
            out_specs=[place(k) for k in range(count)],
        ),
        out_shape=[jax.ShapeDtypeStruct((tokens // count, D), jnp.bfloat16)] * count,
        compiler_params=pltpu.CompilerParams(vmem_limit_bytes=60 << 20),
        cost_estimate=pl.CostEstimate(
            flops=24_000_000_000, bytes_accessed=8 << 20, transcendentals=0
        ),
        name="inputs_products",
    )(jnp.reshape(at, (1,)).astype(jnp.int32), *grads, *weights)


def spread_heads_kernel(at_ref, pool_ref, *refs):
    cols = refs[-1].shape[1]
    for i, ref in enumerate(refs[-3:]):
        ref[...] = pool_ref[:, i * cols : (i + 1) * cols].astype(jnp.float32)


def spread_columns(pool, half, held):
    cols = pool.shape[1] // 3
    return spread_call(
        spread_heads_kernel,
        "spread_columns",
        half,
        (1,),
        (pool,),
        [pl.BlockSpec((D, 3 * cols), lambda i, at: (0, 0))],
        [(D, D)] * 3,
        [pl.BlockSpec((D, cols), lambda i, at: (0, at[0]))] * 3,
        held,
    )


OUT_STEPS = 3


def spread_outer_kernel(at_ref, first_ref, second_ref, *refs):
    i, blocks = pl.program_id(0), pl.num_programs(0)

    @pl.when(i < blocks - 1)
    def _():
        refs[-1][...] = first_ref[...].astype(jnp.float32)

    @pl.when(i == blocks - 1)
    def _():
        refs[-1][...] = second_ref[...].astype(jnp.float32)


def spread_inner_kernel(at_ref, first_ref, second_ref, third_ref, *refs):
    inner_ref, out_ref = refs[-2:]
    i, blocks = pl.program_id(0), pl.num_programs(0) - OUT_STEPS

    @pl.when(i < blocks - 1)
    def _():
        inner_ref[...] = first_ref[...].astype(jnp.float32)

    @pl.when(i == blocks - 1)
    def _():
        inner_ref[...] = second_ref[...].astype(jnp.float32)

    @pl.when(i >= blocks)
    def _():
        out_ref[...] = third_ref[...].astype(jnp.float32)


def spread_call(kernel, name, half, grid, operands, specs, out_shapes, out_specs, held):
    return pl.pallas_call(
        kernel,
        grid_spec=pltpu.PrefetchScalarGridSpec(
            num_scalar_prefetch=1,
            grid=grid,
            in_specs=specs + [pl.BlockSpec(memory_space=pl.ANY)] * len(held),
            out_specs=out_specs,
        ),
        out_shape=[jax.ShapeDtypeStruct(s, jnp.float32) for s in out_shapes],
        input_output_aliases={1 + len(operands) + i: i for i in range(len(held))},
        compiler_params=pltpu.CompilerParams(vmem_limit_bytes=32 << 20),
        cost_estimate=SHORT,
        name=name,
    )(jnp.reshape(half, (1,)).astype(jnp.int32), *operands, *held)


def spread_outer(first, second, half, held):
    rows = second.shape[0]
    blocks = first.shape[0] // rows + 1
    return spread_call(
        spread_outer_kernel,
        "spread_outer",
        half,
        (blocks,),
        (first, second),
        [
            pl.BlockSpec((rows, D), lambda i, at: (jnp.minimum(i, blocks - 2), 0)),
            pl.BlockSpec((rows, D), lambda i, at: (0, 0)),
        ],
        [(2 * rows * blocks, D)],
        [pl.BlockSpec((rows, D), lambda i, at: (at[0] * blocks + i, 0))],
        held,
    )


def spread_inner(first, mixed, half, held):
    rows = 256
    per = D // rows
    blocks = first.shape[0] // rows + 1
    wide = blocks // per
    out_rows = D // 2 // OUT_STEPS
    skip = rows // out_rows

    def inner_at(i, at):
        j = jnp.minimum(i, blocks - 1)
        return (j % per, at[0] * wide + j // per)

    return spread_call(
        spread_inner_kernel,
        "spread_inner",
        half,
        (blocks + OUT_STEPS,),
        (first, mixed, mixed),
        [
            pl.BlockSpec((rows, D), lambda i, at: (jnp.minimum(i, blocks - 2), 0)),
            pl.BlockSpec((rows, D), lambda i, at: (0, 0)),
            pl.BlockSpec((out_rows, D), lambda i, at: (skip + jnp.maximum(i - blocks, 0), 0)),
        ],
        [(D, 2 * wide * D), (D, D)],
        [
            pl.BlockSpec((rows, D), inner_at),
            pl.BlockSpec(
                (out_rows, D), lambda i, at: (at[0] * OUT_STEPS + jnp.maximum(i - blocks, 0), 0)
            ),
        ],
        held,
    )


class Ring:
    def __init__(self, axis, size, at, perm):
        self.axis, self.size, self.at, self.perm = axis, size, at, perm

    def send(self, value, by):
        return lax.ppermute(value, self.axis, self.perm(by))


class Pairs:
    def __init__(self, seq, rows, masks, core):
        me = lax.axis_index("seq") * rows + lax.axis_index("rows")
        bits = [lax.rem(me // mask, 2) for mask in masks]
        self.bit = jnp.where(lax.rem(me // core, 2) == 0, bits[0], bits[1])
        self.perm = [(i, i ^ masks[i // core % 2]) for i in range(seq * rows)]

    def swap(self, value):
        return lax.ppermute(value, ("seq", "rows"), self.perm)

    def keep(self, value):
        part = value.shape[0] // 2
        return lax.dynamic_slice_in_dim(value, self.bit * part, part, 0)

    def give(self, value):
        part = value.shape[0] // 2
        return lax.dynamic_slice_in_dim(value, (1 - self.bit) * part, part, 0)

    def halved(self, value, came):
        return (self.keep(value).astype(jnp.float32) + came.astype(jnp.float32)).astype(value.dtype)

    def halve(self, value):
        return self.halved(value, self.swap(self.give(value)))

    def joined(self, value, came):
        first = jnp.where(self.bit == 0, value, came)
        second = jnp.where(self.bit == 0, came, value)
        return jnp.concatenate([first, second], 0)

    def join(self, value):
        return self.joined(value, self.swap(value))


def powers(step, count):
    masks = []
    while count > 1:
        masks.append(step)
        step, count = step * 2, count // 2
    return masks


def make_links(seq, rows):
    half = seq // 2
    deep = CHIPS_Z if rows % CHIPS_Z == 0 else 1
    wide = rows // deep
    s = lax.axis_index("seq")
    near = Ring(
        "seq",
        half,
        lax.rem(s, half),
        lambda by: [(i, i // half * half + (i + by) % half) for i in range(seq)],
    )

    def pairs(first, second=None):
        return Pairs(seq, rows, (first, second or first), rows)

    far_mask = half * rows
    y, z = powers(1, wide), powers(wide, deep)
    far = pairs(far_mask)
    inside = [pairs(mask) for mask in powers(rows, half)]
    main = [pairs(far_mask, y[0]), pairs(y[0], z[0]), pairs(z[0], far_mask)]
    side = [pairs(z[0]), pairs(far_mask), pairs(y[0])]
    last = [pairs(mask) for mask in y[1:] + z[1:]]
    return near, far, inside, [main, side], last


def in_step(values):
    return list(lax.optimization_barrier(tuple(values)))


def cut(value, sizes):
    out, at = [], 0
    for size in sizes:
        out.append(value[at : at + size])
        at += size
    return out


class HalveStep:
    def __init__(self, pairs):
        self.pairs = pairs

    def start(self, parts):
        return [pair.swap(pair.give(part)) for pair, part in zip(self.pairs, parts)]

    def finish(self, parts, came):
        return [pair.halved(*both) for pair, *both in zip(self.pairs, parts, came)]


class GivenStep:
    def __init__(self, pair, given):
        self.pair, self.given = pair, given

    def start(self, parts):
        return [self.pair.swap(self.given)]

    def finish(self, parts, came):
        total = parts[0].astype(jnp.float32) + came[0].astype(jnp.float32)
        return [total.astype(parts[0].dtype)]


class JoinStep:
    def __init__(self, pairs):
        self.pairs = pairs

    def start(self, parts):
        return [pair.swap(part) for pair, part in zip(self.pairs, parts)]

    def finish(self, parts, came):
        return [pair.joined(*both) for pair, *both in zip(self.pairs, parts, came)]


class SumStep:
    def __init__(self, pair):
        self.pair = pair

    def start(self, parts):
        return cut(self.pair.swap(jnp.concatenate(parts, 0)), [p.shape[0] for p in parts])

    def finish(self, parts, came):
        return [
            (p.astype(jnp.float32) + c.astype(jnp.float32)).astype(p.dtype)
            for p, c in zip(parts, came)
        ]


class Chain:
    def __init__(self, parts, steps):
        self.parts, self.steps, self.came = list(parts), list(steps), None

    def start(self):
        self.came = self.steps[0].start(self.parts)

    def finish(self, *after):
        came = in_step(list(self.came) + list(after))[: len(self.came)]
        self.parts = self.steps.pop(0).finish(self.parts, came)
        self.came = None

    def step(self, *after):
        if self.came is None:
            self.start()
        self.finish(*after)
        if self.steps:
            self.start()


def column_sum(values):
    return jnp.sum(values.astype(jnp.float32), 0)


def per_device(
    seq,
    rows,
    inputs,
    query_weight,
    query_bias,
    key_weight,
    value_weight,
    value_bias,
    output_weight,
    output_bias,
    first_gain,
    first_shift,
    inner_weight,
    inner_bias,
    outer_weight,
    outer_bias,
    second_gain,
    second_shift,
    doc_tokens,
    random_blocks,
    cotangent,
):
    low, full = jnp.bfloat16, jnp.float32
    near, far, inside, routes, last = make_links(seq, rows)
    main, side = routes
    half = seq // 2
    width = inputs.shape[1]
    tokens = 2 * width
    nb = random_blocks.shape[1]
    heads = HEADS // half
    cols = heads * HEAD
    mine, at = far.bit, near.at

    def own_and_other(array):
        own = lax.dynamic_index_in_dim(array, mine, 0, False)
        return own, lax.dynamic_index_in_dim(array, 1 - mine, 0, False)

    def from_rows(own, other):
        return jnp.where(mine == 0, jnp.stack([own, other]), jnp.stack([other, own]))

    def by_device(values):
        stacked = jnp.stack(values)
        order = lax.rem(at + half - jnp.arange(half), half)
        return jnp.take(stacked, order, axis=0) if half > 2 else jnp.where(at == 0, stacked, stacked[::-1])

    def by_two(values):
        return [values[i : i + 2] for i in range(0, len(values), 2)]

    x_own, x_other = own_and_other(inputs)
    x_came = far.swap(x_other)

    shards = []
    for k in range(half):
        own = mine * half + lax.rem(at + k, half)
        shards += [own, lax.rem(own + half, seq)]
    per_shard = width // BLOCK
    block_of_slot = (
        jnp.stack(shards)[:, None] * per_shard + jnp.arange(per_shard, dtype=jnp.int32)
    ).reshape(-1).astype(jnp.int32)
    doc = lax.dynamic_index_in_dim(doc_tokens, mine, 0, False)
    chosen = lax.dynamic_index_in_dim(random_blocks, mine, 0, False)
    tables = block_tables(block_of_slot, doc, chosen)

    def my_cols(weight):
        return lax.dynamic_slice_in_dim(weight, at * cols, cols, weight.ndim - 1)

    weights = (query_weight, key_weight, value_weight)
    w_qkv = jnp.concatenate([my_cols(w) for w in weights], 1)
    b_qkv = jnp.concatenate(
        [my_cols(query_bias), jnp.zeros((cols,), low), my_cols(value_bias)]
    ).astype(full)
    wo = jnp.concatenate(
        [
            lax.dynamic_slice_in_dim(
                output_weight, lax.rem(at + half - k, half) * cols, cols, 0
            )
            for k in range(half)
        ],
        0,
    )
    vec = jnp.stack(
        [output_bias, first_gain, first_shift, outer_bias, second_gain, second_shift]
    ).astype(full)
    vec = jnp.pad(vec, ((0, 2), (0, 0)))
    b1 = jnp.broadcast_to(inner_bias.astype(full), (8, inner_bias.shape[0]))

    x_came, cotangent, w_qkv, b_qkv, wo, vec, b1, *tables = in_step(
        [x_came, cotangent, w_qkv, b_qkv, wo, vec, b1, *tables]
    )
    cot_came = far.swap(lax.dynamic_index_in_dim(cotangent, 1 - mine, 0, False))
    x_parts = [x_own, x_came]
    for k in range(1, half):
        x_parts += [near.send(x_own, half - k), near.send(x_came, half - k)]
    x_all = jnp.concatenate(x_parts, 0)
    qkv = (dot(x_all, w_qkv, NN) + b_qkv).astype(low)
    heads_context, lse = attend(qkv, tables, heads, nb)
    heads_context, lse, cot_came = in_step([heads_context, lse, cot_came])
    context = [heads_context] + [
        near.send(heads_context[k * tokens : (k + 1) * tokens], k) for k in range(1, half)
    ]
    values = feed_forward(
        mine, x_all, cotangent, cot_came, context, wo, inner_weight, outer_weight, vec, b1
    )
    result, result_half, values = values[0], list(values[1:3]), values[3:]
    first_low, active, d_inner, d_outer, d_attended, d_resid, sums, inner_sum, *d_context = values
    heads_grad = [d_context[0]] + [near.send(d_context[k], half - k) for k in range(1, half)]

    packed = jnp.concatenate([sums[:6].reshape(-1), inner_sum[0]]).reshape(-1, D)
    packed = jnp.pad(packed, ((0, 128 - packed.shape[0]), (0, 0))).astype(low)

    def outer_product(part, k, came=()):
        return tall_product(active, d_outer, part, half, 768, came)

    def inner_product(part, k, came=()):
        return wide_product(first_low, d_inner, part, half, 768, came)

    def out_product(part, k, came=()):
        k = (half - k) % half
        if cols % 128:
            total = dot(context[k][:tokens], d_attended, TN)
            return sum([c.astype(full) for c in came], total).astype(low)
        return tall_product(context[k], d_attended, 0, 1, cols, came)

    def packed_part(part, k, came=()):
        size = 128 // half
        total = lax.dynamic_slice_in_dim(packed, part * size, size, 0).astype(full)
        return sum([c.astype(full) for c in came], total).astype(low)

    def give(product):
        return [product(lax.rem(at + k, half), k) for k in range(1, half)]

    def send(parts):
        return [near.send(part, k) for k, part in enumerate(parts, 1)]

    outer_give = give(outer_product)
    outer_give[0], first_low, d_attended = in_step([outer_give[0], first_low, d_attended])
    outer_came = send(outer_give)
    inner_came = send(give(inner_product))
    out_came = send(give(out_product))
    packed_came = send(give(packed_part))
    outer_grad = outer_product(at, 0, outer_came)
    outer_main = outer_grad.shape[0] * 3 // 4
    early = Chain([outer_grad[:outer_main], outer_grad[outer_main:]], [HalveStep([main[0], side[0]])])
    early.start()
    inner_came[0], out_came[0], packed_came[0], *early.parts = in_step(
        [inner_came[0], out_came[0], packed_came[0]] + early.parts
    )
    inner_grad = inner_product(at, 0, inner_came)
    out_grad = out_product(at, 0, out_came)
    packed = packed_part(at, 0, packed_came)
    inner_grad, out_grad, packed, *early.came = in_step(
        [inner_grad, out_grad, packed] + early.came
    )
    early.finish()
    inner_main = inner_grad.shape[0] * 5 // 6
    mixed = jnp.concatenate([inner_grad[inner_main:], out_grad, packed], 0)
    rest = Chain([inner_grad[:inner_main], mixed], [HalveStep([main[0], side[0]])])
    heads_grad[0], *rest.parts = in_step([heads_grad[0]] + early.parts + rest.parts)
    early.parts, rest.parts = rest.parts[:2], rest.parts[2:]

    first_sizes = [
        (outer_main // 2, inner_main // 2),
        ((outer_grad.shape[0] - outer_main) // 2, mixed.shape[0] // 2),
    ]
    first = Chain([], [HalveStep([main[i], side[i]]) for i in (1, 2)])
    first.steps += [SumStep(pair) for pair in last]
    first.steps += [JoinStep([main[i], side[i]]) for i in (2, 1)]

    steps = cols // 128 if cols % 128 == 0 else 1
    d_qkv = ()
    result_came = []
    for k in range(steps):
        chain = first if first.parts else rest
        chain.start()
        if k == 2:
            result_half[0], d_query = in_step([result_half[0], d_qkv[0]])
            d_qkv = (d_query,) + d_qkv[1:]
            result_came.append(far.swap(result_half[0]))
        d_qkv = attend_back(
            qkv, heads_grad, heads_context, lse, tables, heads // steps, nb, d_qkv, k
        )
        d_query, d_key, d_value, *came = in_step(list(d_qkv) + chain.came + result_came)
        d_qkv = (d_query, d_key, d_value)
        chain.came, result_came = came[: len(chain.came)], came[len(chain.came) :]
        chain.finish()
        if chain is rest:
            first.parts = [
                jnp.concatenate([e, r], 0) for e, r in zip(early.parts, rest.parts)
            ]
        d_query, *first.parts = in_step([d_query] + first.parts)
        d_qkv = (d_query, d_key, d_value)

    while len(first.steps) > 3:
        first.start()
        first.finish()
    sums_at_last = first.steps.pop(0)
    some = first.parts[0].shape[0] // 4 // 8 * 8
    main_parts = [first.parts[0][:some], first.parts[0][some:]]
    last_came = sums_at_last.start([main_parts[0], first.parts[1]])
    result_half[1:], d_query = in_step([*result_half[1:], d_query])[:-1], d_query
    result_came += [far.swap(piece) for piece in result_half[len(result_came) :]]
    if cols % 128 == 0:
        heads_give, heads_keep = heads_products(x_all, *d_qkv, main[0].bit)
    else:
        sums_of = [jnp.pad(column_sum(d)[None, :], ((0, 31), (0, 0))) for d in d_qkv]
        heads_part = [
            jnp.concatenate([dot(x_all, d, TN), total], 0) for d, total in zip(d_qkv, sums_of)
        ]
        heads_part = jnp.concatenate(heads_part, 1).astype(low)
        heads_give, heads_keep = main[0].give(heads_part), main[0].keep(heads_part)
    heads_give, heads_keep, d_query, d_key, d_value, *came = in_step(
        [heads_give, heads_keep, d_query, d_key, d_value] + last_came + result_came
    )
    last_came, result_came = came[:2], came[2:]
    main_parts[1], heads_give = in_step([main_parts[1], heads_give])

    second = Chain([heads_keep], [GivenStep(main[0], heads_give)])
    second.steps += [HalveStep([main[i]]) for i in (1, 2)]
    second.steps += [SumStep(pair) for pair in last]
    second.steps += [JoinStep([main[i]]) for i in (2, 1, 0)]
    second.start()
    last_came += sums_at_last.start(main_parts[1:])
    if cols % 128 == 0:
        d_parts = list(inputs_products((d_query, d_key, d_value), weights, at, half))
    else:
        parts = zip((d_query, d_key, d_value), (my_cols(w) for w in weights))
        d_parts = sum(dot(d, w, NT) for d, w in parts).astype(low)
        d_parts = cut(d_parts, [tokens] * half)
    d_parts[0], *came = in_step([d_parts[0]] + last_came + second.came)
    second.came = came[3:]
    sums = sums_at_last.finish([main_parts[0], first.parts[1], main_parts[1]], came[:3])
    first.parts = [jnp.concatenate([sums[0], sums[2]], 0), sums[1]]
    second.finish()

    def together(*beside):
        count = len(first.came or ())
        values = in_step(list(first.came or ()) + second.came + list(beside))
        if count:
            first.came = values[:count]
            first.finish()
        second.came = values[count : count + len(second.came)]
        second.finish()
        return values[len(values) - len(beside) :]

    second.start()
    first.start()
    d_came = [near.send(d_parts[k], k) for k in range(1, half)]
    d_came = together(*d_came)
    second.start()
    first.start()
    d_input = d_resid + d_parts[0].astype(full)
    for value in d_came:
        d_input = d_input + value.astype(full)
    d_input = d_input.astype(low)
    result = from_rows(result, jnp.concatenate(result_came, 0))
    d_input, result = together(d_input, result)
    for _ in last[:-1]:
        second.step()
    second.start()
    pieces = [p for share, size in zip(first.parts, first_sizes) for p in cut(share, size)]
    outer = Chain([pieces[0], pieces[2]], [JoinStep([main[0], side[0]])])
    inner = Chain([pieces[1], pieces[3]], [JoinStep([main[0], side[0]])])
    outer.start()
    d_input_came = [far.swap(d_input[width : width + width // 2])]
    values = together(*outer.came, *inner.parts, *d_input_came)
    outer.came, inner.parts, d_input_came = values[:2], values[2:4], values[4:]
    outer.finish()
    second.start()
    inner.start()
    outer_came = [near.send(part, k) for k in range(1, half) for part in outer.parts]
    placed = spread_outer(*outer.parts, at, ()) if half == 2 else outer.parts
    count = 2 + len(outer_came)
    values = together(*inner.came, *outer_came, d_input, *placed)
    inner.came, outer_came, d_input = values[:2], values[2:count], values[count]
    outer.parts = values[count + 1 :]
    inner.finish()
    second.start()
    inner_came = [near.send(part, k) for k in range(1, half) for part in inner.parts]
    d_input_came.append(far.swap(d_input[width + width // 2 :]))
    if half == 2:
        outer.parts = list(spread_outer(*outer_came, 1 - at, outer.parts))
    count = len(inner_came)
    values = together(*inner_came, *d_input_came, *outer.parts)
    inner_came, d_input_came, outer.parts = (
        values[:count],
        values[count : count + 2],
        values[count + 2 :],
    )
    second.start()
    d_input = from_rows(d_input[:width], jnp.concatenate(d_input_came, 0))
    small = inner_grad.shape[0] - inner_main, out_grad.shape[0], packed.shape[0]
    inner_b, out_grad, packed = cut(inner.parts[1], small)
    packed = [packed] + [cut(p, small)[2] for p in inner_came[1::2]]
    packed = by_device(packed).reshape(-1, D).astype(full)
    if half == 2:
        (outer_grad,) = outer.parts
        placed = spread_inner(*inner.parts, at, ())
        inner_grad, out_grad = spread_inner(*inner_came, 1 - at, placed)
    else:
        outer_grad = [jnp.concatenate(p, 0) for p in [outer.parts] + by_two(outer_came)]
        outer_grad = by_device(outer_grad).reshape(-1, D).astype(full)
        inner_grad = [jnp.concatenate([inner.parts[0], inner_b], 0)]
        out_grad = [out_grad]
        for first_part, other in by_two(inner_came):
            inner_grad.append(jnp.concatenate([first_part, cut(other, small)[0]], 0))
            out_grad.append(cut(other, small)[1])
        inner_grad = by_device(inner_grad).reshape(-1, D, D).astype(full)
        inner_grad = inner_grad.transpose(1, 0, 2).reshape(D, -1)
        out_grad = by_device(out_grad).reshape(-1, D).astype(full)
    small_grads = [packed[i] for i in range(6)] + [packed[6:10].reshape(-1)]
    d_input, inner_grad, out_grad, outer_grad, *small_grads = together(
        d_input, inner_grad, out_grad, outer_grad, *small_grads
    )
    heads_parts = second.parts[0]
    if half == 2:
        heads_came = near.send(heads_parts, 1)
        query_grad, key_grad, value_grad = spread_columns(
            heads_came, 1 - at, spread_columns(heads_parts, at, ())
        )
        biases = [p[D].astype(full) for p in (heads_parts, heads_came)]
        biases = jnp.where(at == 0, jnp.stack(biases), jnp.stack(biases[::-1]))
        query_bias_grad = biases[:, :cols].reshape(-1)
        value_bias_grad = biases[:, 2 * cols :].reshape(-1)
    else:
        heads_parts = by_device([heads_parts] + [near.send(heads_parts, k) for k in range(1, half)])
        query_grad, key_grad, value_grad = (
            jnp.concatenate([p[:, i * cols : (i + 1) * cols] for p in heads_parts], 1).astype(full)
            for i in range(3)
        )
        query_bias_grad, value_bias_grad = query_grad[D], value_grad[D]
        query_grad, key_grad, value_grad = query_grad[:D], key_grad[:D], value_grad[:D]
    return (
        result,
        d_input,
        query_grad,
        query_bias_grad,
        key_grad,
        value_grad,
        value_bias_grad,
        out_grad,
        *small_grads[:3],
        inner_grad,
        small_grads[6],
        outer_grad,
        *small_grads[3:6],
    )


def solution(mesh):
    tokens = P("rows", "seq", None)
    in_specs = (tokens,) + (P(),) * 15 + (P("rows"), P("rows", None, None), tokens)
    out_specs = (tokens, tokens) + (P(),) * 15
    return jax.shard_map(
        partial(per_device, mesh.shape["seq"], mesh.shape["rows"]),
        mesh=mesh,
        in_specs=in_specs,
        out_specs=out_specs,
        check_vma=False,
    )
```
